256 devices in a mesh: wide: 32 (over y, z), bulk: 8 (over x, core).
Axes of the slice: x: 4, y: 4, z: 8, core: 2. Of those that a mesh axis runs over, the one named last changes fastest.
Arguments:
- waveforms: bfloat16 [8, 128, 10240], P('bulk', 'wide'), may hold values from -20 to 20
- owner_of: int32 [8, 128], P('bulk', 'wide'), may hold values from 0 to 31, as said below
- lengths: int32 [8, 128], P('bulk', 'wide'), may hold values from 2560 to 10240, as said below
- cotangent: bfloat16 [8, 32, 2048, 512], P('bulk', 'wide'), may hold values from -0.029907227 to 0.029907227
- conv_first: bfloat16 [10, 512], replicated, may hold values from -2 to 2
- norm_gain: float32 [512], replicated, may hold values from 0.1 to 1.9
- norm_bias: float32 [512], replicated, may hold values from -2 to 2
- conv_second: bfloat16 [1536, 512], replicated, may hold values from -0.15625 to 0.15625
Outputs:
- grad_second: float32 [1536, 512], P('wide', 'bulk')
- grad_first: float32 [10, 512], replicated
- grad_gain: float32 [512], replicated
- grad_bias: float32 [512], replicated
The draws below stay inside these ranges and needn't reach their ends.
Inputs may be any that keep to these rules, and one draw needn't show every extreme that they name: `owner_of`: within each replica group every owner index is named by exactly 4 utterances, whose lengths sum to exactly 20480. Utterance l * 4 + s (loader l, slot s) has owner l XOR m[s], where the 4 values m[s] depend on the group and the slot only and are distinct. `lengths`: every length is a multiple of 10.
All inputs are finite; a program needn't handle non-finite values.
Results may differ from the reference program's by a relative error of at most 0.0049.
Values may be sent and summed in bfloat16 or wider, within the bound.
No kernel may reach another device: no remote copies, remote signals or barrier semaphores. Data moves between devices by JAX's collectives and lax.ppermute only.
A program may use at most 128 MiB of HBM per device.

```python
import math
import jax
import jax.numpy as jnp
from jax import lax

CHANNELS = 512
CAP = 20480
U_DEV = 4
GROUPS = 8
OWNERS = 32
UTTS = 128
FRAMES = 2048
LMAX = 10240
LMIN = 2560


def plan_utterances(key):
    base_key = jax.random.fold_in(key, 7)
    force_key, piece_key, mask_key = jax.random.split(base_key, 3)
    total_units = CAP // 10
    least_unit = LMIN // 10
    most_unit = LMAX // 10
    forced = jax.random.randint(force_key, (GROUPS, 1), 0, OWNERS)
    is_forced = jnp.arange(OWNERS, dtype=jnp.int32)[None, :] == forced
    remain = jnp.full((GROUPS, OWNERS), total_units, jnp.int32)
    pieces = []
    piece_keys = jax.random.split(piece_key, U_DEV - 1)
    for slot_pos in range(U_DEV - 1):
        left_after = U_DEV - 1 - slot_pos
        low_bound = jnp.maximum(least_unit, remain - left_after * most_unit)
        high_bound = jnp.minimum(most_unit, remain - left_after * least_unit)
        drawn = jax.random.randint(piece_keys[slot_pos], (GROUPS, OWNERS), low_bound, high_bound + 1)
        if slot_pos == 0:
            drawn = jnp.where(is_forced, most_unit, drawn)
        if slot_pos == 1:
            drawn = jnp.where(is_forced, least_unit, drawn)
        pieces.append(drawn)
        remain = remain - drawn
    pieces.append(remain)
    unit_lens = jnp.stack(pieces, axis=2)
    masks = jax.vmap(lambda sub_key: jax.random.permutation(sub_key, OWNERS))(jax.random.split(mask_key, GROUPS))[:, :U_DEV]
    loader_ids = jnp.arange(OWNERS, dtype=jnp.int32)[None, :, None]
    owner_table = jnp.bitwise_xor(loader_ids, masks[:, None, :].astype(jnp.int32))
    length_table = jnp.take_along_axis(unit_lens, owner_table, axis=1) * 10
    return (owner_table.reshape(GROUPS, UTTS).astype(jnp.int32), length_table.reshape(GROUPS, UTTS).astype(jnp.int32))


def draw_owner_of(key, part):
    return plan_utterances(key)[0]


def draw_lengths(key, part):
    return plan_utterances(key)[1]


def draw_waveforms(key, part):
    noise_key, scale_key = jax.random.split(jax.random.fold_in(key, 3), 2)
    blocks = LMAX // 160
    noise_part = jax.random.normal(noise_key, (GROUPS, UTTS, blocks, 160), jnp.float32)
    envelope = jnp.exp(jax.random.uniform(scale_key, (GROUPS, UTTS, blocks, 1), jnp.float32, math.log(0.3), math.log(3.0)))
    values = noise_part * envelope
    return jnp.clip(values, -18.0, 18.0).reshape(GROUPS, UTTS, LMAX).astype(jnp.bfloat16)


def block_levels(rng, shape, cuts, smallest, high):
    def one(axis_at, blocks):
        heights = jax.random.uniform(jax.random.fold_in(jax.random.fold_in(rng, 6), axis_at), (blocks,), jnp.float32, smallest / len(cuts), high / len(cuts))
        return jnp.repeat(jnp.exp(heights), shape[axis_at] // blocks).reshape((-1,) + (1,) * (len(shape) - axis_at - 1))

    level = one(*cuts[0])
    for cut in cuts[1:]:
        level = level * one(*cut)
    return level


def normal_values(stream_key, extent, scale, most, cuts=(), kind=jnp.bfloat16):
    factor_of = block_levels(stream_key, extent, cuts, -0.22, 0.18) if cuts else 1.0
    array = jax.random.normal(stream_key, extent, jnp.float32) * scale * factor_of
    return jnp.minimum(jnp.maximum(array, -most), most).astype(kind)


def setup_inputs(seed: int = 0) -> dict:
    keys = jax.random.split(jax.random.key(seed), 9)
    return {
        "waveforms": draw_waveforms(jax.random.fold_in(keys[8], 71), 0),
        "owner_of": draw_owner_of(jax.random.fold_in(keys[8], 71), 0),
        "lengths": draw_lengths(jax.random.fold_in(keys[8], 71), 0),
        "cotangent": normal_values(keys[3], (GROUPS, OWNERS, FRAMES, CHANNELS), 0.005, 0.029907227, ((0, 8), (1, 32))),
        "conv_first": normal_values(keys[4], (10, CHANNELS), 10 ** -0.5, 2.0),
        "norm_gain": jnp.clip(1.0 + 0.18 * jax.random.normal(keys[5], (CHANNELS,), jnp.float32), 0.1, 1.9),
        "norm_bias": normal_values(keys[6], (CHANNELS,), 0.5, 2.0, (), jnp.float32),
        "conv_second": normal_values(keys[7], (3 * CHANNELS, CHANNELS), (3 * CHANNELS) ** -0.5, 0.15625),
    }


def gelu_value(values):
    return 0.5 * values * (1.0 + lax.erf(values * 0.7071067811865476))

def gelu_slope(values):
    return 0.5 * (1.0 + lax.erf(values * 0.7071067811865476)) + values * jnp.exp(-0.5 * values * values) * 0.3989422804014327

def plan_offsets(table_owner, table_len):
    row_index = jnp.arange(table_owner.shape[0], dtype=jnp.int32)
    before = (row_index[None, :] < row_index[:, None]) & (table_owner[None, :] == table_owner[:, None])
    offsets = lax.optimization_barrier(jnp.sum(jnp.where(before, table_len[None, :], 0), axis=1)).astype(jnp.int32)
    ranking = lax.optimization_barrier(jnp.sum(before.astype(jnp.int32), axis=1)).astype(jnp.int32)
    return (offsets, ranking)

def segment_mask(frame_count, begin, length):
    frame_index = jnp.arange(frame_count, dtype=jnp.int32)
    inside = (frame_index[None, :] >= begin[:, None]) & (frame_index[None, :] < (begin + length)[:, None])
    return inside.astype(jnp.float32)

def owner_terms(stream, seg_start, seg_size, cot_rows, conv_first, norm_gain, norm_bias, conv_second):
    highest = lax.Precision.HIGHEST
    capacity = stream.shape[0]
    early_count = capacity // 5
    late_count = capacity // 10
    channels = conv_first.shape[1]
    padded = jnp.concatenate([stream, jnp.zeros((5,), stream.dtype)])
    five_rows = padded.reshape(early_count + 1, 5)
    early_taps = jnp.concatenate([five_rows[:-1], five_rows[1:]], axis=1)
    early_pre = jnp.dot(early_taps, conv_first, preferred_element_type=jnp.float32)
    member = segment_mask(early_count, seg_start // 5, seg_size // 5 - 1)
    early_valid = lax.optimization_barrier(jnp.sum(member, axis=0))[:, None]
    seg_counts = (seg_size // 5 - 1).astype(jnp.float32)[:, None]
    seg_means = jnp.dot(member, early_pre, precision=highest) / seg_counts
    centered = (early_pre - jnp.dot(member.T, seg_means, precision=highest)) * early_valid
    seg_spread = jnp.dot(member, centered * centered, precision=highest) / seg_counts
    inv_scale = lax.rsqrt(seg_spread + 1e-05)
    frame_scale = jnp.dot(member.T, inv_scale, precision=highest)
    normed = centered * frame_scale
    act_in = normed * norm_gain + norm_bias
    early_act = (gelu_value(act_in) * early_valid).astype(jnp.bfloat16)
    padded_rows = jnp.concatenate([early_act, jnp.zeros((1, channels), jnp.bfloat16)])
    late_taps = jnp.concatenate([padded_rows[0:early_count:2], padded_rows[1:early_count:2], padded_rows[2:early_count + 1:2]], axis=1)
    late_pre = jnp.dot(late_taps, conv_second, preferred_element_type=jnp.float32)
    late_valid = lax.optimization_barrier(jnp.sum(segment_mask(late_count, seg_start // 10, seg_size // 10 - 1), axis=0))[:, None]
    late_grad = (cot_rows.astype(jnp.float32) * gelu_slope(late_pre) * late_valid).astype(jnp.bfloat16)
    contract = (((1,), (1,)), ((), ()))
    back_zero = lax.dot_general(late_grad, conv_second[0:channels], contract, preferred_element_type=jnp.float32)
    back_one = lax.dot_general(late_grad, conv_second[channels:2 * channels], contract, preferred_element_type=jnp.float32)
    back_two = lax.dot_general(late_grad, conv_second[2 * channels:3 * channels], contract, preferred_element_type=jnp.float32)
    even_rows = back_zero + jnp.concatenate([jnp.zeros((1, channels), jnp.float32), back_two[:-1]])
    early_back = jnp.stack([even_rows, back_one], axis=1).reshape(early_count, channels)
    act_grad = early_back * gelu_slope(act_in) * early_valid
    grad_bias = lax.optimization_barrier(jnp.sum(act_grad, axis=0))
    grad_gain = lax.optimization_barrier(jnp.sum(act_grad * normed, axis=0))
    scaled = act_grad * norm_gain
    first_mean = jnp.dot(member, scaled, precision=highest) / seg_counts
    cross_mean = jnp.dot(member, scaled * normed, precision=highest) / seg_counts
    spread_back = jnp.dot(member.T, first_mean, precision=highest) + normed * jnp.dot(member.T, cross_mean, precision=highest)
    early_grad = ((scaled - spread_back) * frame_scale).astype(jnp.bfloat16)
    grad_first = lax.dot_general(early_taps, early_grad, (((0,), (0,)), ((), ())), preferred_element_type=jnp.float32)
    return (late_taps, late_grad, grad_first, grad_gain, grad_bias)

def reference(waveforms, owner_of, lengths, cotangent, conv_first, norm_gain, norm_bias, conv_second):
    group_count = waveforms.shape[0]
    utterances = waveforms.shape[1]
    longest = waveforms.shape[2]
    owners = cotangent.shape[1]
    capacity = cotangent.shape[2] * 10
    channels = conv_first.shape[1]
    slot_count = utterances // owners
    positions = jnp.arange(longest, dtype=jnp.int32)
    totals = (jnp.zeros((3 * channels, channels), jnp.float32), jnp.zeros((10, channels), jnp.float32), jnp.zeros((channels,), jnp.float32), jnp.zeros((channels,), jnp.float32))
    for group in range(group_count):
        group_owner = owner_of[group]
        group_len = lengths[group]
        group_waves = waveforms[group]
        offsets, ranking = plan_offsets(group_owner, group_len)

        def put_row(row_pos, loop_state):
            buffer, seg_start, seg_size = loop_state
            target = group_owner[row_pos].astype(jnp.int32)
            length = group_len[row_pos]
            offset = offsets[row_pos].astype(jnp.int32)
            slot_rank = ranking[row_pos]
            samples = lax.dynamic_index_in_dim(group_waves, row_pos, 0, keepdims=False).astype(jnp.float32)
            samples = jnp.where(positions < length, samples, 0.0)
            window = lax.dynamic_slice(buffer, (target, offset), (1, longest)) + samples[None, :]
            buffer = lax.dynamic_update_slice(buffer, window, (target, offset))
            seg_start = seg_start.at[target, slot_rank].set(offset)
            seg_size = seg_size.at[target, slot_rank].set(length)
            return (buffer, seg_start, seg_size)
        start_state = (jnp.zeros((owners, capacity + longest), jnp.float32), jnp.zeros((owners, slot_count), jnp.int32), jnp.zeros((owners, slot_count), jnp.int32))
        buffer, seg_start, seg_size = lax.fori_loop(0, utterances, put_row, start_state)
        streams = buffer[:, :capacity].astype(jnp.bfloat16)

        def per_owner(running, inputs):
            stream, starts, sizes, cot_rows = inputs
            late_taps, late_grad, grad_first, grad_gain, grad_bias = owner_terms(stream, starts, sizes, cot_rows, conv_first, norm_gain, norm_bias, conv_second)
            grad_second = lax.dot_general(late_taps, late_grad, (((0,), (0,)), ((), ())), preferred_element_type=jnp.float32)
            return ((running[0] + grad_second, running[1] + grad_first, running[2] + grad_gain, running[3] + grad_bias), None)
        totals, _ = lax.scan(per_owner, totals, (streams, seg_start, seg_size, cotangent[group]))
    return (totals[0], totals[1], totals[2], totals[3])
```

```python
import functools

import jax
import jax.numpy as jnp
from jax import lax
from jax.experimental import pallas as pl
from jax.experimental.pallas import tpu as pltpu
from jax.sharding import PartitionSpec as P

F32 = jnp.float32
BF16 = jnp.bfloat16
HIGHEST = lax.Precision.HIGHEST
SLOTS = 4
TAPS = 10
GRAN = 1024
ROWS = 2048
CH = 512
BLK = 256


def dot(a, b, precision=None):
    return jnp.dot(a, b, preferred_element_type=F32, precision=precision)


def dot_t(a, b, precision=None):
    return lax.dot_general(
        a, b, (((0,), (0,)), ((), ())), preferred_element_type=F32, precision=precision
    )


def cdf_slope(v):
    e = jnp.exp2(v * v * (-0.5 * 1.4426950408889634))
    d = 1.0 + jnp.abs(v) * (0.3275911 * 0.7071067811865476)
    r = pl.reciprocal(d, approx=True)
    t = r * (2.0 - d * r)
    poly = 0.5 * 1.061405429
    for c in (-1.453152027, 1.421413741, -0.284496736, 0.254829592):
        poly = poly * t + 0.5 * c
    tail = poly * t * e
    cdf = jnp.where(v < 0.0, tail, 1.0 - tail)
    return cdf, cdf + v * (e * 0.3989422804014327)


def plan(sc):
    size = [sc[s] for s in range(SLOTS)]
    src = [sc[SLOTS + s] for s in range(SLOTS)]
    rank, off = [], []
    for s in range(SLOTS):
        before = [(src[q] < src[s]).astype(jnp.int32) for q in range(SLOTS) if q != s]
        sizes = [size[q] for q in range(SLOTS) if q != s]
        rank.append(sum(before))
        off.append(sum(b * n for b, n in zip(before, sizes)))
    out = []
    for r in range(SLOTS):
        hit = [(rank[s] == r).astype(jnp.int32) for s in range(SLOTS)]
        out.append(
            (
                sum(h * s for s, h in enumerate(hit)),
                sum(h * o for o, h in zip(off, hit)),
                sum(h * n for n, h in zip(size, hit)),
            )
        )
    return out


def by_lane(values, index):
    out = values[0]
    for s in range(1, len(values)):
        out = jnp.where(index == s, values[s], out)
    return out


def forward_kernel(
    sc, u, cot, wst, gain, bias, w2,
    lg, sl, keep, send, xs, nst, tc, im,
    buf, xd, xbig, wbig, acc,
):
    step = pl.program_id(0)
    segs = plan(sc)

    @pl.when(step == 0)
    def _():
        buf[pl.ds(ROWS, 8), :] = jnp.zeros((8, 128), F32)
        for slot, off, _n in segs:
            buf[pl.ds(off, GRAN), :] = u[pl.ds(pl.multiple_of(slot * GRAN, GRAN), GRAN), :]
        src = lax.broadcasted_iota(jnp.int32, (128, 256), 0)
        tap = lax.broadcasted_iota(jnp.int32, (128, 256), 1) % 16
        r0 = ((tap == src) & (src < TAPS)).astype(F32).astype(BF16)
        r1 = ((tap == src + TAPS) & (src < 5)).astype(F32).astype(BF16)
        one = (lax.broadcasted_iota(jnp.int32, (1, 256), 1) % 16 == 15).astype(F32)
        lane = lax.broadcasted_iota(jnp.int32, (1, 256), 1)
        starts = [o for _s, o, _n in segs]
        ends = [o + n for _s, o, n in segs]
        lo_big, hi_big = by_lane(starts, lane // 64), by_lane(ends, lane // 64)
        lane1 = lane[:, :128]
        odd = (lane1 // 16) % 2
        lo_d = by_lane(starts, lane1 // 32)
        hi_all = by_lane(ends, lane1 // 32)
        hi_d = hi_all - odd
        count = (hi_d - lo_d).astype(F32)

        sums = jnp.zeros((1, 128), F32)
        for rb in range(ROWS // BLK):
            base = rb * BLK
            b0 = buf[pl.ds(base, BLK), :].astype(BF16)
            b1 = buf[pl.ds(base + 1, BLK), :].astype(BF16)
            xr = dot(b0, r0) + dot(b1, r1) + one
            row = lax.broadcasted_iota(jnp.int32, (BLK, 1), 0) + base
            xbig[pl.ds(base, BLK), :] = jnp.where((row >= lo_big) & (row < hi_big), xr, 0.0).astype(BF16)
            x1 = xr[:, :128]
            raw = jnp.where((row >= lo_d) & (row < hi_d), x1, 0.0)
            sums = sums + jnp.sum(raw, axis=0, keepdims=True)
            xd[pl.ds(base, BLK), :] = x1
            full = jnp.where((row >= lo_d) & (row < hi_all), x1, 0.0)
            xs[0, pl.ds(base, BLK), :] = jnp.where(odd == 0, full, 0.0).astype(BF16)
            xs[1, pl.ds(base, BLK), :] = jnp.where(odd == 1, full, 0.0).astype(BF16)
        xbig[pl.ds(ROWS, 16), :] = jnp.zeros((16, 256), BF16)
        mu = sums / count
        moment = jnp.zeros((128, 128), F32)
        for rb in range(ROWS // BLK):
            base = rb * BLK
            row = lax.broadcasted_iota(jnp.int32, (BLK, 1), 0) + base
            d = jnp.where((row >= lo_d) & (row < hi_d), xd[pl.ds(base, BLK), :] - mu, 0.0)
            moment = moment + dot_t(d, d, HIGHEST)
        ri = lax.broadcasted_iota(jnp.int32, (128, 128), 0)
        ci = lax.broadcasted_iota(jnp.int32, (128, 128), 1)
        moment = jnp.where(ri // 16 == ci // 16, moment, 0.0)
        wrow = wst[...]
        v = dot(moment, wrow, HIGHEST)
        block8 = (
            lax.broadcasted_iota(jnp.int32, (8, 128), 0)
            == lax.broadcasted_iota(jnp.int32, (8, 128), 1) // 16
        ).astype(F32)
        u8 = dot(block8 * mu, wrow, HIGHEST)
        q8 = dot(block8, v * wrow, HIGHEST)
        tcol = jnp.sum(jnp.where(ri == ci, sums, 0.0), axis=1, keepdims=True)
        tc[...] = jnp.broadcast_to(tcol, (128, 128))
        e15 = (lax.broadcasted_iota(jnp.int32, (16, 1), 0) == 15).astype(F32)
        for s, (_slot, _off, n) in enumerate(segs):
            n_even = n.astype(F32)
            n_odd = n_even - 1.0
            n_all = n_even + n_odd
            ue, uo = u8[2 * s : 2 * s + 1], u8[2 * s + 1 : 2 * s + 2]
            mean = (n_even * ue + n_odd * uo) / n_all
            de, do = ue - mean, uo - mean
            spread = (
                q8[2 * s : 2 * s + 1] + q8[2 * s + 1 : 2 * s + 2]
                + n_even * de * de + n_odd * do * do
            ) / n_all
            inv = lax.rsqrt(spread + 1e-05)
            a = gain[...] * inv
            b = bias[...] - a * mean
            im[s : s + 1, :] = inv
            im[4 + s : 5 + s, :] = mean
            for g, dev in enumerate((de, do)):
                at = 32 * s + 16 * g
                nst[at : at + 16, :] = v[at : at + 16] + tcol[at : at + 16] * dev
                f = wrow[at : at + 16] * a + e15 * b
                p0 = f.astype(BF16)
                f = f - p0.astype(F32)
                p1 = f.astype(BF16)
                f = f - p1.astype(F32)
                cols = pl.ds(g * CH, CH)
                wbig[64 * s : 64 * s + 16, cols] = p0
                wbig[64 * s + 16 : 64 * s + 32, cols] = p1
                wbig[64 * s + 32 : 64 * s + 48, cols] = f.astype(BF16)
                wbig[64 * s + 48 : 64 * s + 64, cols] = jnp.zeros((16, CH), BF16)
        acc[...] = jnp.zeros_like(acc)

    base = pl.multiple_of(step * BLK, BLK)
    pre_e = dot(xbig[pl.ds(base, BLK + 16), :], wbig[:, :CH])
    pre_o = dot(xbig[pl.ds(base, BLK), :], wbig[:, CH:])
    c_e, s_e = cdf_slope(pre_e)
    act_e = pre_e * c_e
    c_o, s_o = cdf_slope(pre_o)
    sl[0] = s_e[:BLK]
    sl[1] = s_o
    taps = jnp.concatenate(
        [act_e[:BLK].astype(BF16), (pre_o * c_o).astype(BF16), act_e[1 : BLK + 1].astype(BF16)], axis=1
    )
    late = dot(taps, w2[...])
    _c, slope = cdf_slope(late)
    row = lax.broadcasted_iota(jnp.int32, (BLK, 1), 0) + base
    drop = row == segs[0][1] + segs[0][2] - 1
    for _s, off, n in segs[1:]:
        drop = drop | (row == off + n - 1)
    grad = jnp.where(drop, 0.0, cot[...].astype(F32) * slope).astype(BF16)
    lg[...] = grad
    acc[...] += dot_t(grad, taps)

    @pl.when(step == pl.num_programs(0) - 1)
    def _():
        core = sc[8]
        for x in range(4):
            mine = pl.ds(pl.multiple_of(x * 128 + core * 64, 64), 64)
            other = pl.ds(pl.multiple_of(x * 128 + (1 - core) * 64, 64), 64)
            keep[x] = acc[mine, :]
            send[x] = acc[other, :].astype(BF16)


def backward_kernel(sc, lg, sl, xs, wt, wst, gain, nst, tc, im, out, acc, carry):
    step = pl.program_id(0)

    @pl.when(step == 0)
    def _():
        acc[...] = jnp.zeros_like(acc)
        carry[...] = jnp.zeros_like(carry)

    grad = lg[...]
    third = dot(grad, wt[:, 2 * CH :])
    row = lax.broadcasted_iota(jnp.int32, (BLK, 1), 0)
    shifted = jnp.where(row == 0, carry[0:1, :], pltpu.roll(third, 1, 0))
    carry[0:1, :] = third[BLK - 1 : BLK]
    ag_e = (dot(grad, wt[:, :CH]) + shifted) * sl[0]
    ag_o = dot(grad, wt[:, CH : 2 * CH]) * sl[1]
    total = acc[...]
    for part, ag in ((xs[0], ag_e), (xs[1], ag_o)):
        high = ag.astype(BF16)
        low = (ag - high.astype(F32)).astype(BF16)
        total = total + dot_t(part, high) + dot_t(part, low)
    acc[...] = total

    @pl.when(step == pl.num_programs(0) - 1)
    def _():
        segs = plan(sc)
        z = jnp.zeros((32, CH), F32)
        g_bias = jnp.zeros((1, CH), F32)
        g_gain = jnp.zeros((1, CH), F32)
        g = gain[...]
        for s, (_slot, _off, n) in enumerate(segs):
            at = 32 * s
            a = acc[at : at + 32, :]
            inv, mean = im[s : s + 1, :], im[4 + s : 5 + s, :]
            count = 2.0 * n.astype(F32) - 1.0
            s1 = a[15:16] + a[31:32]
            s2 = inv * (jnp.sum(a * wst[at : at + 32, :], axis=0, keepdims=True) - mean * s1)
            first = g * s1 / count
            cross = g * s2 / count
            z = z + inv * (
                g * a - first * tc[at : at + 32, 0:1] - (cross * inv) * nst[at : at + 32, :]
            )
            g_bias = g_bias + s1
            g_gain = g_gain + s2
        out[0:10, :] = z[0:10] + z[21:31]
        out[10:11, :] = g_gain
        out[11:12, :] = g_bias
        out[12:16, :] = jnp.zeros((4, CH), F32)


def full(shape):
    return pl.BlockSpec(shape, lambda i, sc: (0,) * len(shape))


def forward(sc, u, cot, wst, gain, bias, w2):
    shapes = [
        ((ROWS, CH), BF16, pl.BlockSpec((BLK, CH), lambda i, sc: (i, 0))),
        ((2, ROWS, CH), F32, pl.BlockSpec((2, BLK, CH), lambda i, sc: (0, i, 0))),
        ((4, 64, 3 * CH), F32, None),
        ((4, 64, 3 * CH), BF16, None),
        ((2, ROWS, 128), BF16, None),
        ((128, CH), F32, None),
        ((128, 128), F32, None),
        ((8, CH), F32, None),
    ]
    return pl.pallas_call(
        forward_kernel,
        grid_spec=pltpu.PrefetchScalarGridSpec(
            num_scalar_prefetch=1,
            grid=(ROWS // BLK,),
            in_specs=[
                full((SLOTS * GRAN, 128)),
                pl.BlockSpec((BLK, CH), lambda i, sc: (i, 0)),
                full((128, CH)), full((1, CH)), full((1, CH)), full((3 * CH, CH)),
            ],
            out_specs=[full(s) if b is None else b for s, _d, b in shapes],
            scratch_shapes=[
                pltpu.VMEM((ROWS + GRAN, 128), F32),
                pltpu.VMEM((ROWS, 128), F32),
                pltpu.VMEM((ROWS + 16, 256), BF16),
                pltpu.VMEM((256, 2 * CH), BF16),
                pltpu.VMEM((CH, 3 * CH), F32),
            ],
        ),
        out_shape=[jax.ShapeDtypeStruct(s, d) for s, d, _b in shapes],
        compiler_params=pltpu.CompilerParams(vmem_limit_bytes=50 * 2**20),
        cost_estimate=pl.CostEstimate(flops=8 * 10**9, bytes_accessed=20 * 10**6, transcendentals=0),
        name="forward_window",
    )(sc, u, cot, wst, gain, bias, w2)


def backward(sc, lg, sl, xs, wt, wst, gain, nst, tc, im):
    return pl.pallas_call(
        backward_kernel,
        grid_spec=pltpu.PrefetchScalarGridSpec(
            num_scalar_prefetch=1,
            grid=(ROWS // BLK,),
            in_specs=[
                pl.BlockSpec((BLK, CH), lambda i, sc: (i, 0)),
                pl.BlockSpec((2, BLK, CH), lambda i, sc: (0, i, 0)),
                pl.BlockSpec((2, BLK, 128), lambda i, sc: (0, i, 0)),
                full((CH, 3 * CH)), full((128, CH)), full((1, CH)),
                full((128, CH)), full((128, 128)), full((8, CH)),
            ],
            out_specs=full((16, CH)),
            scratch_shapes=[pltpu.VMEM((128, CH), F32), pltpu.VMEM((8, CH), F32)],
        ),
        out_shape=jax.ShapeDtypeStruct((16, CH), F32),
        compiler_params=pltpu.CompilerParams(vmem_limit_bytes=40 * 2**20),
        cost_estimate=pl.CostEstimate(flops=5 * 10**9, bytes_accessed=14 * 10**6, transcendentals=0),
        name="backward_window",
    )(sc, lg, sl, xs, wt, wst, gain, nst, tc, im)


def swap(value, axis, bit):
    count = 8 if axis == "bulk" else 32
    return lax.ppermute(value, axis, [(i, i ^ bit) for i in range(count)])


def route(rows, sizes, masks):
    units = sizes // TAPS
    extra = jnp.stack([(units // 32).astype(BF16), (units % 32).astype(BF16)], axis=1)
    value = jnp.concatenate([rows, jnp.pad(extra, ((0, 0), (0, 126)))], axis=1)
    for bit in (1, 2, 4, 8, 16):
        moved = swap(value, "wide", bit)
        value = jnp.where(((masks & bit) != 0)[:, None], moved, value)
    tail = value[:, -128:-126].astype(F32)
    return value[:, :-128], (tail[:, 0] * 32.0 + tail[:, 1]).astype(jnp.int32)


def window_inputs(conv_first):
    w = conv_first.astype(F32)
    even = jnp.pad(w, ((0, 6), (0, 0)))
    odd = jnp.pad(w, ((5, 1), (0, 0)))
    return jnp.tile(jnp.concatenate([even, odd], axis=0), (SLOTS, 1))


def halve(pair, bit, axis, dtype, mask):
    low, high = pair
    flag = bit == 1
    mine = jnp.where(flag, high, low)
    other = jnp.where(flag, low, high).astype(dtype)
    return mine + swap(other, axis, mask).astype(F32)


def local(rows, units, sources, core, cot, conv_first, norm_gain, norm_bias, conv_second):
    u = jnp.pad(rows.reshape(SLOTS * GRAN, TAPS).astype(F32), ((0, 0), (0, 128 - TAPS)))
    sc = jnp.concatenate([units, sources, jnp.full((8,), core, jnp.int32)])
    wst = window_inputs(conv_first)
    gain, bias = norm_gain[None, :], norm_bias[None, :]
    lg, sl, keep, send, xs, nst, tc, im = forward(sc, u, cot, wst, gain, bias, conv_second)
    small = backward(sc, lg, sl, xs, conv_second.T, wst, gain, nst, tc, im)
    return keep, send, small


def per_device(waveforms, owner_of, lengths, cotangent, conv_first, norm_gain, norm_bias, conv_second):
    me = lax.axis_index("wide")
    place = lax.axis_index("bulk")
    masks = jnp.bitwise_xor(owner_of[0], me)
    rows, units = route(waveforms[0], lengths[0], masks)
    keep, send, small = local(
        rows, units, jnp.bitwise_xor(masks, me), place % 2, cotangent[0, 0],
        conv_first, norm_gain, norm_bias, conv_second,
    )
    total = keep + swap(send, "bulk", 1).astype(F32)

    x, y, z = place // 2, me // 8, me % 8
    t = total.reshape(2, 2, 64, 3 * CH)
    t = halve((t[:, 0], t[:, 1]), x % 2, "bulk", BF16, 2)
    q = [t[:, :, 384 * k : 384 * (k + 1)] for k in range(4)]
    t = halve(
        (jnp.stack([q[0], q[2]]), jnp.stack([q[1], q[3]])), y % 2, "wide", BF16, 8
    )
    t = halve((t[:, 0], t[:, 1]), x // 2, "bulk", BF16, 4)
    t = halve((t[0], t[1]), y // 2, "wide", F32, 16)
    t = t.T.reshape(8, 48, 64)
    t = t.reshape(4, 2, 48, 64)
    t = halve((t[:, 0], t[:, 1]), z % 2, "wide", F32, 1)
    t = t.reshape(2, 2, 48, 64)
    t = halve((t[:, 0], t[:, 1]), (z // 2) % 2, "wide", F32, 2)
    grad_second = halve((t[0], t[1]), z // 4, "wide", F32, 4)

    for axis, mask in (("bulk", 1), ("bulk", 2), ("bulk", 4), ("wide", 1), ("wide", 2), ("wide", 4), ("wide", 8), ("wide", 16)):
        small = small + swap(small, axis, mask)
    return (grad_second, small[:10], small[10], small[11])


def solution(mesh):
    placed = (
        P("bulk", "wide", None),
        P("bulk", "wide"),
        P("bulk", "wide"),
        P("bulk", "wide", None, None),
        P(),
        P(),
        P(),
        P(),
    )
    return jax.shard_map(
        per_device,
        mesh=mesh,
        in_specs=placed,
        out_specs=(P("wide", "bulk"), P(), P(), P()),
        check_vma=False,
    )
```

```python
import functools

import jax
import jax.numpy as jnp
from jax import lax
from jax.experimental import pallas as pl
from jax.experimental.pallas import tpu as pltpu
from jax.sharding import PartitionSpec as P

F32 = jnp.float32
BF16 = jnp.bfloat16
HIGHEST = lax.Precision.HIGHEST
SLOTS = 4
TAPS = 10
GRAN = 1024
ROWS = 2048
CH = 512
BLK = 256
BLOCKS = [(2 * xh + xl, 2 * yh + yl) for xl in range(2) for yl in range(2) for xh in range(2) for yh in range(2)]


def dot(a, b, precision=None):
    return jnp.dot(a, b, preferred_element_type=F32, precision=precision)


def dot_t(a, b, precision=None):
    return lax.dot_general(
        a, b, (((0,), (0,)), ((), ())), preferred_element_type=F32, precision=precision
    )


def cdf_slope(v):
    e = jnp.exp2(v * v * (-0.5 * 1.4426950408889634))
    d = 1.0 + jnp.abs(v) * (0.3275911 * 0.7071067811865476)
    r = pl.reciprocal(d, approx=True)
    t = r * (2.0 - d * r)
    poly = 0.5 * 1.061405429
    for c in (-1.453152027, 1.421413741, -0.284496736, 0.254829592):
        poly = poly * t + 0.5 * c
    tail = poly * t * e
    cdf = jnp.where(v < 0.0, tail, 1.0 - tail)
    return cdf, cdf + v * (e * 0.3989422804014327)


def plan(sc):
    size = [sc[s] for s in range(SLOTS)]
    src = [sc[SLOTS + s] for s in range(SLOTS)]
    rank, off = [], []
    for s in range(SLOTS):
        before = [(src[q] < src[s]).astype(jnp.int32) for q in range(SLOTS) if q != s]
        sizes = [size[q] for q in range(SLOTS) if q != s]
        rank.append(sum(before))
        off.append(sum(b * n for b, n in zip(before, sizes)))
    out = []
    for r in range(SLOTS):
        hit = [(rank[s] == r).astype(jnp.int32) for s in range(SLOTS)]
        out.append(
            (
                sum(h * s for s, h in enumerate(hit)),
                sum(h * o for o, h in zip(off, hit)),
                sum(h * n for n, h in zip(size, hit)),
            )
        )
    return out


def by_lane(values, index):
    out = values[0]
    for s in range(1, len(values)):
        out = jnp.where(index == s, values[s], out)
    return out


def window_kernel(
    sc, u, cot, wst, gain, bias, w2, wt,
    keep, send, small,
    buf, xd, xbig, xs, wbig, acc, nst, tc, im, grads, carry,
):
    step = pl.program_id(0)
    segs = plan(sc)

    @pl.when(step == 0)
    def _():
        buf[...] = jnp.zeros_like(buf)
        for slot, off, _n in segs:
            piece = u[pl.ds(pl.multiple_of(slot * GRAN, GRAN), GRAN), :].astype(F32)
            buf[pl.ds(off, GRAN), 0:TAPS] = piece
        src = lax.broadcasted_iota(jnp.int32, (128, 256), 0)
        tap = lax.broadcasted_iota(jnp.int32, (128, 256), 1) % 16
        r0 = ((tap == src) & (src < TAPS)).astype(F32).astype(BF16)
        r1 = ((tap == src + TAPS) & (src < 5)).astype(F32).astype(BF16)
        one = (lax.broadcasted_iota(jnp.int32, (1, 256), 1) % 16 == 15).astype(F32)
        lane = lax.broadcasted_iota(jnp.int32, (1, 256), 1)
        starts = [o for _s, o, _n in segs]
        ends = [o + n for _s, o, n in segs]
        lo_big, hi_big = by_lane(starts, lane // 64), by_lane(ends, lane // 64)
        lane1 = lane[:, :128]
        odd = (lane1 // 16) % 2
        lo_d = by_lane(starts, lane1 // 32)
        hi_all = by_lane(ends, lane1 // 32)
        hi_d = hi_all - odd
        count = (hi_d - lo_d).astype(F32)

        sums = jnp.zeros((1, 128), F32)
        for rb in range(ROWS // BLK):
            base = rb * BLK
            b0 = buf[pl.ds(base, BLK), :].astype(BF16)
            b1 = buf[pl.ds(base + 1, BLK), :].astype(BF16)
            xr = dot(b0, r0) + dot(b1, r1) + one
            row = lax.broadcasted_iota(jnp.int32, (BLK, 1), 0) + base
            xbig[pl.ds(base, BLK), :] = jnp.where((row >= lo_big) & (row < hi_big), xr, 0.0).astype(BF16)
            x1 = xr[:, :128]
            raw = jnp.where((row >= lo_d) & (row < hi_d), x1, 0.0)
            sums = sums + jnp.sum(raw, axis=0, keepdims=True)
            xd[pl.ds(base, BLK), :] = x1
            full = jnp.where((row >= lo_d) & (row < hi_all), x1, 0.0)
            xs[0, pl.ds(base, BLK), :] = jnp.where(odd == 0, full, 0.0).astype(BF16)
            xs[1, pl.ds(base, BLK), :] = jnp.where(odd == 1, full, 0.0).astype(BF16)
        xbig[pl.ds(ROWS, 16), :] = jnp.zeros((16, 256), BF16)
        mu = sums / count
        moment = jnp.zeros((128, 128), F32)
        for rb in range(ROWS // BLK):
            base = rb * BLK
            row = lax.broadcasted_iota(jnp.int32, (BLK, 1), 0) + base
            d = jnp.where((row >= lo_d) & (row < hi_d), xd[pl.ds(base, BLK), :] - mu, 0.0)
            moment = moment + dot_t(d, d, HIGHEST)
        ri = lax.broadcasted_iota(jnp.int32, (128, 128), 0)
        ci = lax.broadcasted_iota(jnp.int32, (128, 128), 1)
        moment = jnp.where(ri // 16 == ci // 16, moment, 0.0)
        wrow = wst[...]
        v = dot(moment, wrow, HIGHEST)
        block8 = (
            lax.broadcasted_iota(jnp.int32, (8, 128), 0)
            == lax.broadcasted_iota(jnp.int32, (8, 128), 1) // 16
        ).astype(F32)
        u8 = dot(block8 * mu, wrow, HIGHEST)
        q8 = dot(block8, v * wrow, HIGHEST)
        tcol = jnp.sum(jnp.where(ri == ci, sums, 0.0), axis=1, keepdims=True)
        tc[...] = jnp.broadcast_to(tcol, (128, 128))
        e15 = (lax.broadcasted_iota(jnp.int32, (16, 1), 0) == 15).astype(F32)
        for s, (_slot, _off, n) in enumerate(segs):
            n_even = n.astype(F32)
            n_odd = n_even - 1.0
            n_all = n_even + n_odd
            ue, uo = u8[2 * s : 2 * s + 1], u8[2 * s + 1 : 2 * s + 2]
            mean = (n_even * ue + n_odd * uo) / n_all
            de, do = ue - mean, uo - mean
            spread = (
                q8[2 * s : 2 * s + 1] + q8[2 * s + 1 : 2 * s + 2]
                + n_even * de * de + n_odd * do * do
            ) / n_all
            inv = lax.rsqrt(spread + 1e-05)
            a = gain[...] * inv
            b = bias[...] - a * mean
            im[s : s + 1, :] = inv
            im[4 + s : 5 + s, :] = mean
            for g, dev in enumerate((de, do)):
                at = 32 * s + 16 * g
                nst[at : at + 16, :] = v[at : at + 16] + tcol[at : at + 16] * dev
                f = wrow[at : at + 16] * a + e15 * b
                p0 = f.astype(BF16)
                f = f - p0.astype(F32)
                p1 = f.astype(BF16)
                f = f - p1.astype(F32)
                cols = pl.ds(g * CH, CH)
                wbig[64 * s : 64 * s + 16, cols] = p0
                wbig[64 * s + 16 : 64 * s + 32, cols] = p1
                wbig[64 * s + 32 : 64 * s + 48, cols] = f.astype(BF16)
                wbig[64 * s + 48 : 64 * s + 64, cols] = jnp.zeros((16, CH), BF16)
        acc[...] = jnp.zeros_like(acc)
        grads[...] = jnp.zeros_like(grads)
        carry[...] = jnp.zeros_like(carry)

    base = pl.multiple_of(step * BLK, BLK)
    pre_e = dot(xbig[pl.ds(base, BLK + 16), :], wbig[:, :CH])
    pre_o = dot(xbig[pl.ds(base, BLK), :], wbig[:, CH:])
    c_e, s_e = cdf_slope(pre_e)
    act_e = pre_e * c_e
    c_o, s_o = cdf_slope(pre_o)
    taps = jnp.concatenate(
        [act_e[:BLK].astype(BF16), (pre_o * c_o).astype(BF16), act_e[1 : BLK + 1].astype(BF16)], axis=1
    )
    late = dot(taps, w2[...])
    _c, slope = cdf_slope(late)
    row = lax.broadcasted_iota(jnp.int32, (BLK, 1), 0) + base
    drop = row == segs[0][1] + segs[0][2] - 1
    for _s, off, n in segs[1:]:
        drop = drop | (row == off + n - 1)
    grad = jnp.where(drop, 0.0, cot[...].astype(F32) * slope).astype(BF16)
    acc[...] += dot_t(grad, taps)

    third = dot(grad, wt[:, 2 * CH :])
    row = lax.broadcasted_iota(jnp.int32, (BLK, 1), 0)
    shifted = jnp.where(row == 0, carry[0:1, :], pltpu.roll(third, 1, 0))
    carry[0:1, :] = third[BLK - 1 : BLK]
    ag_e = (dot(grad, wt[:, :CH]) + shifted) * s_e[:BLK]
    ag_o = dot(grad, wt[:, CH : 2 * CH]) * s_o
    total = grads[...]
    for g, ag in enumerate((ag_e, ag_o)):
        part = xs[g, pl.ds(base, BLK), :]
        high = ag.astype(BF16)
        low = (ag - high.astype(F32)).astype(BF16)
        total = total + dot_t(part, high) + dot_t(part, low)
    grads[...] = total

    @pl.when(step == pl.num_programs(0) - 1)
    def _():
        z = jnp.zeros((32, CH), F32)
        g_bias = jnp.zeros((1, CH), F32)
        g_gain = jnp.zeros((1, CH), F32)
        g = gain[...]
        for s, (_slot, _off, n) in enumerate(segs):
            at = 32 * s
            a = grads[at : at + 32, :]
            inv, mean = im[s : s + 1, :], im[4 + s : 5 + s, :]
            count = 2.0 * n.astype(F32) - 1.0
            s1 = a[15:16] + a[31:32]
            s2 = inv * (jnp.sum(a * wst[at : at + 32, :], axis=0, keepdims=True) - mean * s1)
            first = g * s1 / count
            cross = g * s2 / count
            z = z + inv * (
                g * a - first * tc[at : at + 32, 0:1] - (cross * inv) * nst[at : at + 32, :]
            )
            g_bias = g_bias + s1
            g_gain = g_gain + s2
        grads[0:10, :] = z[0:10] + z[21:31]
        grads[10:11, :] = g_gain
        grads[11:12, :] = g_bias
        small[0:12, :] = grads[0:12, 0:384]
        for j in range(3):
            small[12:16, 128 * j : 128 * (j + 1)] = grads[4 * j : 4 * j + 4, 384:512]
        core = sc[8]
        for k, (x, y) in enumerate(BLOCKS):
            lanes = pl.ds(384 * y, 384)
            rows = pl.ds(64 * k, 64)
            keep[rows, :] = acc[pl.ds(pl.multiple_of(x * 128 + core * 64, 64), 64), lanes]
            send[rows, :] = acc[
                pl.ds(pl.multiple_of(x * 128 + (1 - core) * 64, 64), 64), lanes
            ].astype(BF16)
        pack_small(small, send, 1024, True)


def pack_small(small, send, at, coarse):
    value = small[...]
    if not coarse:
        send[at : at + value.shape[0], :] = value
        return
    high = value.astype(BF16)
    low = (value - high.astype(F32)).astype(BF16)
    send[at : at + 16, :] = high
    send[at + 16 : at + 32, :] = low
    small[...] = high.astype(F32) + low.astype(F32)


def received_small(recv, at):
    if recv.dtype == F32:
        return recv[at:, :]
    return recv[at : at + 16, :].astype(F32) + recv[at + 16 : at + 32, :].astype(F32)


def combine_kernel(n, flag, coarse, sc, keep, small, recv, keep_out, small_out, send):
    half = n // 2
    mine = pl.ds(pl.multiple_of(sc[flag] * half, half), half)
    other = pl.ds(pl.multiple_of((1 - sc[flag]) * half, half), half)
    keep_out[...] = keep[mine, :] + recv[mine, :].astype(F32)
    send[0:half, :] = (keep[other, :] + recv[other, :].astype(F32)).astype(send.dtype)
    small_out[...] = small[...] + received_small(recv, n)
    pack_small(small_out, send, half, coarse)


def turn_kernel(sc, keep, small, recv, keep_out, small_out, send):
    total = (keep[...] + recv[0:64, :]).T
    total = jnp.concatenate([total[0:192], total[192:384]], axis=1)
    low = sc[13]
    for mid in range(2):
        even = total[96 * mid : 96 * mid + 48]
        odd = total[96 * mid + 48 : 96 * mid + 96]
        at = pl.ds(48 * mid, 48)
        keep_out[at, :] = jnp.where(low == 1, odd, even)
        send[at, :] = jnp.where(low == 1, even, odd)
    sums = small[...] + recv[64:80, :]
    for j in range(3):
        small_out[16 * j : 16 * j + 16, :] = sums[:, 128 * j : 128 * (j + 1)]
    send[96:144, :] = small_out[...]


def middle_kernel(sc, keep, small, recv, keep_out, small_out, send):
    mine = pl.ds(pl.multiple_of(sc[14] * 48, 8), 48)
    other = pl.ds(pl.multiple_of((1 - sc[14]) * 48, 8), 48)
    kept = keep[mine, :] + recv[mine, :]
    keep_out[...] = kept
    send[0:48, :] = keep[other, :] + recv[other, :]
    sums = small[...] + recv[96:144, :]
    small_out[...] = sums
    send[48:96, :] = sums


def last_kernel(sc, keep, small, recv, keep_out, small_out, send):
    del sc
    kept = keep[...] + recv[0:48, :]
    sums = small[...] + recv[48:96, :]
    keep_out[...] = kept
    small_out[...] = sums
    send[0:48, :] = kept
    send[48:96, :] = sums


def final_kernel(sc, keep, small, recv, second, first, g_gain, g_bias, flat):
    total = keep[...] + recv[0:48, :]
    second[...] = jnp.where(sc[15] == 1, total[:, 64:128], total[:, 0:64])
    sums = small[...] + recv[48:96, :]
    for j in range(3):
        part = sums[16 * j : 16 * j + 16]
        flat[0:12, 128 * j : 128 * (j + 1)] = part[0:12]
        flat[4 * j : 4 * j + 4, 384:512] = part[12:16]
    first[...] = flat[0:10, :]
    g_gain[...] = flat[10:11, :]
    g_bias[...] = flat[11:12, :]


def full(shape):
    return pl.BlockSpec(shape, lambda i, sc: (0,) * len(shape))


def window(sc, u, cot, wst, gain, bias, w2, wt):
    shapes = [((1024, 384), F32), ((1056, 384), BF16), ((16, 384), F32)]
    return pl.pallas_call(
        window_kernel,
        grid_spec=pltpu.PrefetchScalarGridSpec(
            num_scalar_prefetch=1,
            grid=(ROWS // BLK,),
            in_specs=[
                full((SLOTS * GRAN, TAPS)),
                pl.BlockSpec((BLK, CH), lambda i, sc: (i, 0)),
                full((128, CH)), full((1, CH)), full((1, CH)), full((3 * CH, CH)), full((CH, 3 * CH)),
            ],
            out_specs=[full(s) for s, _d in shapes],
            scratch_shapes=[
                pltpu.VMEM((ROWS + GRAN, 128), F32),
                pltpu.VMEM((ROWS, 128), F32),
                pltpu.VMEM((ROWS + 16, 256), BF16),
                pltpu.VMEM((2, ROWS, 128), BF16),
                pltpu.VMEM((256, 2 * CH), BF16),
                pltpu.VMEM((CH, 3 * CH), F32),
                pltpu.VMEM((128, CH), F32),
                pltpu.VMEM((128, 128), F32),
                pltpu.VMEM((8, CH), F32),
                pltpu.VMEM((128, CH), F32),
                pltpu.VMEM((8, CH), F32),
            ],
        ),
        out_shape=[jax.ShapeDtypeStruct(s, d) for s, d in shapes],
        compiler_params=pltpu.CompilerParams(vmem_limit_bytes=56 * 2**20),
        cost_estimate=pl.CostEstimate(flops=14 * 10**9, bytes_accessed=10 * 10**6, transcendentals=0),
        name="window",
    )(sc, u, cot, wst, gain, bias, w2, wt)


def small_call(kernel, name, sc, args, shapes, scratch=()):
    return pl.pallas_call(
        kernel,
        in_specs=[pl.BlockSpec(memory_space=pltpu.SMEM)] + [pl.BlockSpec(memory_space=pltpu.VMEM)] * len(args),
        out_specs=[pl.BlockSpec(memory_space=pltpu.VMEM)] * len(shapes),
        out_shape=[jax.ShapeDtypeStruct(s, d) for s, d in shapes],
        scratch_shapes=list(scratch),
        name=name,
    )(sc, *args)


def swap(value, axis, bit):
    count = 8 if axis == "bulk" else 32
    return lax.ppermute(value, axis, [(i, i ^ bit) for i in range(count)])


def route(rows, sizes, masks):
    units = sizes // TAPS
    extra = jnp.stack([(units // 32).astype(BF16), (units % 32).astype(BF16)], axis=1)
    value = jnp.concatenate([rows, jnp.pad(extra, ((0, 0), (0, 126)))], axis=1)
    for bit in (1, 2, 4, 8, 16):
        moved = swap(value, "wide", bit)
        value = jnp.where(((masks & bit) != 0)[:, None], moved, value)
    tail = value[:, -128:-126].astype(F32)
    return value[:, :-128], (tail[:, 0] * 32.0 + tail[:, 1]).astype(jnp.int32)


def window_inputs(conv_first):
    w = conv_first.astype(F32)
    even = jnp.pad(w, ((0, 6), (0, 0)))
    odd = jnp.pad(w, ((5, 1), (0, 0)))
    return jnp.tile(jnp.concatenate([even, odd], axis=0), (SLOTS, 1))


def local(rows, units, sources, places, cot, conv_first, norm_gain, norm_bias, conv_second):
    u = rows.reshape(SLOTS * GRAN, TAPS)
    sc = jnp.concatenate([units, sources, places])
    wst = window_inputs(conv_first)
    gain, bias = norm_gain[None, :], norm_bias[None, :]
    return sc, window(sc, u, cot, wst, gain, bias, conv_second, conv_second.T)


def per_device(waveforms, owner_of, lengths, cotangent, conv_first, norm_gain, norm_bias, conv_second):
    me = lax.axis_index("wide")
    place = lax.axis_index("bulk")
    masks = jnp.bitwise_xor(owner_of[0], me)
    rows, units = route(waveforms[0], lengths[0], masks)
    places = jnp.stack(
        [place % 2, (place // 2) % 2, (me // 8) % 2, place // 4, me // 16, me % 2, (me // 2) % 2, (me // 4) % 2]
    ).astype(jnp.int32)
    sc, (keep, send, small) = local(
        rows, units, jnp.bitwise_xor(masks, me), places, cotangent[0, 0],
        conv_first, norm_gain, norm_bias, conv_second,
    )
    n = 1024
    recv = swap(send, "bulk", 1)
    for flag, axis, bit, coarse in ((9, "bulk", 2, True), (10, "wide", 8, True), (11, "bulk", 4, True), (12, "wide", 16, False)):
        half = n // 2
        out = [
            ((half, 384), F32), ((16, 384), F32),
            ((half + 32, 384), BF16) if coarse else ((half + 16, 384), F32),
        ]
        kernel = functools.partial(combine_kernel, n, flag, coarse)
        keep, small, send = small_call(kernel, "combine%d" % n, sc, (keep, small, recv), out)
        recv = swap(send, axis, bit)
        n = half
    out = [((96, 128), F32), ((48, 128), F32), ((144, 128), F32)]
    keep, small, send = small_call(turn_kernel, "turn", sc, (keep, small, recv), out)
    recv = swap(send, "wide", 1)
    out = [((48, 128), F32), ((48, 128), F32), ((96, 128), F32)]
    keep, small, send = small_call(middle_kernel, "middle", sc, (keep, small, recv), out)
    recv = swap(send, "wide", 2)
    keep, small, send = small_call(last_kernel, "last", sc, (keep, small, recv), out)
    recv = swap(send, "wide", 4)
    out = [((48, 64), F32), ((10, CH), F32), ((1, CH), F32), ((1, CH), F32)]
    second, first, g_gain, g_bias = small_call(
        final_kernel, "final", sc, (keep, small, recv), out, [pltpu.VMEM((16, CH), F32)]
    )
    return (second, first, g_gain[0], g_bias[0])


def solution(mesh):
    placed = (
        P("bulk", "wide", None),
        P("bulk", "wide"),
        P("bulk", "wide"),
        P("bulk", "wide", None, None),
        P(),
        P(),
        P(),
        P(),
    )
    return jax.shard_map(
        per_device,
        mesh=mesh,
        in_specs=placed,
        out_specs=(P("wide", "bulk"), P(), P(), P()),
        check_vma=False,
    )
```

```python
import functools

import jax
import jax.numpy as jnp
from jax import lax
from jax.experimental import pallas as pl
from jax.experimental.pallas import tpu as pltpu
from jax.sharding import PartitionSpec as P

F32 = jnp.float32
BF16 = jnp.bfloat16
HIGHEST = lax.Precision.HIGHEST
SLOTS = 4
TAPS = 10
GRAN = 1024
ROWS = 2048
CH = 512
BLK = 256
BLOCKS = [
    (2 * xh + (xl ^ xh), 2 * yh + (yl ^ yh)) for xl in range(2) for yl in range(2) for xh in range(2) for yh in range(2)
]


def dot(a, b, precision=None):
    return jnp.dot(a, b, preferred_element_type=F32, precision=precision)


def dot_t(a, b, precision=None):
    return lax.dot_general(
        a, b, (((0,), (0,)), ((), ())), preferred_element_type=F32, precision=precision
    )


def cdf_slope(v):
    e = jnp.exp2(v * v * (-0.5 * 1.4426950408889634))
    d = 1.0 + jnp.abs(v) * (0.3275911 * 0.7071067811865476)
    r = pl.reciprocal(d, approx=True)
    t = r * (2.0 - d * r)
    poly = 0.5 * 1.061405429
    for c in (-1.453152027, 1.421413741, -0.284496736, 0.254829592):
        poly = poly * t + 0.5 * c
    tail = poly * t * e
    cdf = jnp.where(v < 0.0, tail, 1.0 - tail)
    return cdf, cdf + v * (e * 0.3989422804014327)


def plan(sc):
    size = [sc[s] for s in range(SLOTS)]
    src = [sc[SLOTS + s] for s in range(SLOTS)]
    rank, off = [], []
    for s in range(SLOTS):
        before = [(src[q] < src[s]).astype(jnp.int32) for q in range(SLOTS) if q != s]
        sizes = [size[q] for q in range(SLOTS) if q != s]
        rank.append(sum(before))
        off.append(sum(b * n for b, n in zip(before, sizes)))
    out = []
    for r in range(SLOTS):
        hit = [(rank[s] == r).astype(jnp.int32) for s in range(SLOTS)]
        out.append(
            (
                sum(h * s for s, h in enumerate(hit)),
                sum(h * o for o, h in zip(off, hit)),
                sum(h * n for n, h in zip(size, hit)),
            )
        )
    return out


def by_lane(values, index):
    out = values[0]
    for s in range(1, len(values)):
        out = jnp.where(index == s, values[s], out)
    return out


def window_kernel(
    sc, u, cot, wst, gain, bias, w2, wt,
    keep, send, small,
    buf, xd, xbig, xs, wbig, acc, nst, tc, im, grads, carry,
):
    step = pl.program_id(0)
    segs = plan(sc)

    @pl.when(step == 0)
    def _():
        buf[...] = jnp.zeros_like(buf)
        for slot, off, _n in segs:
            piece = u[pl.ds(pl.multiple_of(slot * GRAN, GRAN), GRAN), :].astype(F32)
            buf[pl.ds(off, GRAN), 0:TAPS] = piece
        src = lax.broadcasted_iota(jnp.int32, (128, 256), 0)
        tap = lax.broadcasted_iota(jnp.int32, (128, 256), 1) % 16
        r0 = ((tap == src) & (src < TAPS)).astype(F32).astype(BF16)
        r1 = ((tap == src + TAPS) & (src < 5)).astype(F32).astype(BF16)
        one = (lax.broadcasted_iota(jnp.int32, (1, 256), 1) % 16 == 15).astype(F32)
        lane = lax.broadcasted_iota(jnp.int32, (1, 256), 1)
        starts = [o for _s, o, _n in segs]
        ends = [o + n for _s, o, n in segs]
        lo_big, hi_big = by_lane(starts, lane // 64), by_lane(ends, lane // 64)
        lane1 = lane[:, :128]
        odd = (lane1 // 16) % 2
        lo_d = by_lane(starts, lane1 // 32)
        hi_all = by_lane(ends, lane1 // 32)
        hi_d = hi_all - odd
        count = (hi_d - lo_d).astype(F32)

        sums = jnp.zeros((1, 128), F32)
        for rb in range(ROWS // BLK):
            base = rb * BLK
            b0 = buf[pl.ds(base, BLK), :].astype(BF16)
            b1 = buf[pl.ds(base + 1, BLK), :].astype(BF16)
            xr = dot(b0, r0) + dot(b1, r1) + one
            row = lax.broadcasted_iota(jnp.int32, (BLK, 1), 0) + base
            xbig[pl.ds(base, BLK), :] = jnp.where((row >= lo_big) & (row < hi_big), xr, 0.0).astype(BF16)
            x1 = xr[:, :128]
            raw = jnp.where((row >= lo_d) & (row < hi_d), x1, 0.0)
            sums = sums + jnp.sum(raw, axis=0, keepdims=True)
            xd[pl.ds(base, BLK), :] = x1
            full = jnp.where((row >= lo_d) & (row < hi_all), x1, 0.0)
            xs[0, pl.ds(base, BLK), :] = jnp.where(odd == 0, full, 0.0).astype(BF16)
            xs[1, pl.ds(base, BLK), :] = jnp.where(odd == 1, full, 0.0).astype(BF16)
        xbig[pl.ds(ROWS, 16), :] = jnp.zeros((16, 256), BF16)
        mu = sums / count
        moment = jnp.zeros((128, 128), F32)
        for rb in range(ROWS // BLK):
            base = rb * BLK
            row = lax.broadcasted_iota(jnp.int32, (BLK, 1), 0) + base
            d = jnp.where((row >= lo_d) & (row < hi_d), xd[pl.ds(base, BLK), :] - mu, 0.0)
            moment = moment + dot_t(d, d, HIGHEST)
        ri = lax.broadcasted_iota(jnp.int32, (128, 128), 0)
        ci = lax.broadcasted_iota(jnp.int32, (128, 128), 1)
        moment = jnp.where(ri // 16 == ci // 16, moment, 0.0)
        wrow = jnp.concatenate([wst[...]] * SLOTS, axis=0)
        v = dot(moment, wrow, HIGHEST)
        block8 = (
            lax.broadcasted_iota(jnp.int32, (8, 128), 0)
            == lax.broadcasted_iota(jnp.int32, (8, 128), 1) // 16
        ).astype(F32)
        u8 = dot(block8 * mu, wrow, HIGHEST)
        q8 = dot(block8, v * wrow, HIGHEST)
        tcol = jnp.sum(jnp.where(ri == ci, sums, 0.0), axis=1, keepdims=True)
        tc[...] = jnp.broadcast_to(tcol, (128, 128))
        e15 = (lax.broadcasted_iota(jnp.int32, (16, 1), 0) == 15).astype(F32)
        for s, (_slot, _off, n) in enumerate(segs):
            n_even = n.astype(F32)
            n_odd = n_even - 1.0
            n_all = n_even + n_odd
            ue, uo = u8[2 * s : 2 * s + 1], u8[2 * s + 1 : 2 * s + 2]
            mean = (n_even * ue + n_odd * uo) / n_all
            de, do = ue - mean, uo - mean
            spread = (
                q8[2 * s : 2 * s + 1] + q8[2 * s + 1 : 2 * s + 2]
                + n_even * de * de + n_odd * do * do
            ) / n_all
            inv = lax.rsqrt(spread + 1e-05)
            a = gain[...] * inv
            b = bias[...] - a * mean
            im[s : s + 1, :] = inv
            im[4 + s : 5 + s, :] = mean
            for g, dev in enumerate((de, do)):
                at = 32 * s + 16 * g
                nst[at : at + 16, :] = v[at : at + 16] + tcol[at : at + 16] * dev
                f = wrow[at : at + 16] * a + e15 * b
                p0 = f.astype(BF16)
                f = f - p0.astype(F32)
                p1 = f.astype(BF16)
                f = f - p1.astype(F32)
                cols = pl.ds(g * CH, CH)
                wbig[64 * s : 64 * s + 16, cols] = p0
                wbig[64 * s + 16 : 64 * s + 32, cols] = p1
                wbig[64 * s + 32 : 64 * s + 48, cols] = f.astype(BF16)
                wbig[64 * s + 48 : 64 * s + 64, cols] = jnp.zeros((16, CH), BF16)
        acc[...] = jnp.zeros_like(acc)
        grads[...] = jnp.zeros_like(grads)
        carry[...] = jnp.zeros_like(carry)

    base = pl.multiple_of(step * BLK, BLK)
    pre_e = dot(xbig[pl.ds(base, BLK + 16), :], wbig[:, :CH])
    pre_o = dot(xbig[pl.ds(base, BLK), :], wbig[:, CH:])
    c_e, s_e = cdf_slope(pre_e)
    act_e = pre_e * c_e
    c_o, s_o = cdf_slope(pre_o)
    taps = jnp.concatenate(
        [act_e[:BLK].astype(BF16), (pre_o * c_o).astype(BF16), act_e[1 : BLK + 1].astype(BF16)], axis=1
    )
    late = dot(taps, w2[...])
    _c, slope = cdf_slope(late)
    row = lax.broadcasted_iota(jnp.int32, (BLK, 1), 0) + base
    drop = row == segs[0][1] + segs[0][2] - 1
    for _s, off, n in segs[1:]:
        drop = drop | (row == off + n - 1)
    grad = jnp.where(drop, 0.0, cot[...].astype(F32) * slope).astype(BF16)
    acc[...] += dot_t(grad, taps)

    third = dot(grad, wt[:, 2 * CH :])
    row = lax.broadcasted_iota(jnp.int32, (BLK, 1), 0)
    shifted = jnp.where(row == 0, carry[0:1, :], pltpu.roll(third, 1, 0))
    carry[0:1, :] = third[BLK - 1 : BLK]
    ag_e = (dot(grad, wt[:, :CH]) + shifted) * s_e[:BLK]
    ag_o = dot(grad, wt[:, CH : 2 * CH]) * s_o
    total = grads[...]
    for g, ag in enumerate((ag_e, ag_o)):
        part = xs[g, pl.ds(base, BLK), :]
        high = ag.astype(BF16)
        low = (ag - high.astype(F32)).astype(BF16)
        total = total + dot_t(part, high) + dot_t(part, low)
    grads[...] = total

    @pl.when(step == pl.num_programs(0) - 1)
    def _():
        z = jnp.zeros((32, CH), F32)
        g_bias = jnp.zeros((1, CH), F32)
        g_gain = jnp.zeros((1, CH), F32)
        g = gain[...]
        for s, (_slot, _off, n) in enumerate(segs):
            at = 32 * s
            a = grads[at : at + 32, :]
            inv, mean = im[s : s + 1, :], im[4 + s : 5 + s, :]
            count = 2.0 * n.astype(F32) - 1.0
            s1 = a[15:16] + a[31:32]
            s2 = inv * (jnp.sum(a * wst[...], axis=0, keepdims=True) - mean * s1)
            first = g * s1 / count
            cross = g * s2 / count
            z = z + inv * (
                g * a - first * tc[at : at + 32, 0:1] - (cross * inv) * nst[at : at + 32, :]
            )
            g_bias = g_bias + s1
            g_gain = g_gain + s2
        grads[0:10, :] = z[0:10] + z[21:31]
        grads[10:11, :] = g_gain
        grads[11:12, :] = g_bias
        small[0:12, :] = grads[0:12, 0:384]
        for j in range(3):
            small[12:16, 128 * j : 128 * (j + 1)] = grads[4 * j : 4 * j + 4, 384:512]
        core = sc[8]
        for k, (x, y) in enumerate(BLOCKS):
            lanes = pl.ds(384 * y, 384)
            rows = pl.ds(64 * k, 64)
            keep[rows, :] = acc[pl.ds(pl.multiple_of(x * 128 + core * 64, 64), 64), lanes]
            send[rows, :] = acc[
                pl.ds(pl.multiple_of(x * 128 + (1 - core) * 64, 64), 64), lanes
            ].astype(BF16)
        pack_small(small, send, 1024, True)


def pack_small(small, send, at, coarse):
    value = small[...]
    if not coarse:
        send[at : at + value.shape[0], :] = value
        return
    high = value.astype(BF16)
    low = (value - high.astype(F32)).astype(BF16)
    send[at : at + 16, :] = high
    send[at + 16 : at + 32, :] = low
    small[...] = high.astype(F32) + low.astype(F32)


def received_small(recv, at):
    if recv.dtype == F32:
        return recv[at:, :]
    return recv[at : at + 16, :].astype(F32) + recv[at + 16 : at + 32, :].astype(F32)


def combine_kernel(n, flag, coarse, sc, keep, small, recv, keep_out, small_out, send):
    half = n // 2
    mine = pl.ds(pl.multiple_of(sc[flag] * half, half), half)
    other = pl.ds(pl.multiple_of((1 - sc[flag]) * half, half), half)
    keep_out[...] = keep[mine, :] + recv[mine, :].astype(F32)
    send[0:half, :] = (keep[other, :] + recv[other, :].astype(F32)).astype(send.dtype)
    small_out[...] = small[...] + received_small(recv, n)
    pack_small(small_out, send, half, coarse)


def turn_kernel(sc, keep, small, recv, keep_out, small_out, send):
    total = (keep[...] + recv[0:64, :]).T
    low = sc[13]
    for mid in range(2):
        halves = []
        for bit in range(2):
            at = [192 * high + 96 * (mid ^ high) + 48 * (bit ^ high) for high in range(2)]
            halves.append(jnp.concatenate([total[at[0] : at[0] + 48], total[at[1] : at[1] + 48]], axis=1))
        rows = pl.ds(48 * mid, 48)
        keep_out[rows, :] = jnp.where(low == 1, halves[1], halves[0])
        send[rows, :] = jnp.where(low == 1, halves[0], halves[1])
    sums = small[...] + recv[64:80, :]
    for j in range(3):
        small_out[16 * j : 16 * j + 16, :] = sums[:, 128 * j : 128 * (j + 1)]
    send[96:144, :] = small_out[...]


def middle_kernel(sc, keep, small, recv, keep_out, small_out, send):
    mine = pl.ds(pl.multiple_of(sc[14] * 48, 8), 48)
    other = pl.ds(pl.multiple_of((1 - sc[14]) * 48, 8), 48)
    kept = keep[mine, :] + recv[mine, :]
    keep_out[...] = kept
    send[0:48, :] = keep[other, :] + recv[other, :]
    sums = small[...] + recv[96:144, :]
    small_out[...] = sums
    send[48:96, :] = sums


def last_kernel(sc, keep, small, recv, keep_out, small_out, send):
    del sc
    kept = keep[...] + recv[0:48, :]
    sums = small[...] + recv[48:96, :]
    keep_out[...] = kept
    small_out[...] = sums
    send[0:48, :] = kept
    send[48:96, :] = sums


def final_kernel(sc, keep, small, recv, second, first, g_gain, g_bias, flat):
    total = keep[...] + recv[0:48, :]
    second[...] = jnp.where(sc[15] == 1, total[:, 64:128], total[:, 0:64])
    sums = small[...] + recv[48:96, :]
    for j in range(3):
        part = sums[16 * j : 16 * j + 16]
        flat[0:12, 128 * j : 128 * (j + 1)] = part[0:12]
        flat[4 * j : 4 * j + 4, 384:512] = part[12:16]
    first[...] = flat[0:10, :]
    g_gain[...] = flat[10:11, :]
    g_bias[...] = flat[11:12, :]


def in_vmem(value):
    return pltpu.with_memory_space_constraint(value, pltpu.VMEM)


def window(sc, u, cot, wst, gain, bias, w2, wt):
    whole = pl.BlockSpec(memory_space=pltpu.VMEM)
    shapes = [((1024, 384), F32), ((1056, 384), BF16), ((16, 384), F32)]
    return pl.pallas_call(
        window_kernel,
        grid_spec=pltpu.PrefetchScalarGridSpec(
            num_scalar_prefetch=1,
            grid=(ROWS // BLK,),
            in_specs=[
                whole,
                pl.BlockSpec((BLK, CH), lambda i, sc: (i, 0)),
                whole, whole, whole, whole, whole,
            ],
            out_specs=[pl.BlockSpec(memory_space=pltpu.VMEM)] * len(shapes),
            scratch_shapes=[
                pltpu.VMEM((ROWS + GRAN, 128), F32),
                pltpu.VMEM((ROWS, 128), F32),
                pltpu.VMEM((ROWS + 16, 256), BF16),
                pltpu.VMEM((2, ROWS, 128), BF16),
                pltpu.VMEM((256, 2 * CH), BF16),
                pltpu.VMEM((CH, 3 * CH), F32),
                pltpu.VMEM((128, CH), F32),
                pltpu.VMEM((128, 128), F32),
                pltpu.VMEM((8, CH), F32),
                pltpu.VMEM((128, CH), F32),
                pltpu.VMEM((8, CH), F32),
            ],
        ),
        out_shape=[pltpu.VMEM(s, d) for s, d in shapes],
        compiler_params=pltpu.CompilerParams(vmem_limit_bytes=40 * 2**20),
        cost_estimate=pl.CostEstimate(flops=14 * 10**9, bytes_accessed=10 * 10**6, transcendentals=0),
        name="window",
    )(
        sc, in_vmem(u), pltpu.with_memory_space_constraint(cot, pltpu.HBM),
        in_vmem(wst), in_vmem(gain), in_vmem(bias), in_vmem(w2), in_vmem(wt),
    )


def small_call(kernel, name, sc, args, shapes, scratch=(), place=pltpu.VMEM):
    args = [in_vmem(a) for a in args]
    return pl.pallas_call(
        kernel,
        in_specs=[pl.BlockSpec(memory_space=pltpu.SMEM)] + [pl.BlockSpec(memory_space=pltpu.VMEM)] * len(args),
        out_specs=[pl.BlockSpec(memory_space=pltpu.VMEM)] * len(shapes),
        out_shape=[place(s, d) for s, d in shapes],
        scratch_shapes=list(scratch),
        compiler_params=pltpu.CompilerParams(vmem_limit_bytes=8 * 2**20),
        name=name,
    )(sc, *args)


def swap(value, axis, bit):
    count = 8 if axis == "bulk" else 32
    return lax.ppermute(value, axis, [(i, i ^ bit) for i in range(count)])


def route(rows, sizes, masks):
    high_z, high_y = masks & 4, masks & 16
    steps = (
        (1, (masks & 1) ^ (high_z // 4)),
        (2, (masks & 2) ^ (high_z // 2)),
        (7, high_z),
        (8, (masks & 8) ^ (high_y // 2)),
        (24, high_y),
    )
    units = sizes // TAPS
    extra = jnp.stack([(units // 32).astype(BF16), (units % 32).astype(BF16)], axis=1)
    value = jnp.concatenate([rows, jnp.pad(extra, ((0, 0), (0, 126)))], axis=1)
    for bit, used in steps:
        moved = swap(value, "wide", bit)
        value = jnp.where((used != 0)[:, None], moved, value)
    tail = value[:, -128:-126].astype(F32)
    return value[:, :-128], (tail[:, 0] * 32.0 + tail[:, 1]).astype(jnp.int32)


def window_inputs(conv_first):
    w = conv_first.astype(F32)
    even = jnp.pad(w, ((0, 6), (0, 0)))
    odd = jnp.pad(w, ((5, 1), (0, 0)))
    return jnp.concatenate([even, odd], axis=0)


def local(rows, units, sources, places, cot, conv_first, norm_gain, norm_bias, conv_second):
    u = rows.reshape(SLOTS * GRAN, TAPS)
    sc = jnp.concatenate([units, sources, places])
    wst = window_inputs(conv_first)
    gain, bias = norm_gain[None, :], norm_bias[None, :]
    return sc, window(sc, u, cot, wst, gain, bias, conv_second, conv_second.T)


def per_device(waveforms, owner_of, lengths, cotangent, conv_first, norm_gain, norm_bias, conv_second):
    me = lax.axis_index("wide")
    place = lax.axis_index("bulk")
    masks = jnp.bitwise_xor(owner_of[0], me)
    rows, units = route(waveforms[0], lengths[0], masks)
    x_low, x_high, y_low, y_high = (place // 2) % 2, place // 4, (me // 8) % 2, me // 16
    z_low, z_mid, z_high = me % 2, (me // 2) % 2, (me // 4) % 2
    places = jnp.stack(
        [place % 2, x_low ^ x_high, y_low ^ y_high, x_high, y_high, z_low ^ z_high, z_mid ^ z_high, z_high]
    ).astype(jnp.int32)
    sc, (keep, send, small) = local(
        rows, units, jnp.bitwise_xor(masks, me), places, cotangent[0, 0],
        conv_first, norm_gain, norm_bias, conv_second,
    )
    n = 1024
    recv = swap(send, "bulk", 1)
    for flag, axis, bit, coarse in ((9, "bulk", 2, True), (10, "wide", 8, True), (11, "bulk", 6, True), (12, "wide", 24, False)):
        half = n // 2
        out = [
            ((half, 384), F32), ((16, 384), F32),
            ((half + 32, 384), BF16) if coarse else ((half + 16, 384), F32),
        ]
        kernel = functools.partial(combine_kernel, n, flag, coarse)
        keep, small, send = small_call(kernel, "combine%d" % n, sc, (keep, small, recv), out)
        recv = swap(send, axis, bit)
        n = half
    out = [((96, 128), F32), ((48, 128), F32), ((144, 128), F32)]
    keep, small, send = small_call(turn_kernel, "turn", sc, (keep, small, recv), out)
    recv = swap(send, "wide", 1)
    out = [((48, 128), F32), ((48, 128), F32), ((96, 128), F32)]
    keep, small, send = small_call(middle_kernel, "middle", sc, (keep, small, recv), out)
    recv = swap(send, "wide", 2)
    keep, small, send = small_call(last_kernel, "last", sc, (keep, small, recv), out)
    recv = swap(send, "wide", 7)
    out = [((48, 64), F32), ((10, CH), F32), ((1, CH), F32), ((1, CH), F32)]
    second, first, g_gain, g_bias = small_call(
        final_kernel, "final", sc, (keep, small, recv), out, [pltpu.VMEM((16, CH), F32)], jax.ShapeDtypeStruct
    )
    return (second, first, g_gain[0], g_bias[0])


def solution(mesh):
    placed = (
        P("bulk", "wide", None),
        P("bulk", "wide"),
        P("bulk", "wide"),
        P("bulk", "wide", None, None),
        P(),
        P(),
        P(),
        P(),
    )
    return jax.shard_map(
        per_device,
        mesh=mesh,
        in_specs=placed,
        out_specs=(P("wide", "bulk"), P(), P(), P()),
        check_vma=False,
    )
```

```python
import functools

import jax
import jax.numpy as jnp
from jax import lax
from jax.experimental import pallas as pl
from jax.experimental.pallas import tpu as pltpu
from jax.sharding import PartitionSpec as P

F32 = jnp.float32
BF16 = jnp.bfloat16
HIGHEST = lax.Precision.HIGHEST
SLOTS = 4
TAPS = 10
GRAN = 1024
ROWS = 2048
CH = 512
BLK = 256
BLOCKS = [
    (2 * xh + (xl ^ xh), 2 * yh + (yl ^ yh)) for xl in range(2) for yl in range(2) for xh in range(2) for yh in range(2)
]


def dot(a, b, precision=None):
    return jnp.dot(a, b, preferred_element_type=F32, precision=precision)


def dot_t(a, b, precision=None):
    return lax.dot_general(
        a, b, (((0,), (0,)), ((), ())), preferred_element_type=F32, precision=precision
    )


def cdf_slope(v):
    e = jnp.exp2(v * v * (-0.5 * 1.4426950408889634))
    d = 1.0 + jnp.abs(v) * (0.3275911 * 0.7071067811865476)
    r = pl.reciprocal(d, approx=True)
    t = r * (2.0 - d * r)
    poly = 0.5 * 1.061405429
    for c in (-1.453152027, 1.421413741, -0.284496736, 0.254829592):
        poly = poly * t + 0.5 * c
    tail = poly * t * e
    cdf = jnp.where(v < 0.0, tail, 1.0 - tail)
    return cdf, cdf + v * (e * 0.3989422804014327)


def plan(sc):
    size = [sc[s] for s in range(SLOTS)]
    src = [sc[SLOTS + s] for s in range(SLOTS)]
    rank, off = [], []
    for s in range(SLOTS):
        before = [(src[q] < src[s]).astype(jnp.int32) for q in range(SLOTS) if q != s]
        sizes = [size[q] for q in range(SLOTS) if q != s]
        rank.append(sum(before))
        off.append(sum(b * n for b, n in zip(before, sizes)))
    out = []
    for r in range(SLOTS):
        hit = [(rank[s] == r).astype(jnp.int32) for s in range(SLOTS)]
        out.append(
            (
                sum(h * s for s, h in enumerate(hit)),
                sum(h * o for o, h in zip(off, hit)),
                sum(h * n for n, h in zip(size, hit)),
            )
        )
    return out


def by_lane(values, index):
    out = values[0]
    for s in range(1, len(values)):
        out = jnp.where(index == s, values[s], out)
    return out


def window_kernel(
    sc, u, cot, wst, gain, bias, w2, wt,
    keep, send, small,
    buf, xd, xbig, xs, wbig, acc, nst, tc, im, grads, carry,
):
    step = pl.program_id(0)
    segs = plan(sc)

    @pl.when(step == 0)
    def _():
        buf[...] = jnp.zeros_like(buf)
        for slot, off, _n in segs:
            piece = u[pl.ds(pl.multiple_of(slot * GRAN, GRAN), GRAN), :].astype(F32)
            buf[pl.ds(off, GRAN), 0:TAPS] = piece
        src = lax.broadcasted_iota(jnp.int32, (128, 256), 0)
        tap = lax.broadcasted_iota(jnp.int32, (128, 256), 1) % 16
        r0 = ((tap == src) & (src < TAPS)).astype(F32).astype(BF16)
        r1 = ((tap == src + TAPS) & (src < 5)).astype(F32).astype(BF16)
        one = (lax.broadcasted_iota(jnp.int32, (1, 256), 1) % 16 == 15).astype(F32)
        lane = lax.broadcasted_iota(jnp.int32, (1, 256), 1)
        starts = [o for _s, o, _n in segs]
        ends = [o + n for _s, o, n in segs]
        lo_big, hi_big = by_lane(starts, lane // 64), by_lane(ends, lane // 64)
        lane1 = lane[:, :128]
        odd = (lane1 // 16) % 2
        lo_d = by_lane(starts, lane1 // 32)
        hi_all = by_lane(ends, lane1 // 32)
        hi_d = hi_all - odd
        count = (hi_d - lo_d).astype(F32)

        sums = jnp.zeros((1, 128), F32)
        for rb in range(ROWS // BLK):
            base = rb * BLK
            b0 = buf[pl.ds(base, BLK), :].astype(BF16)
            b1 = buf[pl.ds(base + 1, BLK), :].astype(BF16)
            xr = dot(b0, r0) + dot(b1, r1) + one
            row = lax.broadcasted_iota(jnp.int32, (BLK, 1), 0) + base
            xbig[pl.ds(base, BLK), :] = jnp.where((row >= lo_big) & (row < hi_big), xr, 0.0).astype(BF16)
            x1 = xr[:, :128]
            raw = jnp.where((row >= lo_d) & (row < hi_d), x1, 0.0)
            sums = sums + jnp.sum(raw, axis=0, keepdims=True)
            xd[pl.ds(base, BLK), :] = x1
            full = jnp.where((row >= lo_d) & (row < hi_all), x1, 0.0)
            xs[0, pl.ds(base, BLK), :] = jnp.where(odd == 0, full, 0.0).astype(BF16)
            xs[1, pl.ds(base, BLK), :] = jnp.where(odd == 1, full, 0.0).astype(BF16)
        xbig[pl.ds(ROWS, 16), :] = jnp.zeros((16, 256), BF16)
        mu = sums / count
        moment = jnp.zeros((128, 128), F32)
        for rb in range(ROWS // BLK):
            base = rb * BLK
            row = lax.broadcasted_iota(jnp.int32, (BLK, 1), 0) + base
            d = jnp.where((row >= lo_d) & (row < hi_d), xd[pl.ds(base, BLK), :] - mu, 0.0)
            moment = moment + dot_t(d, d, HIGHEST)
        ri = lax.broadcasted_iota(jnp.int32, (128, 128), 0)
        ci = lax.broadcasted_iota(jnp.int32, (128, 128), 1)
        moment = jnp.where(ri // 16 == ci // 16, moment, 0.0)
        wrow = jnp.concatenate([wst[...]] * SLOTS, axis=0)
        v = dot(moment, wrow, HIGHEST)
        block8 = (
            lax.broadcasted_iota(jnp.int32, (8, 128), 0)
            == lax.broadcasted_iota(jnp.int32, (8, 128), 1) // 16
        ).astype(F32)
        u8 = dot(block8 * mu, wrow, HIGHEST)
        q8 = dot(block8, v * wrow, HIGHEST)
        tcol = jnp.sum(jnp.where(ri == ci, sums, 0.0), axis=1, keepdims=True)
        tc[...] = jnp.broadcast_to(tcol, (128, 128))
        e15 = (lax.broadcasted_iota(jnp.int32, (16, 1), 0) == 15).astype(F32)
        for s, (_slot, _off, n) in enumerate(segs):
            n_even = n.astype(F32)
            n_odd = n_even - 1.0
            n_all = n_even + n_odd
            ue, uo = u8[2 * s : 2 * s + 1], u8[2 * s + 1 : 2 * s + 2]
            mean = (n_even * ue + n_odd * uo) / n_all
            de, do = ue - mean, uo - mean
            spread = (
                q8[2 * s : 2 * s + 1] + q8[2 * s + 1 : 2 * s + 2]
                + n_even * de * de + n_odd * do * do
            ) / n_all
            inv = lax.rsqrt(spread + 1e-05)
            a = gain[...] * inv
            b = bias[...] - a * mean
            im[s : s + 1, :] = inv
            im[4 + s : 5 + s, :] = mean
            for g, dev in enumerate((de, do)):
                at = 32 * s + 16 * g
                nst[at : at + 16, :] = v[at : at + 16] + tcol[at : at + 16] * dev
                f = wrow[at : at + 16] * a + e15 * b
                p0 = f.astype(BF16)
                f = f - p0.astype(F32)
                p1 = f.astype(BF16)
                f = f - p1.astype(F32)
                cols = pl.ds(g * CH, CH)
                wbig[64 * s : 64 * s + 16, cols] = p0
                wbig[64 * s + 16 : 64 * s + 32, cols] = p1
                wbig[64 * s + 32 : 64 * s + 48, cols] = f.astype(BF16)
                wbig[64 * s + 48 : 64 * s + 64, cols] = jnp.zeros((16, CH), BF16)
        acc[...] = jnp.zeros_like(acc)
        grads[...] = jnp.zeros_like(grads)
        carry[...] = jnp.zeros_like(carry)

    base = pl.multiple_of(step * BLK, BLK)
    pre_e = dot(xbig[pl.ds(base, BLK + 16), :], wbig[:, :CH])
    pre_o = dot(xbig[pl.ds(base, BLK), :], wbig[:, CH:])
    c_e, s_e = cdf_slope(pre_e)
    act_e = pre_e * c_e
    c_o, s_o = cdf_slope(pre_o)
    taps = jnp.concatenate(
        [act_e[:BLK].astype(BF16), (pre_o * c_o).astype(BF16), act_e[1 : BLK + 1].astype(BF16)], axis=1
    )
    late = dot(taps, w2[...])
    _c, slope = cdf_slope(late)
    row = lax.broadcasted_iota(jnp.int32, (BLK, 1), 0) + base
    drop = row == segs[0][1] + segs[0][2] - 1
    for _s, off, n in segs[1:]:
        drop = drop | (row == off + n - 1)
    grad = jnp.where(drop, 0.0, cot[...].astype(F32) * slope).astype(BF16)
    acc[...] += dot_t(grad, taps)

    third = dot(grad, wt[:, 2 * CH :])
    row = lax.broadcasted_iota(jnp.int32, (BLK, 1), 0)
    shifted = jnp.where(row == 0, carry[0:1, :], pltpu.roll(third, 1, 0))
    carry[0:1, :] = third[BLK - 1 : BLK]
    ag_e = (dot(grad, wt[:, :CH]) + shifted) * s_e[:BLK]
    ag_o = dot(grad, wt[:, CH : 2 * CH]) * s_o
    total = grads[...]
    for g, ag in enumerate((ag_e, ag_o)):
        part = xs[g, pl.ds(base, BLK), :]
        high = ag.astype(BF16)
        low = (ag - high.astype(F32)).astype(BF16)
        total = total + dot_t(part, high) + dot_t(part, low)
    grads[...] = total

    @pl.when(step == pl.num_programs(0) - 1)
    def _():
        z = jnp.zeros((32, CH), F32)
        g_bias = jnp.zeros((1, CH), F32)
        g_gain = jnp.zeros((1, CH), F32)
        g = gain[...]
        for s, (_slot, _off, n) in enumerate(segs):
            at = 32 * s
            a = grads[at : at + 32, :]
            inv, mean = im[s : s + 1, :], im[4 + s : 5 + s, :]
            count = 2.0 * n.astype(F32) - 1.0
            s1 = a[15:16] + a[31:32]
            s2 = inv * (jnp.sum(a * wst[...], axis=0, keepdims=True) - mean * s1)
            first = g * s1 / count
            cross = g * s2 / count
            z = z + inv * (
                g * a - first * tc[at : at + 32, 0:1] - (cross * inv) * nst[at : at + 32, :]
            )
            g_bias = g_bias + s1
            g_gain = g_gain + s2
        grads[0:10, :] = z[0:10] + z[21:31]
        grads[10:11, :] = g_gain
        grads[11:12, :] = g_bias
        small[0:12, :] = grads[0:12, 0:384]
        for j in range(3):
            small[12:16, 128 * j : 128 * (j + 1)] = grads[4 * j : 4 * j + 4, 384:512]
        core = sc[8]
        for k, (x, y) in enumerate(BLOCKS):
            lanes = pl.ds(384 * y, 384)
            rows = pl.ds(64 * k, 64)
            keep[rows, :] = acc[pl.ds(pl.multiple_of(x * 128 + core * 64, 64), 64), lanes]
            send[rows, :] = acc[
                pl.ds(pl.multiple_of(x * 128 + (1 - core) * 64, 64), 64), lanes
            ].astype(BF16)
        pack_small(small, small[...], send, 1024)


def pack_small(small, value, send, at):
    high = value.astype(BF16)
    low = (value - high.astype(F32)).astype(BF16)
    send[at : at + 16, :] = high
    send[at + 16 : at + 32, :] = low
    small[...] = high.astype(F32) + low.astype(F32)


def received_small(recv, at):
    if recv.dtype == F32:
        return recv[at:, :]
    return recv[at : at + 16, :].astype(F32) + recv[at + 16 : at + 32, :].astype(F32)


def quarters(sc, at):
    a, b = sc[at], sc[at + 1]
    return 2 * a + b, (2 * a + 1 - b, 2 * (1 - a) + b, 2 * (1 - a) + 1 - b)


def add_small(small, recvs, at):
    r = [received_small(recv, at) for recv in recvs]
    return small[...] + r[0] if len(r) == 1 else (small[...] + r[0]) + (r[1] + r[2])


def combine_kernel(n, recvs, flag, sc, keep, small, *refs):
    recv, (keep_out, small_out, *sends) = refs[:recvs], refs[recvs:]
    quarter = n // 4
    mine, others = quarters(sc, flag)

    def rows(index):
        at = pl.ds(pl.multiple_of(index * quarter, quarter), quarter)
        total = keep[at, :]
        for r in recv:
            total = total + r[at, :].astype(F32)
        return total

    keep_out[...] = rows(mine)
    small_out[...] = add_small(small, recv, n)
    for index, send in zip(others, sends):
        send[0:quarter, :] = rows(index).astype(BF16)
    value = small_out[...]
    for send in sends:
        pack_small(small_out, value, send, quarter)


def turn_kernel(sc, keep, small, r0, r1, r2, keep_out, small_out, s0, s1, s2, turned):
    total = keep[...]
    for r in (r0, r1, r2):
        total = total + r[0:64, :].astype(F32)
    total = total.T
    for mid in range(2):
        for low in range(2):
            at = [192 * high + 96 * (mid ^ high) + 48 * (low ^ high) for high in range(2)]
            turned[96 * low + 48 * mid : 96 * low + 48 * mid + 48, :] = jnp.concatenate(
                [total[at[0] : at[0] + 48], total[at[1] : at[1] + 48]], axis=1
            )
    mine, others = quarters(sc, 13)
    keep_out[...] = turned[pl.ds(pl.multiple_of(mine * 48, 8), 48), :]
    sums = add_small(small, (r0, r1, r2), 64)
    for j in range(3):
        small_out[16 * j : 16 * j + 16, :] = sums[:, 128 * j : 128 * (j + 1)]
    for index, send in zip(others, (s0, s1, s2)):
        send[0:48, :] = turned[pl.ds(pl.multiple_of(index * 48, 8), 48), :]
        send[48:96, :] = small_out[...]


def last_kernel(sc, keep, small, r0, r1, r2, keep_out, small_out, send):
    del sc
    kept = keep[...] + r0[0:48, :] + r1[0:48, :] + r2[0:48, :]
    sums = add_small(small, (r0, r1, r2), 48)
    keep_out[...] = kept
    small_out[...] = sums
    send[0:48, :] = kept
    send[48:96, :] = sums


def final_kernel(sc, keep, small, recv, second, first, g_gain, g_bias, flat):
    total = keep[...] + recv[0:48, :]
    second[...] = jnp.where(sc[15] == 1, total[:, 64:128], total[:, 0:64])
    sums = small[...] + recv[48:96, :]
    for j in range(3):
        part = sums[16 * j : 16 * j + 16]
        flat[0:12, 128 * j : 128 * (j + 1)] = part[0:12]
        flat[4 * j : 4 * j + 4, 384:512] = part[12:16]
    first[...] = flat[0:10, :]
    g_gain[...] = flat[10:11, :]
    g_bias[...] = flat[11:12, :]


def in_vmem(value):
    return pltpu.with_memory_space_constraint(value, pltpu.VMEM)


def window(sc, u, cot, wst, gain, bias, w2, wt):
    whole = pl.BlockSpec(memory_space=pltpu.VMEM)
    shapes = [((1024, 384), F32), ((1056, 384), BF16), ((16, 384), F32)]
    return pl.pallas_call(
        window_kernel,
        grid_spec=pltpu.PrefetchScalarGridSpec(
            num_scalar_prefetch=1,
            grid=(ROWS // BLK,),
            in_specs=[
                whole,
                pl.BlockSpec((BLK, CH), lambda i, sc: (i, 0)),
                whole, whole, whole, whole, whole,
            ],
            out_specs=[pl.BlockSpec(memory_space=pltpu.VMEM)] * len(shapes),
            scratch_shapes=[
                pltpu.VMEM((ROWS + GRAN, 128), F32),
                pltpu.VMEM((ROWS, 128), F32),
                pltpu.VMEM((ROWS + 16, 256), BF16),
                pltpu.VMEM((2, ROWS, 128), BF16),
                pltpu.VMEM((256, 2 * CH), BF16),
                pltpu.VMEM((CH, 3 * CH), F32),
                pltpu.VMEM((128, CH), F32),
                pltpu.VMEM((128, 128), F32),
                pltpu.VMEM((8, CH), F32),
                pltpu.VMEM((128, CH), F32),
                pltpu.VMEM((8, CH), F32),
            ],
        ),
        out_shape=[pltpu.VMEM(s, d) for s, d in shapes],
        compiler_params=pltpu.CompilerParams(vmem_limit_bytes=40 * 2**20),
        cost_estimate=pl.CostEstimate(flops=14 * 10**9, bytes_accessed=10 * 10**6, transcendentals=0),
        name="window",
    )(
        sc, in_vmem(u), pltpu.with_memory_space_constraint(cot, pltpu.HBM),
        in_vmem(wst), in_vmem(gain), in_vmem(bias), in_vmem(w2), in_vmem(wt),
    )


def small_call(kernel, name, sc, args, shapes, scratch=(), place=pltpu.VMEM):
    args = [in_vmem(a) for a in args]
    return pl.pallas_call(
        kernel,
        in_specs=[pl.BlockSpec(memory_space=pltpu.SMEM)] + [pl.BlockSpec(memory_space=pltpu.VMEM)] * len(args),
        out_specs=[pl.BlockSpec(memory_space=pltpu.VMEM)] * len(shapes),
        out_shape=[place(s, d) for s, d in shapes],
        scratch_shapes=list(scratch),
        compiler_params=pltpu.CompilerParams(vmem_limit_bytes=8 * 2**20),
        name=name,
    )(sc, *args)


def swap(value, wide, bulk=0):
    return lax.ppermute(value, ("wide", "bulk"), [(i, i ^ (8 * wide + bulk)) for i in range(256)])


def route(rows, sizes, masks):
    z_high, y_high = (masks & 4) // 4, (masks & 16) // 16
    z_low, z_mid, y_low = (masks & 1) ^ z_high, (masks & 2) // 2 ^ z_high, (masks & 8) // 8 ^ y_high
    units = sizes // TAPS
    extra = jnp.stack([(units // 32).astype(BF16), (units % 32).astype(BF16)], axis=1)
    value = jnp.concatenate([rows, jnp.pad(extra, ((0, 0), (0, 126)))], axis=1)
    for a, use_a, b, use_b in ((1, z_low, 8, y_low), (2, z_mid, 24, y_high)):
        got_a, got_b, got_both = swap(value, a), swap(value, b), swap(value, a ^ b)
        far, use_a = (use_b != 0)[:, None], (use_a != 0)[:, None]
        value = jnp.where(use_a, jnp.where(far, got_both, got_a), jnp.where(far, got_b, value))
    value = jnp.where((z_high != 0)[:, None], swap(value, 7), value)
    tail = value[:, -128:-126].astype(F32)
    return value[:, :-128], (tail[:, 0] * 32.0 + tail[:, 1]).astype(jnp.int32)


def window_inputs(conv_first):
    w = conv_first.astype(F32)
    even = jnp.pad(w, ((0, 6), (0, 0)))
    odd = jnp.pad(w, ((5, 1), (0, 0)))
    return jnp.concatenate([even, odd], axis=0)


def local(rows, units, sources, places, cot, conv_first, norm_gain, norm_bias, conv_second):
    u = rows.reshape(SLOTS * GRAN, TAPS)
    sc = jnp.concatenate([units, sources, places])
    wst = window_inputs(conv_first)
    gain, bias = norm_gain[None, :], norm_bias[None, :]
    return sc, window(sc, u, cot, wst, gain, bias, conv_second, conv_second.T)


def per_device(waveforms, owner_of, lengths, cotangent, conv_first, norm_gain, norm_bias, conv_second):
    me = lax.axis_index("wide")
    place = lax.axis_index("bulk")
    masks = jnp.bitwise_xor(owner_of[0], me)
    rows, units = route(waveforms[0], lengths[0], masks)
    x_low, x_high, y_low, y_high = (place // 2) % 2, place // 4, (me // 8) % 2, me // 16
    z_low, z_mid, z_high = me % 2, (me // 2) % 2, (me // 4) % 2
    places = jnp.stack(
        [place % 2, x_low ^ x_high, y_low ^ y_high, x_high, y_high, z_low ^ z_high, z_mid ^ z_high, z_high]
    ).astype(jnp.int32)
    sc, (keep, send, small) = local(
        rows, units, jnp.bitwise_xor(masks, me), places, cotangent[0, 0],
        conv_first, norm_gain, norm_bias, conv_second,
    )
    recv = [swap(send, 0, 1)]
    for n, flag, y, x in ((1024, 9, 8, 2), (256, 11, 24, 6)):
        out = [((n // 4, 384), F32), ((16, 384), F32)] + [((n // 4 + 32, 384), BF16)] * 3
        kernel = functools.partial(combine_kernel, n, len(recv), flag)
        keep, small, *sends = small_call(kernel, "combine%d" % n, sc, (keep, small, *recv), out)
        recv = [swap(sends[0], y), swap(sends[1], 0, x), swap(sends[2], y, x)]
    out = [((48, 128), F32), ((48, 128), F32)] + [((96, 128), F32)] * 3
    keep, small, *sends = small_call(
        turn_kernel, "turn", sc, (keep, small, *recv), out, [pltpu.VMEM((192, 128), F32)]
    )
    recv = [swap(sends[0], 2), swap(sends[1], 1), swap(sends[2], 3)]
    keep, small, send = small_call(last_kernel, "last", sc, (keep, small, *recv), out[:3])
    recv = swap(send, 7)
    out = [((48, 64), F32), ((10, CH), F32), ((1, CH), F32), ((1, CH), F32)]
    second, first, g_gain, g_bias = small_call(
        final_kernel, "final", sc, (keep, small, recv), out, [pltpu.VMEM((16, CH), F32)], jax.ShapeDtypeStruct
    )
    return (second, first, g_gain[0], g_bias[0])


def solution(mesh):
    placed = (
        P("bulk", "wide", None),
        P("bulk", "wide"),
        P("bulk", "wide"),
        P("bulk", "wide", None, None),
        P(),
        P(),
        P(),
        P(),
    )
    return jax.shard_map(
        per_device,
        mesh=mesh,
        in_specs=placed,
        out_specs=(P("wide", "bulk"), P(), P(), P()),
        check_vma=False,
    )
```

```python
import functools

import jax
import jax.numpy as jnp
from jax import lax
from jax.experimental import pallas as pl
from jax.experimental.pallas import tpu as pltpu
from jax.sharding import PartitionSpec as P

F32 = jnp.float32
BF16 = jnp.bfloat16
HIGHEST = lax.Precision.HIGHEST
SLOTS = 4
TAPS = 10
GRAN = 1024
ROWS = 2048
CH = 512
BLK = 512
BLOCKS = [
    (2 * xh + (xl ^ xh), 2 * yh + (yl ^ yh)) for xl in range(2) for yl in range(2) for xh in range(2) for yh in range(2)
]


def dot(a, b, precision=None):
    return jnp.dot(a, b, preferred_element_type=F32, precision=precision)


def dot_t(a, b, precision=None):
    return lax.dot_general(
        a, b, (((0,), (0,)), ((), ())), preferred_element_type=F32, precision=precision
    )


def cdf_slope(v):
    cdf = 0.5 + 0.5 * lax.erf(v * 0.7071067811865476)
    return cdf, cdf + v * (jnp.exp2(v * v * (-0.5 * 1.4426950408889634)) * 0.3989422804014327)


def plan(sc):
    size = [sc[s] for s in range(SLOTS)]
    src = [sc[SLOTS + s] for s in range(SLOTS)]
    rank, off = [], []
    for s in range(SLOTS):
        before = [(src[q] < src[s]).astype(jnp.int32) for q in range(SLOTS) if q != s]
        sizes = [size[q] for q in range(SLOTS) if q != s]
        rank.append(sum(before))
        off.append(sum(b * n for b, n in zip(before, sizes)))
    out = []
    for r in range(SLOTS):
        hit = [(rank[s] == r).astype(jnp.int32) for s in range(SLOTS)]
        out.append(
            (
                sum(h * s for s, h in enumerate(hit)),
                sum(h * o for o, h in zip(off, hit)),
                sum(h * n for n, h in zip(size, hit)),
            )
        )
    return out


def by_lane(values, index):
    out = values[0]
    for s in range(1, len(values)):
        out = jnp.where(index == s, values[s], out)
    return out


def window_kernel(
    sc, u, perm, cot, wst, gain, bias, w2, wt,
    keep, send, small,
    wide, lanes16, buf, xd, xbig, xs, wbig, acc, nst, tc, im, grads, carry,
):
    step = pl.program_id(0)
    segs = plan(sc)

    @pl.when(step == 0)
    def _():
        samples = u[:, : GRAN * TAPS].astype(F32)
        for s in range(SLOTS):
            for r in range(16):
                wide[16 * s + r : 16 * s + r + 1, :] = samples[s : s + 1, 640 * r : 640 * (r + 1)]
        lanes16[...] = dot(wide[...].astype(BF16), perm[...])
        buf[pl.ds(ROWS, 8), :] = jnp.zeros((8, 128), F32)
        own = (
            lax.broadcasted_iota(jnp.int32, (8, 1024), 1) % 128 // 16
            == lax.broadcasted_iota(jnp.int32, (8, 1024), 0)
        )
        for slot, off, _n in segs:
            for r in range(16):
                line = jnp.where(own, lanes16[pl.ds(16 * slot + r, 1), :], 0.0)
                for j in range(8):
                    buf[pl.ds(off + 64 * r + 8 * j, 8), :] = line[:, 128 * j : 128 * j + 128]
        src = lax.broadcasted_iota(jnp.int32, (128, 256), 0) % 16
        tap = lax.broadcasted_iota(jnp.int32, (128, 256), 1) % 16
        r0 = ((tap == src) & (src < TAPS)).astype(F32).astype(BF16)
        r1 = ((tap == src + TAPS) & (src < 5)).astype(F32).astype(BF16)
        one = (lax.broadcasted_iota(jnp.int32, (1, 256), 1) % 16 == 15).astype(F32)
        lane = lax.broadcasted_iota(jnp.int32, (1, 256), 1)
        starts = [o for _s, o, _n in segs]
        ends = [o + n for _s, o, n in segs]
        lo_big, hi_big = by_lane(starts, lane // 64), by_lane(ends, lane // 64)
        lane1 = lane[:, :128]
        odd = (lane1 // 16) % 2
        lo_d = by_lane(starts, lane1 // 32)
        hi_all = by_lane(ends, lane1 // 32)
        hi_d = hi_all - odd
        count = (hi_d - lo_d).astype(F32)

        sums = jnp.zeros((1, 128), F32)
        for rb in range(ROWS // BLK):
            base = rb * BLK
            b0 = buf[pl.ds(base, BLK), :].astype(BF16)
            b1 = buf[pl.ds(base + 1, BLK), :].astype(BF16)
            xr = dot(b0, r0) + dot(b1, r1) + one
            row = lax.broadcasted_iota(jnp.int32, (BLK, 1), 0) + base
            xbig[pl.ds(base, BLK), :] = jnp.where((row >= lo_big) & (row < hi_big), xr, 0.0).astype(BF16)
            x1 = xr[:, :128]
            raw = jnp.where((row >= lo_d) & (row < hi_d), x1, 0.0)
            sums = sums + jnp.sum(raw, axis=0, keepdims=True)
            xd[pl.ds(base, BLK), :] = x1
            full = jnp.where((row >= lo_d) & (row < hi_all), x1, 0.0)
            xs[0, pl.ds(base, BLK), :] = jnp.where(odd == 0, full, 0.0).astype(BF16)
            xs[1, pl.ds(base, BLK), :] = jnp.where(odd == 1, full, 0.0).astype(BF16)
        xbig[pl.ds(ROWS, 16), :] = jnp.zeros((16, 256), BF16)
        mu = sums / count
        main = jnp.zeros((128, 128), F32)
        rest = jnp.zeros((128, 128), F32)
        for rb in range(ROWS // BLK):
            base = rb * BLK
            row = lax.broadcasted_iota(jnp.int32, (BLK, 1), 0) + base
            d = jnp.where((row >= lo_d) & (row < hi_d), xd[pl.ds(base, BLK), :] - mu, 0.0)
            high = d.astype(BF16)
            low = (d - high.astype(F32)).astype(BF16)
            main = main + dot_t(high, high)
            rest = rest + dot_t(high, low)
        ri = lax.broadcasted_iota(jnp.int32, (128, 128), 0)
        ci = lax.broadcasted_iota(jnp.int32, (128, 128), 1)
        moment = jnp.where(ri // 16 == ci // 16, main + (rest + rest.T), 0.0)
        wrow = jnp.concatenate([wst[...]] * SLOTS, axis=0)
        v = dot(moment, wrow, HIGHEST)
        block8 = (
            lax.broadcasted_iota(jnp.int32, (8, 128), 0)
            == lax.broadcasted_iota(jnp.int32, (8, 128), 1) // 16
        ).astype(F32)
        u8 = dot(block8 * mu, wrow, HIGHEST)
        q8 = dot(block8, v * wrow, HIGHEST)
        tcol = jnp.sum(jnp.where(ri == ci, sums, 0.0), axis=1, keepdims=True)
        tc[...] = jnp.broadcast_to(tcol, (128, 128))
        e15 = (lax.broadcasted_iota(jnp.int32, (16, 1), 0) == 15).astype(F32)
        for s, (_slot, _off, n) in enumerate(segs):
            n_even = n.astype(F32)
            n_odd = n_even - 1.0
            n_all = n_even + n_odd
            ue, uo = u8[2 * s : 2 * s + 1], u8[2 * s + 1 : 2 * s + 2]
            mean = (n_even * ue + n_odd * uo) / n_all
            de, do = ue - mean, uo - mean
            spread = (
                q8[2 * s : 2 * s + 1] + q8[2 * s + 1 : 2 * s + 2]
                + n_even * de * de + n_odd * do * do
            ) / n_all
            inv = lax.rsqrt(spread + 1e-05)
            a = gain[...] * inv
            b = bias[...] - a * mean
            im[s : s + 1, :] = inv
            im[4 + s : 5 + s, :] = mean
            for g, dev in enumerate((de, do)):
                at = 32 * s + 16 * g
                nst[at : at + 16, :] = v[at : at + 16] + tcol[at : at + 16] * dev
                f = wrow[at : at + 16] * a + e15 * b
                p0 = f.astype(BF16)
                f = f - p0.astype(F32)
                p1 = f.astype(BF16)
                f = f - p1.astype(F32)
                cols = pl.ds(g * CH, CH)
                wbig[64 * s : 64 * s + 16, cols] = p0
                wbig[64 * s + 16 : 64 * s + 32, cols] = p1
                wbig[64 * s + 32 : 64 * s + 48, cols] = f.astype(BF16)
                wbig[64 * s + 48 : 64 * s + 64, cols] = jnp.zeros((16, CH), BF16)
        acc[...] = jnp.zeros_like(acc)
        grads[...] = jnp.zeros_like(grads)
        carry[...] = jnp.zeros_like(carry)

    base = pl.multiple_of(step * BLK, BLK)
    pre_e = dot(xbig[pl.ds(base, BLK + 16), :], wbig[:, :CH])
    pre_o = dot(xbig[pl.ds(base, BLK), :], wbig[:, CH:])
    c_e, s_e = cdf_slope(pre_e)
    act_e = pre_e * c_e
    c_o, s_o = cdf_slope(pre_o)
    taps = jnp.concatenate(
        [act_e[:BLK].astype(BF16), (pre_o * c_o).astype(BF16), act_e[1 : BLK + 1].astype(BF16)], axis=1
    )
    late = dot(taps, w2[...])
    _c, slope = cdf_slope(late)
    row = lax.broadcasted_iota(jnp.int32, (BLK, 1), 0) + base
    drop = row == segs[0][1] + segs[0][2] - 1
    for _s, off, n in segs[1:]:
        drop = drop | (row == off + n - 1)
    grad = jnp.where(drop, 0.0, cot[...].astype(F32) * slope).astype(BF16)
    acc[...] += dot_t(grad, taps)

    third = dot(grad, wt[:, 2 * CH :])
    row = lax.broadcasted_iota(jnp.int32, (BLK, 1), 0)
    shifted = jnp.where(row == 0, carry[0:1, :], pltpu.roll(third, 1, 0))
    carry[0:1, :] = third[BLK - 1 : BLK]
    ag_e = (dot(grad, wt[:, :CH]) + shifted) * s_e[:BLK]
    ag_o = dot(grad, wt[:, CH : 2 * CH]) * s_o
    total = grads[...]
    for g, ag in enumerate((ag_e, ag_o)):
        part = xs[g, pl.ds(base, BLK), :]
        high = ag.astype(BF16)
        low = (ag - high.astype(F32)).astype(BF16)
        total = total + dot_t(part, high) + dot_t(part, low)
    grads[...] = total

    @pl.when(step == pl.num_programs(0) - 1)
    def _():
        z = jnp.zeros((32, CH), F32)
        g_bias = jnp.zeros((1, CH), F32)
        g_gain = jnp.zeros((1, CH), F32)
        g = gain[...]
        for s, (_slot, _off, n) in enumerate(segs):
            at = 32 * s
            a = grads[at : at + 32, :]
            inv, mean = im[s : s + 1, :], im[4 + s : 5 + s, :]
            count = 2.0 * n.astype(F32) - 1.0
            s1 = a[15:16] + a[31:32]
            s2 = inv * (jnp.sum(a * wst[...], axis=0, keepdims=True) - mean * s1)
            first = g * s1 / count
            cross = g * s2 / count
            z = z + inv * (
                g * a - first * tc[at : at + 32, 0:1] - (cross * inv) * nst[at : at + 32, :]
            )
            g_bias = g_bias + s1
            g_gain = g_gain + s2
        grads[0:10, :] = z[0:10] + z[21:31]
        grads[10:11, :] = g_gain
        grads[11:12, :] = g_bias
        small[0:12, :] = grads[0:12, 0:384]
        for j in range(3):
            small[12:16, 128 * j : 128 * (j + 1)] = grads[4 * j : 4 * j + 4, 384:512]
        core = sc[8]
        for k, (x, y) in enumerate(BLOCKS):
            lanes = pl.ds(384 * y, 384)
            rows = pl.ds(64 * k, 64)
            keep[rows, :] = acc[pl.ds(pl.multiple_of(x * 128 + core * 64, 64), 64), lanes]
            send[rows, :] = acc[
                pl.ds(pl.multiple_of(x * 128 + (1 - core) * 64, 64), 64), lanes
            ].astype(BF16)
        pack_small(small, small[...], send, 1024)


def pack_small(small, value, send, at):
    high = value.astype(BF16)
    low = (value - high.astype(F32)).astype(BF16)
    send[at : at + 16, :] = high
    send[at + 16 : at + 32, :] = low
    small[...] = high.astype(F32) + low.astype(F32)


def received_small(recv, at):
    if recv.dtype == F32:
        return recv[at:, :]
    return recv[at : at + 16, :].astype(F32) + recv[at + 16 : at + 32, :].astype(F32)


def quarters(sc, at):
    a, b = sc[at], sc[at + 1]
    return 2 * a + b, (2 * a + 1 - b, 2 * (1 - a) + b, 2 * (1 - a) + 1 - b)


def add_small(small, recvs, at):
    r = [received_small(recv, at) for recv in recvs]
    return small[...] + r[0] if len(r) == 1 else (small[...] + r[0]) + (r[1] + r[2])


def combine_kernel(n, recvs, flag, sc, keep, small, *refs):
    recv, (keep_out, small_out, *sends) = refs[:recvs], refs[recvs:]
    quarter = n // 4
    mine, others = quarters(sc, flag)

    def rows(index):
        at = pl.ds(pl.multiple_of(index * quarter, quarter), quarter)
        total = keep[at, :]
        for r in recv:
            total = total + r[at, :].astype(F32)
        return total

    keep_out[...] = rows(mine)
    small_out[...] = add_small(small, recv, n)
    for index, send in zip(others, sends):
        send[0:quarter, :] = rows(index).astype(BF16)
    value = small_out[...]
    for send in sends:
        pack_small(small_out, value, send, quarter)


def turn_kernel(sc, keep, small, r0, r1, r2, keep_out, small_out, s0, s1, s2, turned):
    total = keep[...]
    for r in (r0, r1, r2):
        total = total + r[0:64, :].astype(F32)
    total = total.T
    for mid in range(2):
        for low in range(2):
            at = [192 * high + 96 * (mid ^ high) + 48 * (low ^ high) for high in range(2)]
            turned[96 * low + 48 * mid : 96 * low + 48 * mid + 48, :] = jnp.concatenate(
                [total[at[0] : at[0] + 48], total[at[1] : at[1] + 48]], axis=1
            )
    mine, others = quarters(sc, 13)
    keep_out[...] = turned[pl.ds(pl.multiple_of(mine * 48, 8), 48), :]
    sums = add_small(small, (r0, r1, r2), 64)
    for j in range(3):
        small_out[16 * j : 16 * j + 16, :] = sums[:, 128 * j : 128 * (j + 1)]
    for index, send in zip(others, (s0, s1, s2)):
        send[0:48, :] = turned[pl.ds(pl.multiple_of(index * 48, 8), 48), :]
        send[48:96, :] = small_out[...]


def last_kernel(sc, keep, small, r0, r1, r2, keep_out, small_out, send):
    del sc
    kept = keep[...] + r0[0:48, :] + r1[0:48, :] + r2[0:48, :]
    sums = add_small(small, (r0, r1, r2), 48)
    keep_out[...] = kept
    small_out[...] = sums
    send[0:48, :] = kept
    send[48:96, :] = sums


def final_kernel(sc, keep, small, recv, second, first, g_gain, g_bias, flat):
    total = keep[...] + recv[0:48, :]
    second[...] = jnp.where(sc[15] == 1, total[:, 64:128], total[:, 0:64])
    sums = small[...] + recv[48:96, :]
    for j in range(3):
        part = sums[16 * j : 16 * j + 16]
        flat[0:12, 128 * j : 128 * (j + 1)] = part[0:12]
        flat[4 * j : 4 * j + 4, 384:512] = part[12:16]
    first[...] = flat[0:10, :]
    g_gain[...] = flat[10:11, :]
    g_bias[...] = flat[11:12, :]


def in_vmem(value):
    return pltpu.with_memory_space_constraint(value, pltpu.VMEM)


def window(sc, u, perm, cot, wst, gain, bias, w2, wt):
    whole = pl.BlockSpec(memory_space=pltpu.VMEM)
    shapes = [((1024, 384), F32), ((1056, 384), BF16), ((16, 384), F32)]
    return pl.pallas_call(
        window_kernel,
        grid_spec=pltpu.PrefetchScalarGridSpec(
            num_scalar_prefetch=1,
            grid=(ROWS // BLK,),
            in_specs=[
                whole, whole,
                pl.BlockSpec((BLK, CH), lambda i, sc: (i, 0)),
                whole, whole, whole, whole, whole,
            ],
            out_specs=[pl.BlockSpec(memory_space=pltpu.VMEM)] * len(shapes),
            scratch_shapes=[
                pltpu.VMEM((64, 640), F32),
                pltpu.VMEM((64, 1024), F32),
                pltpu.VMEM((ROWS + GRAN, 128), F32),
                pltpu.VMEM((ROWS, 128), F32),
                pltpu.VMEM((ROWS + 16, 256), BF16),
                pltpu.VMEM((2, ROWS, 128), BF16),
                pltpu.VMEM((256, 2 * CH), BF16),
                pltpu.VMEM((CH, 3 * CH), F32),
                pltpu.VMEM((128, CH), F32),
                pltpu.VMEM((128, 128), F32),
                pltpu.VMEM((8, CH), F32),
                pltpu.VMEM((128, CH), F32),
                pltpu.VMEM((8, CH), F32),
            ],
        ),
        out_shape=[pltpu.VMEM(s, d) for s, d in shapes],
        compiler_params=pltpu.CompilerParams(vmem_limit_bytes=40 * 2**20),
        cost_estimate=pl.CostEstimate(flops=14 * 10**9, bytes_accessed=10 * 10**6, transcendentals=0),
        name="window",
    )(
        sc, in_vmem(u), in_vmem(perm), pltpu.with_memory_space_constraint(cot, pltpu.HBM),
        in_vmem(wst), in_vmem(gain), in_vmem(bias), in_vmem(w2), in_vmem(wt),
    )


def small_call(kernel, name, sc, args, shapes, scratch=(), place=pltpu.VMEM):
    args = [in_vmem(a) for a in args]
    return pl.pallas_call(
        kernel,
        in_specs=[pl.BlockSpec(memory_space=pltpu.SMEM)] + [pl.BlockSpec(memory_space=pltpu.VMEM)] * len(args),
        out_specs=[pl.BlockSpec(memory_space=pltpu.VMEM)] * len(shapes),
        out_shape=[place(s, d) for s, d in shapes],
        scratch_shapes=list(scratch),
        compiler_params=pltpu.CompilerParams(vmem_limit_bytes=8 * 2**20),
        name=name,
    )(sc, *args)


def swap(value, wide, bulk=0):
    return lax.ppermute(value, ("wide", "bulk"), [(i, i ^ (8 * wide + bulk)) for i in range(256)])


def route(rows, sizes, masks):
    z_high, y_high = (masks & 4) // 4, (masks & 16) // 16
    z_low, z_mid, y_low = (masks & 1) ^ z_high, (masks & 2) // 2 ^ z_high, (masks & 8) // 8 ^ y_high
    units = sizes // TAPS
    extra = jnp.stack([(units // 32).astype(BF16), (units % 32).astype(BF16)], axis=1)
    value = jnp.concatenate([rows, jnp.pad(extra, ((0, 0), (0, 126)))], axis=1)
    for a, use_a, b, use_b in ((1, z_low, 8, y_low), (2, z_mid, 24, y_high)):
        got_a, got_b, got_both = swap(value, a), swap(value, b), swap(value, a ^ b)
        far, use_a = (use_b != 0)[:, None], (use_a != 0)[:, None]
        value = jnp.where(use_a, jnp.where(far, got_both, got_a), jnp.where(far, got_b, value))
    value = jnp.where((z_high != 0)[:, None], swap(value, 7), value)
    tail = value[:, -128:-126].astype(F32)
    return value, (tail[:, 0] * 32.0 + tail[:, 1]).astype(jnp.int32)


def window_inputs(conv_first):
    w = conv_first.astype(F32)
    even = jnp.pad(w, ((0, 6), (0, 0)))
    odd = jnp.pad(w, ((5, 1), (0, 0)))
    return jnp.concatenate([even, odd], axis=0)


def local(rows, units, sources, places, cot, conv_first, norm_gain, norm_bias, conv_second):
    lane = jnp.arange(1024, dtype=jnp.int32)[None, :]
    perm = (jnp.arange(640, dtype=jnp.int32)[:, None] == lane // 16 * TAPS + lane % 16) & (lane % 16 < TAPS)
    sc = jnp.concatenate([units, sources, places])
    wst = window_inputs(conv_first)
    gain, bias = norm_gain[None, :], norm_bias[None, :]
    return sc, window(sc, rows, perm.astype(BF16), cot, wst, gain, bias, conv_second, conv_second.T)


def per_device(waveforms, owner_of, lengths, cotangent, conv_first, norm_gain, norm_bias, conv_second):
    me = lax.axis_index("wide")
    place = lax.axis_index("bulk")
    masks = jnp.bitwise_xor(owner_of[0], me)
    rows, units = route(waveforms[0], lengths[0], masks)
    x_low, x_high, y_low, y_high = (place // 2) % 2, place // 4, (me // 8) % 2, me // 16
    z_low, z_mid, z_high = me % 2, (me // 2) % 2, (me // 4) % 2
    places = jnp.stack(
        [place % 2, x_low ^ x_high, y_low ^ y_high, x_high, y_high, z_low ^ z_high, z_mid ^ z_high, z_high]
    ).astype(jnp.int32)
    sc, (keep, send, small) = local(
        rows, units, jnp.bitwise_xor(masks, me), places, cotangent[0, 0],
        conv_first, norm_gain, norm_bias, conv_second,
    )
    recv = [swap(send, 0, 1)]
    for n, flag, y, x in ((1024, 9, 8, 2), (256, 11, 24, 6)):
        out = [((n // 4, 384), F32), ((16, 384), F32)] + [((n // 4 + 32, 384), BF16)] * 3
        kernel = functools.partial(combine_kernel, n, len(recv), flag)
        keep, small, *sends = small_call(kernel, "combine%d" % n, sc, (keep, small, *recv), out)
        recv = [swap(sends[0], y), swap(sends[1], 0, x), swap(sends[2], y, x)]
    out = [((48, 128), F32), ((48, 128), F32)] + [((96, 128), F32)] * 3
    keep, small, *sends = small_call(
        turn_kernel, "turn", sc, (keep, small, *recv), out, [pltpu.VMEM((192, 128), F32)]
    )
    recv = [swap(sends[0], 2), swap(sends[1], 1), swap(sends[2], 3)]
    keep, small, send = small_call(last_kernel, "last", sc, (keep, small, *recv), out[:3])
    recv = swap(send, 7)
    out = [((48, 64), F32), ((10, CH), F32), ((1, CH), F32), ((1, CH), F32)]
    second, first, g_gain, g_bias = small_call(
        final_kernel, "final", sc, (keep, small, recv), out, [pltpu.VMEM((16, CH), F32)], jax.ShapeDtypeStruct
    )
    return (second, first, g_gain[0], g_bias[0])


def solution(mesh):
    placed = (
        P("bulk", "wide", None),
        P("bulk", "wide"),
        P("bulk", "wide"),
        P("bulk", "wide", None, None),
        P(),
        P(),
        P(),
        P(),
    )
    return jax.shard_map(
        per_device,
        mesh=mesh,
        in_specs=placed,
        out_specs=(P("wide", "bulk"), P(), P(), P()),
        check_vma=False,
    )
```

```python
import functools

import jax
import jax.numpy as jnp
from jax import lax
from jax.experimental import pallas as pl
from jax.experimental.pallas import tpu as pltpu
from jax.sharding import PartitionSpec as P

F32 = jnp.float32
BF16 = jnp.bfloat16
HIGHEST = lax.Precision.HIGHEST
SLOTS = 4
TAPS = 10
GRAN = 1024
ROWS = 2048
CH = 512
BLK = 1024
BLOCKS = [
    (2 * xh + (xl ^ xh), 2 * yh + (yl ^ yh)) for xl in range(2) for yl in range(2) for xh in range(2) for yh in range(2)
]


def dot(a, b, precision=None):
    return jnp.dot(a, b, preferred_element_type=F32, precision=precision)


def dot_b(a, b):
    return lax.dot_general(a, b, (((1,), (1,)), ((), ())), preferred_element_type=F32)


def dot_t(a, b, precision=None):
    return lax.dot_general(
        a, b, (((0,), (0,)), ((), ())), preferred_element_type=F32, precision=precision
    )


def cdf_slope(v):
    cdf = 0.5 + 0.5 * lax.erf(v * 0.7071067811865476)
    return cdf, cdf + v * (jnp.exp2(v * v * (-0.5 * 1.4426950408889634)) * 0.3989422804014327)


def plan(sc):
    size = [sc[s] for s in range(SLOTS)]
    src = [sc[SLOTS + s] ^ sc[16] for s in range(SLOTS)]
    rank, off = [], []
    for s in range(SLOTS):
        before = [(src[q] < src[s]).astype(jnp.int32) for q in range(SLOTS) if q != s]
        sizes = [size[q] for q in range(SLOTS) if q != s]
        rank.append(sum(before))
        off.append(sum(b * n for b, n in zip(before, sizes)))
    out = []
    for r in range(SLOTS):
        hit = [(rank[s] == r).astype(jnp.int32) for s in range(SLOTS)]
        out.append(
            (
                sum(h * s for s, h in enumerate(hit)),
                sum(h * o for o, h in zip(off, hit)),
                sum(h * n for n, h in zip(size, hit)),
            )
        )
    return out


def by_lane(values, index):
    out = values[0]
    for s in range(1, len(values)):
        out = jnp.where(index == s, values[s], out)
    return out


def window_kernel(
    sc, own_rows, moved, cot, wst, gain, bias, w2,
    keep, send, small,
    lines, wide, lanes16, buf, xd, xbig, xs, wbig, acc, nst, tc, im, grads, carry,
):
    step = pl.program_id(0)
    segs = plan(sc)

    @pl.when(step == 0)
    def _():
        for s in range(SLOTS):
            at = pl.ds(80 * s, 80)
            lines[at, :] = jnp.where((sc[SLOTS + s] & 4) != 0, moved[at, :], own_rows[at, :]).astype(F32)
            for c in range(5):
                wide[16 * s : 16 * s + 16, 128 * c : 128 * c + 128] = lines[pl.ds(80 * s + c, 16, stride=5), :]
        place = lax.broadcasted_iota(jnp.int32, (1, 1024), 1)
        place = jnp.where(place % 16 < TAPS, place // 16 * TAPS + place % 16, -1)
        perm = (lax.broadcasted_iota(jnp.int32, (640, 1), 0) == place).astype(F32).astype(BF16)
        lanes16[...] = dot(wide[...].astype(BF16), perm)
        buf[pl.ds(ROWS, 8), :] = jnp.zeros((8, 128), F32)
        own = (
            lax.broadcasted_iota(jnp.int32, (8, 1024), 1) % 128 // 16
            == lax.broadcasted_iota(jnp.int32, (8, 1024), 0)
        )
        for slot, off, _n in segs:
            for r in range(16):
                line = jnp.where(own, lanes16[pl.ds(16 * slot + r, 1), :], 0.0)
                for j in range(8):
                    buf[pl.ds(off + 64 * r + 8 * j, 8), :] = line[:, 128 * j : 128 * j + 128]
        src = lax.broadcasted_iota(jnp.int32, (128, 256), 0) % 16
        tap = lax.broadcasted_iota(jnp.int32, (128, 256), 1) % 16
        r0 = ((tap == src) & (src < TAPS)).astype(F32).astype(BF16)
        r1 = ((tap == src + TAPS) & (src < 5)).astype(F32).astype(BF16)
        one = (lax.broadcasted_iota(jnp.int32, (1, 256), 1) % 16 == 15).astype(F32)
        lane = lax.broadcasted_iota(jnp.int32, (1, 256), 1)
        starts = [o for _s, o, _n in segs]
        ends = [o + n for _s, o, n in segs]
        lo_big, hi_big = by_lane(starts, lane // 64), by_lane(ends, lane // 64)
        lane1 = lane[:, :128]
        odd = (lane1 // 16) % 2
        lo_d = by_lane(starts, lane1 // 32)
        hi_all = by_lane(ends, lane1 // 32)
        hi_d = hi_all - odd
        count = (hi_d - lo_d).astype(F32)

        sums = jnp.zeros((1, 128), F32)
        for rb in range(ROWS // BLK):
            base = rb * BLK
            b0 = buf[pl.ds(base, BLK), :].astype(BF16)
            b1 = buf[pl.ds(base + 1, BLK), :].astype(BF16)
            xr = dot(b0, r0) + dot(b1, r1) + one
            row = lax.broadcasted_iota(jnp.int32, (BLK, 1), 0) + base
            xbig[pl.ds(base, BLK), :] = jnp.where((row >= lo_big) & (row < hi_big), xr, 0.0).astype(BF16)
            x1 = xr[:, :128]
            raw = jnp.where((row >= lo_d) & (row < hi_d), x1, 0.0)
            sums = sums + jnp.sum(raw, axis=0, keepdims=True)
            xd[pl.ds(base, BLK), :] = x1
            full = jnp.where((row >= lo_d) & (row < hi_all), x1, 0.0)
            xs[0, :, base : base + BLK] = jnp.where(odd == 0, full, 0.0).T.astype(BF16)
            xs[1, :, base : base + BLK] = jnp.where(odd == 1, full, 0.0).T.astype(BF16)
        xbig[pl.ds(ROWS, 16), :] = jnp.zeros((16, 256), BF16)
        mu = sums / count
        main = jnp.zeros((128, 128), F32)
        rest = jnp.zeros((128, 128), F32)
        for rb in range(ROWS // BLK):
            base = rb * BLK
            row = lax.broadcasted_iota(jnp.int32, (BLK, 1), 0) + base
            d = jnp.where((row >= lo_d) & (row < hi_d), xd[pl.ds(base, BLK), :] - mu, 0.0)
            high = d.astype(BF16)
            low = (d - high.astype(F32)).astype(BF16)
            main = main + dot_t(high, high)
            rest = rest + dot_t(high, low)
        ri = lax.broadcasted_iota(jnp.int32, (128, 128), 0)
        ci = lax.broadcasted_iota(jnp.int32, (128, 128), 1)
        moment = jnp.where(ri // 16 == ci // 16, main + (rest + rest.T), 0.0)
        wrow = jnp.concatenate([wst[...]] * SLOTS, axis=0)
        v = dot(moment, wrow, HIGHEST)
        block8 = (
            lax.broadcasted_iota(jnp.int32, (8, 128), 0)
            == lax.broadcasted_iota(jnp.int32, (8, 128), 1) // 16
        ).astype(F32)
        u8 = dot(block8 * mu, wrow, HIGHEST)
        q8 = dot(block8, v * wrow, HIGHEST)
        tcol = jnp.sum(jnp.where(ri == ci, sums, 0.0), axis=1, keepdims=True)
        tc[...] = jnp.broadcast_to(tcol, (128, 128))
        e15 = (lax.broadcasted_iota(jnp.int32, (16, 1), 0) == 15).astype(F32)
        for s, (_slot, _off, n) in enumerate(segs):
            n_even = n.astype(F32)
            n_odd = n_even - 1.0
            n_all = n_even + n_odd
            ue, uo = u8[2 * s : 2 * s + 1], u8[2 * s + 1 : 2 * s + 2]
            mean = (n_even * ue + n_odd * uo) / n_all
            de, do = ue - mean, uo - mean
            spread = (
                q8[2 * s : 2 * s + 1] + q8[2 * s + 1 : 2 * s + 2]
                + n_even * de * de + n_odd * do * do
            ) / n_all
            inv = lax.rsqrt(spread + 1e-05)
            a = gain[...] * inv
            b = bias[...] - a * mean
            im[s : s + 1, :] = inv
            im[4 + s : 5 + s, :] = mean
            for g, dev in enumerate((de, do)):
                at = 32 * s + 16 * g
                nst[at : at + 16, :] = v[at : at + 16] + tcol[at : at + 16] * dev
                f = wrow[at : at + 16] * a + e15 * b
                p0 = f.astype(BF16)
                f = f - p0.astype(F32)
                p1 = f.astype(BF16)
                f = f - p1.astype(F32)
                cols = pl.ds(g * CH, CH)
                wbig[64 * s : 64 * s + 16, cols] = p0
                wbig[64 * s + 16 : 64 * s + 32, cols] = p1
                wbig[64 * s + 32 : 64 * s + 48, cols] = f.astype(BF16)
                wbig[64 * s + 48 : 64 * s + 64, cols] = jnp.zeros((16, CH), BF16)
        acc[...] = jnp.zeros_like(acc)
        grads[...] = jnp.zeros_like(grads)
        carry[...] = jnp.zeros_like(carry)

    base = pl.multiple_of(step * BLK, BLK)
    pre_e = dot(xbig[pl.ds(base, BLK + 16), :], wbig[:, :CH])
    pre_o = dot(xbig[pl.ds(base, BLK), :], wbig[:, CH:])
    c_e, s_e = cdf_slope(pre_e)
    act_e = pre_e * c_e
    c_o, s_o = cdf_slope(pre_o)
    taps = jnp.concatenate(
        [act_e[:BLK].astype(BF16), (pre_o * c_o).astype(BF16), act_e[1 : BLK + 1].astype(BF16)], axis=1
    )
    late = dot(taps, w2[...])
    _c, slope = cdf_slope(late)
    row = lax.broadcasted_iota(jnp.int32, (BLK, 1), 0) + base
    drop = row == segs[0][1] + segs[0][2] - 1
    for _s, off, n in segs[1:]:
        drop = drop | (row == off + n - 1)
    grad = jnp.where(drop, 0.0, cot[...].astype(F32) * slope).astype(BF16)
    acc[...] += dot_t(grad, taps)

    third = dot_b(grad, w2[2 * CH :, :])
    row = lax.broadcasted_iota(jnp.int32, (BLK, 1), 0)
    shifted = jnp.where(row == 0, carry[0:1, :], pltpu.roll(third, 1, 0))
    carry[0:1, :] = third[BLK - 1 : BLK]
    ag_e = (dot_b(grad, w2[:CH, :]) + shifted) * s_e[:BLK]
    ag_o = dot_b(grad, w2[CH : 2 * CH, :]) * s_o
    total = grads[...]
    for g, ag in enumerate((ag_e, ag_o)):
        part = xs[g, :, pl.ds(base, BLK)]
        high = ag.astype(BF16)
        low = (ag - high.astype(F32)).astype(BF16)
        total = total + dot(part, high) + dot(part, low)
    grads[...] = total

    @pl.when(step == pl.num_programs(0) - 1)
    def _():
        z = jnp.zeros((32, CH), F32)
        g_bias = jnp.zeros((1, CH), F32)
        g_gain = jnp.zeros((1, CH), F32)
        g = gain[...]
        for s, (_slot, _off, n) in enumerate(segs):
            at = 32 * s
            a = grads[at : at + 32, :]
            inv, mean = im[s : s + 1, :], im[4 + s : 5 + s, :]
            count = 2.0 * n.astype(F32) - 1.0
            s1 = a[15:16] + a[31:32]
            s2 = inv * (jnp.sum(a * wst[...], axis=0, keepdims=True) - mean * s1)
            first = g * s1 / count
            cross = g * s2 / count
            z = z + inv * (
                g * a - first * tc[at : at + 32, 0:1] - (cross * inv) * nst[at : at + 32, :]
            )
            g_bias = g_bias + s1
            g_gain = g_gain + s2
        grads[0:10, :] = z[0:10] + z[21:31]
        grads[10:11, :] = g_gain
        grads[11:12, :] = g_bias
        small[0:12, :] = grads[0:12, 0:384]
        for j in range(3):
            small[12:16, 128 * j : 128 * (j + 1)] = grads[4 * j : 4 * j + 4, 384:512]
        core = sc[8]
        for k, (x, y) in enumerate(BLOCKS):
            lanes = pl.ds(384 * y, 384)
            rows = pl.ds(64 * k, 64)
            keep[rows, :] = acc[pl.ds(pl.multiple_of(x * 128 + core * 64, 64), 64), lanes]
            send[rows, :] = acc[
                pl.ds(pl.multiple_of(x * 128 + (1 - core) * 64, 64), 64), lanes
            ].astype(BF16)
        pack_small(small, small[...], send, 1024)


def pack_small(small, value, send, at):
    high = value.astype(BF16)
    low = (value - high.astype(F32)).astype(BF16)
    send[at : at + 16, :] = high
    send[at + 16 : at + 32, :] = low
    small[...] = high.astype(F32) + low.astype(F32)


def received_small(recv, at):
    if recv.dtype == F32:
        return recv[at:, :]
    return recv[at : at + 16, :].astype(F32) + recv[at + 16 : at + 32, :].astype(F32)


def quarters(sc, at):
    a, b = sc[at], sc[at + 1]
    return 2 * a + b, (2 * a + 1 - b, 2 * (1 - a) + b, 2 * (1 - a) + 1 - b)


def add_small(small, recvs, at):
    r = [received_small(recv, at) for recv in recvs]
    return small[...] + r[0] if len(r) == 1 else (small[...] + r[0]) + (r[1] + r[2])


def combine_kernel(n, recvs, flag, sc, keep, small, *refs):
    recv, (keep_out, small_out, *sends) = refs[:recvs], refs[recvs:]
    quarter = n // 4
    mine, others = quarters(sc, flag)

    def rows(index):
        at = pl.ds(pl.multiple_of(index * quarter, quarter), quarter)
        total = keep[at, :]
        for r in recv:
            total = total + r[at, :].astype(F32)
        return total

    keep_out[...] = rows(mine)
    small_out[...] = add_small(small, recv, n)
    for index, send in zip(others, sends):
        send[0:quarter, :] = rows(index).astype(BF16)
    value = small_out[...]
    for send in sends:
        pack_small(small_out, value, send, quarter)


def turn_kernel(sc, keep, small, r0, r1, r2, keep_out, small_out, s0, s1, s2, turned):
    total = keep[...]
    for r in (r0, r1, r2):
        total = total + r[0:64, :].astype(F32)
    total = total.T
    for mid in range(2):
        for low in range(2):
            at = [192 * high + 96 * (mid ^ high) + 48 * (low ^ high) for high in range(2)]
            turned[96 * low + 48 * mid : 96 * low + 48 * mid + 48, :] = jnp.concatenate(
                [total[at[0] : at[0] + 48], total[at[1] : at[1] + 48]], axis=1
            )
    mine, others = quarters(sc, 13)
    keep_out[...] = turned[pl.ds(pl.multiple_of(mine * 48, 8), 48), :]
    sums = add_small(small, (r0, r1, r2), 64)
    for j in range(3):
        small_out[16 * j : 16 * j + 16, :] = sums[:, 128 * j : 128 * (j + 1)]
    for index, send in zip(others, (s0, s1, s2)):
        send[0:48, :] = turned[pl.ds(pl.multiple_of(index * 48, 8), 48), :]
        send[48:96, :] = small_out[...]


def last_kernel(sc, keep, small, r0, r1, r2, keep_out, small_out, send):
    del sc
    kept = keep[...] + r0[0:48, :] + r1[0:48, :] + r2[0:48, :]
    sums = add_small(small, (r0, r1, r2), 48)
    keep_out[...] = kept
    small_out[...] = sums
    send[0:48, :] = kept
    send[48:96, :] = sums


def final_kernel(sc, keep, small, recv, second, first, g_gain, g_bias, flat):
    total = keep[...] + recv[0:48, :]
    second[...] = jnp.where(sc[15] == 1, total[:, 64:128], total[:, 0:64])
    sums = small[...] + recv[48:96, :]
    for j in range(3):
        part = sums[16 * j : 16 * j + 16]
        flat[0:12, 128 * j : 128 * (j + 1)] = part[0:12]
        flat[4 * j : 4 * j + 4, 384:512] = part[12:16]
    first[...] = flat[0:10, :]
    g_gain[...] = flat[10:11, :]
    g_bias[...] = flat[11:12, :]


def in_vmem(value):
    return pltpu.with_memory_space_constraint(value, pltpu.VMEM)


def window(sc, own_rows, moved, cot, wst, gain, bias, w2):
    whole = pl.BlockSpec(memory_space=pltpu.VMEM)
    shapes = [((1024, 384), F32), ((1056, 384), BF16), ((16, 384), F32)]
    return pl.pallas_call(
        window_kernel,
        grid_spec=pltpu.PrefetchScalarGridSpec(
            num_scalar_prefetch=1,
            grid=(ROWS // BLK,),
            in_specs=[
                whole, whole,
                pl.BlockSpec((BLK, CH), lambda i, sc: (i, 0)),
                whole, whole, whole, whole,
            ],
            out_specs=[pl.BlockSpec(memory_space=pltpu.VMEM)] * len(shapes),
            scratch_shapes=[
                pltpu.VMEM((320, 128), F32),
                pltpu.VMEM((64, 640), F32),
                pltpu.VMEM((64, 1024), F32),
                pltpu.VMEM((ROWS + GRAN, 128), F32),
                pltpu.VMEM((ROWS, 128), F32),
                pltpu.VMEM((ROWS + 16, 256), BF16),
                pltpu.VMEM((2, 128, ROWS), BF16),
                pltpu.VMEM((256, 2 * CH), BF16),
                pltpu.VMEM((CH, 3 * CH), F32),
                pltpu.VMEM((128, CH), F32),
                pltpu.VMEM((128, 128), F32),
                pltpu.VMEM((8, CH), F32),
                pltpu.VMEM((128, CH), F32),
                pltpu.VMEM((8, CH), F32),
            ],
        ),
        out_shape=[pltpu.VMEM(s, d) for s, d in shapes],
        compiler_params=pltpu.CompilerParams(vmem_limit_bytes=40 * 2**20),
        cost_estimate=pl.CostEstimate(flops=14 * 10**9, bytes_accessed=10 * 10**6, transcendentals=0),
        name="window",
    )(
        sc, in_vmem(own_rows), in_vmem(moved), pltpu.with_memory_space_constraint(cot, pltpu.HBM),
        in_vmem(wst), in_vmem(gain), in_vmem(bias), in_vmem(w2),
    )


def small_call(kernel, name, sc, args, shapes, scratch=(), place=pltpu.VMEM):
    args = [in_vmem(a) for a in args]
    return pl.pallas_call(
        kernel,
        in_specs=[pl.BlockSpec(memory_space=pltpu.SMEM)] + [pl.BlockSpec(memory_space=pltpu.VMEM)] * len(args),
        out_specs=[pl.BlockSpec(memory_space=pltpu.VMEM)] * len(shapes),
        out_shape=[place(s, d) for s, d in shapes],
        scratch_shapes=list(scratch),
        compiler_params=pltpu.CompilerParams(vmem_limit_bytes=8 * 2**20),
        name=name,
    )(sc, *args)


def swap(value, wide, bulk=0):
    return lax.ppermute(value, ("wide", "bulk"), [(i, i ^ (8 * wide + bulk)) for i in range(256)])


def rows_kernel(lengths, waves, out):
    for s in range(SLOTS):
        for i in range(80):
            lines_at = 80 * s + i
            out[lines_at : lines_at + 1, :] = waves[s : s + 1, 128 * i : 128 * i + 128]
    lane = lax.broadcasted_iota(jnp.int32, (16, 128), 1)
    tail = jnp.zeros((16, 128), F32)
    for s in range(SLOTS):
        units = lengths[s] // TAPS
        tail = jnp.where(lane == 32 * s, (units // 32).astype(F32), tail)
        tail = jnp.where(lane == 32 * s + 1, (units % 32).astype(F32), tail)
    out[320:336, :] = tail.astype(BF16)


def pick_kernel(first, sc, own, got_a, got_b, got_both, out):
    lane = lax.broadcasted_iota(jnp.int32, (16, 128), 1)
    refs = (own, got_b, got_a, got_both)
    tails = [r[320:336, :].astype(F32) for r in refs]
    tail = tails[0]
    for s in range(SLOTS):
        mask = sc[s]
        z_high, y_high = (mask >> 2) & 1, (mask >> 4) & 1
        if first:
            code = 2 * ((mask & 1) ^ z_high) + (((mask >> 3) & 1) ^ y_high)
        else:
            code = 2 * (((mask >> 1) & 1) ^ z_high) + y_high
        at = pl.ds(80 * s, 80)
        for k, ref in enumerate(refs):

            @pl.when(code == k)
            def _(ref=ref):
                out[at, :] = ref[at, :]

            if k:
                tail = jnp.where((lane // 32 == s) & (code == k), tails[k], tail)
    out[320:336, :] = tail.astype(BF16)


def route(waves, lengths, masks):
    out = [((336, 128), BF16)]
    (value,) = small_call(rows_kernel, "rows", lengths, (waves,), out)
    for a, b in ((1, 8), (2, 24)):
        got = [swap(value, a), swap(value, b), swap(value, a ^ b)]
        (value,) = small_call(functools.partial(pick_kernel, a == 1), "pick%d" % a, masks, (value, *got), out)
    moved = swap(value, 7)
    far = ((masks & 4) != 0)[:, None]
    tail = jnp.where(far, moved[320].reshape(4, 32), value[320].reshape(4, 32)).astype(F32)
    return value, moved, (tail[:, 0] * 32.0 + tail[:, 1]).astype(jnp.int32)


def window_inputs(conv_first):
    w = conv_first.astype(F32)
    even = jnp.pad(w, ((0, 6), (0, 0)))
    odd = jnp.pad(w, ((5, 1), (0, 0)))
    return jnp.concatenate([even, odd], axis=0)


def local(value, moved, units, masks, places, cot, conv_first, norm_gain, norm_bias, conv_second):
    sc = jnp.concatenate([units, masks, places])
    gain, bias = norm_gain[None, :], norm_bias[None, :]
    return sc, window(sc, value, moved, cot, window_inputs(conv_first), gain, bias, conv_second)


def per_device(waveforms, owner_of, lengths, cotangent, conv_first, norm_gain, norm_bias, conv_second):
    me = lax.axis_index("wide")
    place = lax.axis_index("bulk")
    masks = jnp.bitwise_xor(owner_of[0], me)
    value, moved, units = route(waveforms[0], lengths[0], masks)
    x_low, x_high, y_low, y_high = (place // 2) % 2, place // 4, (me // 8) % 2, me // 16
    z_low, z_mid, z_high = me % 2, (me // 2) % 2, (me // 4) % 2
    places = jnp.stack(
        [place % 2, x_low ^ x_high, y_low ^ y_high, x_high, y_high, z_low ^ z_high, z_mid ^ z_high, z_high, me]
    ).astype(jnp.int32)
    sc, (keep, send, small) = local(
        value, moved, units, masks, places, cotangent[0, 0],
        conv_first, norm_gain, norm_bias, conv_second,
    )
    recv = [swap(send, 0, 1)]
    for n, flag, y, x in ((1024, 9, 8, 2), (256, 11, 24, 6)):
        out = [((n // 4, 384), F32), ((16, 384), F32)] + [((n // 4 + 32, 384), BF16)] * 3
        kernel = functools.partial(combine_kernel, n, len(recv), flag)
        keep, small, *sends = small_call(kernel, "combine%d" % n, sc, (keep, small, *recv), out)
        recv = [swap(sends[0], y), swap(sends[1], 0, x), swap(sends[2], y, x)]
    out = [((48, 128), F32), ((48, 128), F32)] + [((96, 128), F32)] * 3
    keep, small, *sends = small_call(
        turn_kernel, "turn", sc, (keep, small, *recv), out, [pltpu.VMEM((192, 128), F32)]
    )
    recv = [swap(sends[0], 2), swap(sends[1], 1), swap(sends[2], 3)]
    keep, small, send = small_call(last_kernel, "last", sc, (keep, small, *recv), out[:3])
    recv = swap(send, 7)
    out = [((48, 64), F32), ((10, CH), F32), ((1, CH), F32), ((1, CH), F32)]
    second, first, g_gain, g_bias = small_call(
        final_kernel, "final", sc, (keep, small, recv), out, [pltpu.VMEM((16, CH), F32)], jax.ShapeDtypeStruct
    )
    return (second, first, g_gain[0], g_bias[0])


def solution(mesh):
    placed = (
        P("bulk", "wide", None),
        P("bulk", "wide"),
        P("bulk", "wide"),
        P("bulk", "wide", None, None),
        P(),
        P(),
        P(),
        P(),
    )
    return jax.shard_map(
        per_device,
        mesh=mesh,
        in_specs=placed,
        out_specs=(P("wide", "bulk"), P(), P(), P()),
        check_vma=False,
    )
```

```python
import functools

import jax
import jax.numpy as jnp
from jax import lax
from jax.experimental import pallas as pl
from jax.experimental.pallas import tpu as pltpu
from jax.sharding import PartitionSpec as P

F32 = jnp.float32
BF16 = jnp.bfloat16
HIGHEST = lax.Precision.HIGHEST
SLOTS = 4
TAPS = 10
GRAN = 1024
ROWS = 2048
CH = 512
BLK = 1024
BLOCKS = [
    (2 * xh + (xl ^ xh), 2 * yh + (yl ^ yh)) for xl in range(2) for yl in range(2) for xh in range(2) for yh in range(2)
]


def dot(a, b, precision=None):
    return jnp.dot(a, b, preferred_element_type=F32, precision=precision)


def dot_b(a, b):
    return lax.dot_general(a, b, (((1,), (1,)), ((), ())), preferred_element_type=F32)


def dot_t(a, b, precision=None):
    return lax.dot_general(
        a, b, (((0,), (0,)), ((), ())), preferred_element_type=F32, precision=precision
    )


def cdf_slope(v):
    cdf = 0.5 + 0.5 * lax.erf(v * 0.7071067811865476)
    return cdf, cdf + v * (jnp.exp2(v * v * (-0.5 * 1.4426950408889634)) * 0.3989422804014327)


def plan(sc):
    size = [sc[s] for s in range(SLOTS)]
    src = [sc[SLOTS + s] ^ sc[16] for s in range(SLOTS)]
    rank, off = [], []
    for s in range(SLOTS):
        before = [(src[q] < src[s]).astype(jnp.int32) for q in range(SLOTS) if q != s]
        sizes = [size[q] for q in range(SLOTS) if q != s]
        rank.append(sum(before))
        off.append(sum(b * n for b, n in zip(before, sizes)))
    out = []
    for r in range(SLOTS):
        hit = [(rank[s] == r).astype(jnp.int32) for s in range(SLOTS)]
        out.append(
            (
                sum(h * s for s, h in enumerate(hit)),
                sum(h * o for o, h in zip(off, hit)),
                sum(h * n for n, h in zip(size, hit)),
            )
        )
    return out


def by_lane(values, index):
    out = values[0]
    for s in range(1, len(values)):
        out = jnp.where(index == s, values[s], out)
    return out


def window_kernel(
    sc, own_rows, moved, params, cot_hbm, w2_hbm,
    keep, send, small,
    lines, wide, lanes16, buf, xd, xbig, xs, wbig, acc, nst, tc, im, grads, carry, cot, w2, cot_sem, w2_sem,
):
    step = pl.program_id(0)
    segs = plan(sc)

    wst = params.at[0:32]
    gain = params.at[32:33]
    bias = params.at[33:34]
    copies = (
        pltpu.make_async_copy(w2_hbm, w2, w2_sem),
        pltpu.make_async_copy(cot_hbm, cot, cot_sem),
    )

    @pl.when(step == 0)
    def _():
        for copy in copies:
            copy.start()
        for s in range(SLOTS):
            at = pl.ds(80 * s, 80)
            lines[at, :] = jnp.where((sc[SLOTS + s] & 4) != 0, moved[at, :], own_rows[at, :]).astype(F32)
            for c in range(5):
                wide[16 * s : 16 * s + 16, 128 * c : 128 * c + 128] = lines[pl.ds(80 * s + c, 16, stride=5), :]
        place = lax.broadcasted_iota(jnp.int32, (1, 1024), 1)
        place = jnp.where(place % 16 < TAPS, place // 16 * TAPS + place % 16, -1)
        perm = (lax.broadcasted_iota(jnp.int32, (640, 1), 0) == place).astype(F32).astype(BF16)
        lanes16[...] = dot(wide[...].astype(BF16), perm)
        buf[pl.ds(ROWS, 8), :] = jnp.zeros((8, 128), F32)
        own = (
            lax.broadcasted_iota(jnp.int32, (8, 1024), 1) % 128 // 16
            == lax.broadcasted_iota(jnp.int32, (8, 1024), 0)
        )
        for slot, off, _n in segs:
            for r in range(16):
                line = jnp.where(own, lanes16[pl.ds(16 * slot + r, 1), :], 0.0)
                for j in range(8):
                    buf[pl.ds(off + 64 * r + 8 * j, 8), :] = line[:, 128 * j : 128 * j + 128]
        src = lax.broadcasted_iota(jnp.int32, (128, 256), 0) % 16
        tap = lax.broadcasted_iota(jnp.int32, (128, 256), 1) % 16
        r0 = ((tap == src) & (src < TAPS)).astype(F32).astype(BF16)
        r1 = ((tap == src + TAPS) & (src < 5)).astype(F32).astype(BF16)
        one = (lax.broadcasted_iota(jnp.int32, (1, 256), 1) % 16 == 15).astype(F32)
        lane = lax.broadcasted_iota(jnp.int32, (1, 256), 1)
        starts = [o for _s, o, _n in segs]
        ends = [o + n for _s, o, n in segs]
        lo_big, hi_big = by_lane(starts, lane // 64), by_lane(ends, lane // 64)
        lane1 = lane[:, :128]
        odd = (lane1 // 16) % 2
        lo_d = by_lane(starts, lane1 // 32)
        hi_all = by_lane(ends, lane1 // 32)
        hi_d = hi_all - odd
        count = (hi_d - lo_d).astype(F32)

        sums = jnp.zeros((1, 128), F32)
        for rb in range(ROWS // BLK):
            base = rb * BLK
            b0 = buf[pl.ds(base, BLK), :].astype(BF16)
            b1 = buf[pl.ds(base + 1, BLK), :].astype(BF16)
            xr = dot(b0, r0) + dot(b1, r1) + one
            row = lax.broadcasted_iota(jnp.int32, (BLK, 1), 0) + base
            xbig[pl.ds(base, BLK), :] = jnp.where((row >= lo_big) & (row < hi_big), xr, 0.0).astype(BF16)
            x1 = xr[:, :128]
            raw = jnp.where((row >= lo_d) & (row < hi_d), x1, 0.0)
            sums = sums + jnp.sum(raw, axis=0, keepdims=True)
            xd[pl.ds(base, BLK), :] = x1
            full = jnp.where((row >= lo_d) & (row < hi_all), x1, 0.0)
            xs[0, :, base : base + BLK] = jnp.where(odd == 0, full, 0.0).T.astype(BF16)
            xs[1, :, base : base + BLK] = jnp.where(odd == 1, full, 0.0).T.astype(BF16)
        xbig[pl.ds(ROWS, 16), :] = jnp.zeros((16, 256), BF16)
        mu = sums / count
        main = jnp.zeros((128, 128), F32)
        rest = jnp.zeros((128, 128), F32)
        for rb in range(ROWS // BLK):
            base = rb * BLK
            row = lax.broadcasted_iota(jnp.int32, (BLK, 1), 0) + base
            d = jnp.where((row >= lo_d) & (row < hi_d), xd[pl.ds(base, BLK), :] - mu, 0.0)
            high = d.astype(BF16)
            low = (d - high.astype(F32)).astype(BF16)
            main = main + dot_t(high, high)
            rest = rest + dot_t(high, low)
        ri = lax.broadcasted_iota(jnp.int32, (128, 128), 0)
        ci = lax.broadcasted_iota(jnp.int32, (128, 128), 1)
        moment = jnp.where(ri // 16 == ci // 16, main + (rest + rest.T), 0.0)
        wrow = jnp.concatenate([wst[...]] * SLOTS, axis=0)
        v = dot(moment, wrow, HIGHEST)
        block8 = (
            lax.broadcasted_iota(jnp.int32, (8, 128), 0)
            == lax.broadcasted_iota(jnp.int32, (8, 128), 1) // 16
        ).astype(F32)
        u8 = dot(block8 * mu, wrow, HIGHEST)
        q8 = dot(block8, v * wrow, HIGHEST)
        tcol = jnp.sum(jnp.where(ri == ci, sums, 0.0), axis=1, keepdims=True)
        tc[...] = jnp.broadcast_to(tcol, (128, 128))
        e15 = (lax.broadcasted_iota(jnp.int32, (16, 1), 0) == 15).astype(F32)
        for s, (_slot, _off, n) in enumerate(segs):
            n_even = n.astype(F32)
            n_odd = n_even - 1.0
            n_all = n_even + n_odd
            ue, uo = u8[2 * s : 2 * s + 1], u8[2 * s + 1 : 2 * s + 2]
            mean = (n_even * ue + n_odd * uo) / n_all
            de, do = ue - mean, uo - mean
            spread = (
                q8[2 * s : 2 * s + 1] + q8[2 * s + 1 : 2 * s + 2]
                + n_even * de * de + n_odd * do * do
            ) / n_all
            inv = lax.rsqrt(spread + 1e-05)
            a = gain[...] * inv
            b = bias[...] - a * mean
            im[s : s + 1, :] = inv
            im[4 + s : 5 + s, :] = mean
            for g, dev in enumerate((de, do)):
                at = 32 * s + 16 * g
                nst[at : at + 16, :] = v[at : at + 16] + tcol[at : at + 16] * dev
                f = wrow[at : at + 16] * a + e15 * b
                p0 = f.astype(BF16)
                f = f - p0.astype(F32)
                p1 = f.astype(BF16)
                f = f - p1.astype(F32)
                cols = pl.ds(g * CH, CH)
                wbig[64 * s : 64 * s + 16, cols] = p0
                wbig[64 * s + 16 : 64 * s + 32, cols] = p1
                wbig[64 * s + 32 : 64 * s + 48, cols] = f.astype(BF16)
                wbig[64 * s + 48 : 64 * s + 64, cols] = jnp.zeros((16, CH), BF16)
        acc[...] = jnp.zeros_like(acc)
        grads[...] = jnp.zeros_like(grads)
        carry[...] = jnp.zeros_like(carry)
        for copy in copies:
            copy.wait()

    base = pl.multiple_of(step * BLK, BLK)
    pre_e = dot(xbig[pl.ds(base, BLK + 16), :], wbig[:, :CH])
    pre_o = dot(xbig[pl.ds(base, BLK), :], wbig[:, CH:])
    c_e, s_e = cdf_slope(pre_e)
    act_e = pre_e * c_e
    c_o, s_o = cdf_slope(pre_o)
    taps = jnp.concatenate(
        [act_e[:BLK].astype(BF16), (pre_o * c_o).astype(BF16), act_e[1 : BLK + 1].astype(BF16)], axis=1
    )
    late = dot(taps, w2[...])
    _c, slope = cdf_slope(late)
    row = lax.broadcasted_iota(jnp.int32, (BLK, 1), 0) + base
    drop = row == segs[0][1] + segs[0][2] - 1
    for _s, off, n in segs[1:]:
        drop = drop | (row == off + n - 1)
    grad = jnp.where(drop, 0.0, cot[pl.ds(base, BLK), :].astype(F32) * slope).astype(BF16)
    acc[...] += dot_t(grad, taps)

    third = dot_b(grad, w2[2 * CH :, :])
    row = lax.broadcasted_iota(jnp.int32, (BLK, 1), 0)
    shifted = jnp.where(row == 0, carry[0:1, :], pltpu.roll(third, 1, 0))
    carry[0:1, :] = third[BLK - 1 : BLK]
    ag_e = (dot_b(grad, w2[:CH, :]) + shifted) * s_e[:BLK]
    ag_o = dot_b(grad, w2[CH : 2 * CH, :]) * s_o
    total = grads[...]
    for g, ag in enumerate((ag_e, ag_o)):
        part = xs[g, :, pl.ds(base, BLK)]
        high = ag.astype(BF16)
        low = (ag - high.astype(F32)).astype(BF16)
        total = total + dot(part, high) + dot(part, low)
    grads[...] = total

    @pl.when(step == pl.num_programs(0) - 1)
    def _():
        z = jnp.zeros((32, CH), F32)
        g_bias = jnp.zeros((1, CH), F32)
        g_gain = jnp.zeros((1, CH), F32)
        g = gain[...]
        for s, (_slot, _off, n) in enumerate(segs):
            at = 32 * s
            a = grads[at : at + 32, :]
            inv, mean = im[s : s + 1, :], im[4 + s : 5 + s, :]
            count = 2.0 * n.astype(F32) - 1.0
            s1 = a[15:16] + a[31:32]
            s2 = inv * (jnp.sum(a * wst[...], axis=0, keepdims=True) - mean * s1)
            first = g * s1 / count
            cross = g * s2 / count
            z = z + inv * (
                g * a - first * tc[at : at + 32, 0:1] - (cross * inv) * nst[at : at + 32, :]
            )
            g_bias = g_bias + s1
            g_gain = g_gain + s2
        grads[0:10, :] = z[0:10] + z[21:31]
        grads[10:11, :] = g_gain
        grads[11:12, :] = g_bias
        small[0:12, :] = grads[0:12, 0:384]
        for j in range(3):
            small[12:16, 128 * j : 128 * (j + 1)] = grads[4 * j : 4 * j + 4, 384:512]
        core = sc[8]
        for k, (x, y) in enumerate(BLOCKS):
            lanes = pl.ds(384 * y, 384)
            rows = pl.ds(64 * k, 64)
            keep[rows, :] = acc[pl.ds(pl.multiple_of(x * 128 + core * 64, 64), 64), lanes]
            send[rows, :] = acc[
                pl.ds(pl.multiple_of(x * 128 + (1 - core) * 64, 64), 64), lanes
            ].astype(BF16)
        pack_small(small, small[...], send, 1024)


def pack_small(small, value, send, at):
    high = value.astype(BF16)
    low = (value - high.astype(F32)).astype(BF16)
    send[at : at + 16, :] = high
    send[at + 16 : at + 32, :] = low
    small[...] = high.astype(F32) + low.astype(F32)


def received_small(recv, at):
    if recv.dtype == F32:
        return recv[at:, :]
    return recv[at : at + 16, :].astype(F32) + recv[at + 16 : at + 32, :].astype(F32)


def quarters(sc, at):
    a, b = sc[at], sc[at + 1]
    return 2 * a + b, (2 * a + 1 - b, 2 * (1 - a) + b, 2 * (1 - a) + 1 - b)


def add_small(small, recvs, at):
    r = [received_small(recv, at) for recv in recvs]
    return small[...] + r[0] if len(r) == 1 else (small[...] + r[0]) + (r[1] + r[2])


def combine_kernel(n, recvs, flag, sc, keep, small, *refs):
    recv, (keep_out, small_out, *sends) = refs[:recvs], refs[recvs:]
    quarter = n // 4
    mine, others = quarters(sc, flag)

    def rows(index):
        at = pl.ds(pl.multiple_of(index * quarter, quarter), quarter)
        total = keep[at, :]
        for r in recv:
            total = total + r[at, :].astype(F32)
        return total

    keep_out[...] = rows(mine)
    small_out[...] = add_small(small, recv, n)
    for index, send in zip(others, sends):
        send[0:quarter, :] = rows(index).astype(BF16)
    value = small_out[...]
    for send in sends:
        pack_small(small_out, value, send, quarter)


def turn_kernel(sc, keep, small, r0, r1, r2, keep_out, small_out, s0, s1, s2, turned):
    total = keep[...]
    for r in (r0, r1, r2):
        total = total + r[0:64, :].astype(F32)
    total = total.T
    for mid in range(2):
        for low in range(2):
            at = [192 * high + 96 * (mid ^ high) + 48 * (low ^ high) for high in range(2)]
            turned[96 * low + 48 * mid : 96 * low + 48 * mid + 48, :] = jnp.concatenate(
                [total[at[0] : at[0] + 48], total[at[1] : at[1] + 48]], axis=1
            )
    mine, others = quarters(sc, 13)
    keep_out[...] = turned[pl.ds(pl.multiple_of(mine * 48, 8), 48), :]
    sums = add_small(small, (r0, r1, r2), 64)
    for j in range(3):
        small_out[16 * j : 16 * j + 16, :] = sums[:, 128 * j : 128 * (j + 1)]
    for index, send in zip(others, (s0, s1, s2)):
        send[0:48, :] = turned[pl.ds(pl.multiple_of(index * 48, 8), 48), :]
        send[48:96, :] = small_out[...]


def last_kernel(sc, keep, small, r0, r1, r2, keep_out, small_out, send):
    del sc
    kept = keep[...] + r0[0:48, :] + r1[0:48, :] + r2[0:48, :]
    sums = add_small(small, (r0, r1, r2), 48)
    keep_out[...] = kept
    small_out[...] = sums
    send[0:48, :] = kept
    send[48:96, :] = sums


def final_kernel(sc, keep, small, recv, second, first, g_gain, g_bias, flat):
    total = keep[...] + recv[0:48, :]
    second[...] = jnp.where(sc[15] == 1, total[:, 64:128], total[:, 0:64])
    sums = small[...] + recv[48:96, :]
    for j in range(3):
        part = sums[16 * j : 16 * j + 16]
        flat[0:12, 128 * j : 128 * (j + 1)] = part[0:12]
        flat[4 * j : 4 * j + 4, 384:512] = part[12:16]
    first[...] = flat[0:10, :]
    g_gain[...] = flat[10:11, :]
    g_bias[...] = flat[11:12, :]


def in_vmem(value):
    return pltpu.with_memory_space_constraint(value, pltpu.VMEM)


def window(sc, own_rows, moved, params, cot, w2):
    whole = pl.BlockSpec(memory_space=pltpu.VMEM)
    shapes = [((1024, 384), F32), ((1056, 384), BF16), ((16, 384), F32)]
    return pl.pallas_call(
        window_kernel,
        grid_spec=pltpu.PrefetchScalarGridSpec(
            num_scalar_prefetch=1,
            grid=(ROWS // BLK,),
            in_specs=[
                whole, whole, whole,
                pl.BlockSpec(memory_space=pltpu.HBM), pl.BlockSpec(memory_space=pltpu.HBM),
            ],
            out_specs=[pl.BlockSpec(memory_space=pltpu.VMEM)] * len(shapes),
            scratch_shapes=[
                pltpu.VMEM((320, 128), F32),
                pltpu.VMEM((64, 640), F32),
                pltpu.VMEM((64, 1024), F32),
                pltpu.VMEM((ROWS + GRAN, 128), F32),
                pltpu.VMEM((ROWS, 128), F32),
                pltpu.VMEM((ROWS + 16, 256), BF16),
                pltpu.VMEM((2, 128, ROWS), BF16),
                pltpu.VMEM((256, 2 * CH), BF16),
                pltpu.VMEM((CH, 3 * CH), F32),
                pltpu.VMEM((128, CH), F32),
                pltpu.VMEM((128, 128), F32),
                pltpu.VMEM((8, CH), F32),
                pltpu.VMEM((128, CH), F32),
                pltpu.VMEM((8, CH), F32),
                pltpu.VMEM((ROWS, CH), BF16),
                pltpu.VMEM((3 * CH, CH), BF16),
                pltpu.SemaphoreType.DMA,
                pltpu.SemaphoreType.DMA,
            ],
        ),
        out_shape=[pltpu.VMEM(s, d) for s, d in shapes],
        compiler_params=pltpu.CompilerParams(vmem_limit_bytes=40 * 2**20),
        cost_estimate=pl.CostEstimate(flops=14 * 10**9, bytes_accessed=10 * 10**6, transcendentals=0),
        name="window",
    )(
        sc, in_vmem(own_rows), in_vmem(moved), in_vmem(params),
        pltpu.with_memory_space_constraint(cot, pltpu.HBM), pltpu.with_memory_space_constraint(w2, pltpu.HBM),
    )


def small_call(kernel, name, sc, args, shapes, scratch=(), place=pltpu.VMEM):
    args = [in_vmem(a) for a in args]
    return pl.pallas_call(
        kernel,
        in_specs=[pl.BlockSpec(memory_space=pltpu.SMEM)] + [pl.BlockSpec(memory_space=pltpu.VMEM)] * len(args),
        out_specs=[pl.BlockSpec(memory_space=pltpu.VMEM)] * len(shapes),
        out_shape=[place(s, d) for s, d in shapes],
        scratch_shapes=list(scratch),
        compiler_params=pltpu.CompilerParams(vmem_limit_bytes=8 * 2**20),
        name=name,
    )(sc, *args)


def swap(value, wide, bulk=0):
    return lax.ppermute(value, ("wide", "bulk"), [(i, i ^ (8 * wide + bulk)) for i in range(256)])


def rows_kernel(lengths, waves, out):
    for s in range(SLOTS):
        for i in range(80):
            lines_at = 80 * s + i
            out[lines_at : lines_at + 1, :] = waves[s : s + 1, 128 * i : 128 * i + 128]
    lane = lax.broadcasted_iota(jnp.int32, (16, 128), 1)
    tail = jnp.zeros((16, 128), F32)
    for s in range(SLOTS):
        units = lengths[s] // TAPS
        tail = jnp.where(lane == 32 * s, (units // 32).astype(F32), tail)
        tail = jnp.where(lane == 32 * s + 1, (units % 32).astype(F32), tail)
    out[320:336, :] = tail.astype(BF16)


def lay_rows(lengths, waves):
    return pl.pallas_call(
        rows_kernel,
        in_specs=[pl.BlockSpec(memory_space=pltpu.SMEM), pl.BlockSpec(memory_space=pltpu.VMEM)],
        out_specs=pl.BlockSpec(memory_space=pltpu.VMEM),
        out_shape=pltpu.VMEM((336, 128), BF16),
        compiler_params=pltpu.CompilerParams(vmem_limit_bytes=8 * 2**20),
        name="rows",
    )(*(pltpu.with_memory_space_constraint(a, pltpu.HBM) for a in (lengths, waves)))


def pick_kernel(first, sc, own, got_a, got_b, got_both, out):
    lane = lax.broadcasted_iota(jnp.int32, (16, 128), 1)
    refs = (own, got_b, got_a, got_both)
    tails = [r[320:336, :].astype(F32) for r in refs]
    tail = tails[0]
    for s in range(SLOTS):
        mask = sc[s]
        z_high, y_high = (mask >> 2) & 1, (mask >> 4) & 1
        if first:
            code = 2 * ((mask & 1) ^ z_high) + (((mask >> 3) & 1) ^ y_high)
        else:
            code = 2 * (((mask >> 1) & 1) ^ z_high) + y_high
        at = pl.ds(80 * s, 80)
        for k, ref in enumerate(refs):

            @pl.when(code == k)
            def _(ref=ref):
                out[at, :] = ref[at, :]

            if k:
                tail = jnp.where((lane // 32 == s) & (code == k), tails[k], tail)
    out[320:336, :] = tail.astype(BF16)


def route(waves, lengths, masks):
    out = [((336, 128), BF16)]
    value = lay_rows(lengths, waves)
    for a, b in ((1, 8), (2, 24)):
        got = [swap(value, a), swap(value, b), swap(value, a ^ b)]
        (value,) = small_call(functools.partial(pick_kernel, a == 1), "pick%d" % a, masks, (value, *got), out)
    moved = swap(value, 7)
    far = ((masks & 4) != 0)[:, None]
    tail = jnp.where(far, moved[320].reshape(4, 32), value[320].reshape(4, 32)).astype(F32)
    return value, moved, (tail[:, 0] * 32.0 + tail[:, 1]).astype(jnp.int32)


def window_inputs(conv_first, gain, bias):
    w = conv_first.astype(F32)
    rows = [jnp.pad(w, ((0, 6), (0, 0))), jnp.pad(w, ((5, 1), (0, 0))), gain[None, :], bias[None, :]]
    return jnp.concatenate(rows + [jnp.zeros((6, CH), F32)], axis=0)


def local(value, moved, units, masks, places, cot, conv_first, norm_gain, norm_bias, conv_second):
    sc = jnp.concatenate([units, masks, places])
    params = window_inputs(conv_first, norm_gain, norm_bias)
    return sc, window(sc, value, moved, params, cot, conv_second)


def per_device(waveforms, owner_of, lengths, cotangent, conv_first, norm_gain, norm_bias, conv_second):
    me = lax.axis_index("wide")
    place = lax.axis_index("bulk")
    masks = jnp.bitwise_xor(owner_of[0], me)
    value, moved, units = route(waveforms[0], lengths[0], masks)
    x_low, x_high, y_low, y_high = (place // 2) % 2, place // 4, (me // 8) % 2, me // 16
    z_low, z_mid, z_high = me % 2, (me // 2) % 2, (me // 4) % 2
    places = jnp.stack(
        [place % 2, x_low ^ x_high, y_low ^ y_high, x_high, y_high, z_low ^ z_high, z_mid ^ z_high, z_high, me]
    ).astype(jnp.int32)
    sc, (keep, send, small) = local(
        value, moved, units, masks, places, cotangent[0, 0],
        conv_first, norm_gain, norm_bias, conv_second,
    )
    recv = [swap(send, 0, 1)]
    for n, flag, y, x in ((1024, 9, 8, 2), (256, 11, 24, 6)):
        out = [((n // 4, 384), F32), ((16, 384), F32)] + [((n // 4 + 32, 384), BF16)] * 3
        kernel = functools.partial(combine_kernel, n, len(recv), flag)
        keep, small, *sends = small_call(kernel, "combine%d" % n, sc, (keep, small, *recv), out)
        recv = [swap(sends[0], y), swap(sends[1], 0, x), swap(sends[2], y, x)]
    out = [((48, 128), F32), ((48, 128), F32)] + [((96, 128), F32)] * 3
    keep, small, *sends = small_call(
        turn_kernel, "turn", sc, (keep, small, *recv), out, [pltpu.VMEM((192, 128), F32)]
    )
    recv = [swap(sends[0], 2), swap(sends[1], 1), swap(sends[2], 3)]
    keep, small, send = small_call(last_kernel, "last", sc, (keep, small, *recv), out[:3])
    recv = swap(send, 7)
    out = [((48, 64), F32), ((10, CH), F32), ((1, CH), F32), ((1, CH), F32)]
    second, first, g_gain, g_bias = small_call(
        final_kernel, "final", sc, (keep, small, recv), out, [pltpu.VMEM((16, CH), F32)], jax.ShapeDtypeStruct
    )
    return (second, first, g_gain[0], g_bias[0])


def solution(mesh):
    placed = (
        P("bulk", "wide", None),
        P("bulk", "wide"),
        P("bulk", "wide"),
        P("bulk", "wide", None, None),
        P(),
        P(),
        P(),
        P(),
    )
    return jax.shard_map(
        per_device,
        mesh=mesh,
        in_specs=placed,
        out_specs=(P("wide", "bulk"), P(), P(), P()),
        check_vma=False,
    )
```

```python
import functools

import jax
import jax.numpy as jnp
from jax import lax
from jax.experimental import pallas as pl
from jax.experimental.pallas import tpu as pltpu
from jax.sharding import PartitionSpec as P

F32 = jnp.float32
BF16 = jnp.bfloat16
HIGHEST = lax.Precision.HIGHEST
SLOTS = 4
TAPS = 10
GRAN = 1024
ROWS = 2048
CH = 512
BLK = 1024
BLOCKS = [
    (2 * xh + (xl ^ xh), 2 * yh + (yl ^ yh)) for xl in range(2) for yl in range(2) for xh in range(2) for yh in range(2)
]


def dot(a, b, precision=None):
    return jnp.dot(a, b, preferred_element_type=F32, precision=precision)


def dot_b(a, b):
    return lax.dot_general(a, b, (((1,), (1,)), ((), ())), preferred_element_type=F32)


def dot_t(a, b, precision=None):
    return lax.dot_general(
        a, b, (((0,), (0,)), ((), ())), preferred_element_type=F32, precision=precision
    )


def cdf_slope(v):
    cdf = 0.5 + 0.5 * lax.erf(v * 0.7071067811865476)
    return cdf, cdf + v * (jnp.exp2(v * v * (-0.5 * 1.4426950408889634)) * 0.3989422804014327)


def plan(sc):
    size = [sc[s] for s in range(SLOTS)]
    src = [sc[SLOTS + s] ^ sc[16] for s in range(SLOTS)]
    rank, off = [], []
    for s in range(SLOTS):
        before = [(src[q] < src[s]).astype(jnp.int32) for q in range(SLOTS) if q != s]
        sizes = [size[q] for q in range(SLOTS) if q != s]
        rank.append(sum(before))
        off.append(sum(b * n for b, n in zip(before, sizes)))
    out = []
    for r in range(SLOTS):
        hit = [(rank[s] == r).astype(jnp.int32) for s in range(SLOTS)]
        out.append(
            (
                sum(h * s for s, h in enumerate(hit)),
                sum(h * o for o, h in zip(off, hit)),
                sum(h * n for n, h in zip(size, hit)),
            )
        )
    return out


def by_lane(values, index):
    out = values[0]
    for s in range(1, len(values)):
        out = jnp.where(index == s, values[s], out)
    return out


def window_kernel(
    sc, own_rows, moved, params, cot_hbm, w2_hbm,
    keep, send, small,
    lines, wide, lanes16, buf, xd, xbig, xs, wbig, acc, nst, tc, im, grads, carry, cot, w2, cot_sem, w2_sem,
):
    step = pl.program_id(0)
    segs = plan(sc)

    wst = params.at[0:32]
    gain = params.at[32:33]
    bias = params.at[33:34]
    copies = (
        pltpu.make_async_copy(w2_hbm, w2, w2_sem),
        pltpu.make_async_copy(cot_hbm, cot, cot_sem),
    )

    @pl.when(step == 0)
    def _():
        for copy in copies:
            copy.start()
        for s in range(SLOTS):
            at = pl.ds(80 * s, 80)
            lines[at, :] = jnp.where((sc[SLOTS + s] & 4) != 0, moved[at, :], own_rows[at, :]).astype(F32)
            for c in range(5):
                wide[16 * s : 16 * s + 16, 128 * c : 128 * c + 128] = lines[pl.ds(80 * s + c, 16, stride=5), :]
        place = lax.broadcasted_iota(jnp.int32, (1, 1024), 1)
        place = jnp.where(place % 16 < TAPS, place // 16 * TAPS + place % 16, -1)
        perm = (lax.broadcasted_iota(jnp.int32, (640, 1), 0) == place).astype(F32).astype(BF16)
        lanes16[...] = dot(wide[...].astype(BF16), perm)
        buf[pl.ds(ROWS, 8), :] = jnp.zeros((8, 128), F32)
        own = (
            lax.broadcasted_iota(jnp.int32, (8, 1024), 1) % 128 // 16
            == lax.broadcasted_iota(jnp.int32, (8, 1024), 0)
        )
        for slot, off, _n in segs:
            for r in range(16):
                line = jnp.where(own, lanes16[pl.ds(16 * slot + r, 1), :], 0.0)
                for j in range(8):
                    buf[pl.ds(off + 64 * r + 8 * j, 8), :] = line[:, 128 * j : 128 * j + 128]
        src = lax.broadcasted_iota(jnp.int32, (128, 256), 0) % 16
        tap = lax.broadcasted_iota(jnp.int32, (128, 256), 1) % 16
        r0 = ((tap == src) & (src < TAPS)).astype(F32).astype(BF16)
        r1 = ((tap == src + TAPS) & (src < 5)).astype(F32).astype(BF16)
        one = (lax.broadcasted_iota(jnp.int32, (1, 256), 1) % 16 == 15).astype(F32)
        lane = lax.broadcasted_iota(jnp.int32, (1, 256), 1)
        starts = [o for _s, o, _n in segs]
        ends = [o + n for _s, o, n in segs]
        lo_big, hi_big = by_lane(starts, lane // 64), by_lane(ends, lane // 64)
        lane1 = lane[:, :128]
        odd = (lane1 // 16) % 2
        lo_d = by_lane(starts, lane1 // 32)
        hi_all = by_lane(ends, lane1 // 32)
        hi_d = hi_all - odd
        count = (hi_d - lo_d).astype(F32)

        sums = jnp.zeros((1, 128), F32)
        for rb in range(ROWS // BLK):
            base = rb * BLK
            b0 = buf[pl.ds(base, BLK), :].astype(BF16)
            b1 = buf[pl.ds(base + 1, BLK), :].astype(BF16)
            xr = dot(b0, r0) + dot(b1, r1) + one
            row = lax.broadcasted_iota(jnp.int32, (BLK, 1), 0) + base
            xbig[pl.ds(base, BLK), :] = jnp.where((row >= lo_big) & (row < hi_big), xr, 0.0).astype(BF16)
            x1 = xr[:, :128]
            raw = jnp.where((row >= lo_d) & (row < hi_d), x1, 0.0)
            sums = sums + jnp.sum(raw, axis=0, keepdims=True)
            xd[pl.ds(base, BLK), :] = x1
            full = jnp.where((row >= lo_d) & (row < hi_all), x1, 0.0)
            xs[0, :, base : base + BLK] = jnp.where(odd == 0, full, 0.0).T.astype(BF16)
            xs[1, :, base : base + BLK] = jnp.where(odd == 1, full, 0.0).T.astype(BF16)
        xbig[pl.ds(ROWS, 16), :] = jnp.zeros((16, 256), BF16)
        mu = sums / count
        main = jnp.zeros((128, 128), F32)
        rest = jnp.zeros((128, 128), F32)
        for rb in range(ROWS // BLK):
            base = rb * BLK
            row = lax.broadcasted_iota(jnp.int32, (BLK, 1), 0) + base
            d = jnp.where((row >= lo_d) & (row < hi_d), xd[pl.ds(base, BLK), :] - mu, 0.0)
            high = d.astype(BF16)
            low = (d - high.astype(F32)).astype(BF16)
            main = main + dot_t(high, high)
            rest = rest + dot_t(high, low)
        ri = lax.broadcasted_iota(jnp.int32, (128, 128), 0)
        ci = lax.broadcasted_iota(jnp.int32, (128, 128), 1)
        moment = jnp.where(ri // 16 == ci // 16, main + (rest + rest.T), 0.0)
        wrow = jnp.concatenate([wst[...]] * SLOTS, axis=0)
        v = dot(moment, wrow, HIGHEST)
        block8 = (
            lax.broadcasted_iota(jnp.int32, (8, 128), 0)
            == lax.broadcasted_iota(jnp.int32, (8, 128), 1) // 16
        ).astype(F32)
        u8 = dot(block8 * mu, wrow, HIGHEST)
        q8 = dot(block8, v * wrow, HIGHEST)
        tcol = jnp.sum(jnp.where(ri == ci, sums, 0.0), axis=1, keepdims=True)
        tc[...] = jnp.broadcast_to(tcol, (128, 128))
        e15 = (lax.broadcasted_iota(jnp.int32, (16, 1), 0) == 15).astype(F32)
        for s, (_slot, _off, n) in enumerate(segs):
            n_even = n.astype(F32)
            n_odd = n_even - 1.0
            n_all = n_even + n_odd
            ue, uo = u8[2 * s : 2 * s + 1], u8[2 * s + 1 : 2 * s + 2]
            mean = (n_even * ue + n_odd * uo) / n_all
            de, do = ue - mean, uo - mean
            spread = (
                q8[2 * s : 2 * s + 1] + q8[2 * s + 1 : 2 * s + 2]
                + n_even * de * de + n_odd * do * do
            ) / n_all
            inv = lax.rsqrt(spread + 1e-05)
            a = gain[...] * inv
            b = bias[...] - a * mean
            im[s : s + 1, :] = inv
            im[4 + s : 5 + s, :] = mean
            for g, dev in enumerate((de, do)):
                at = 32 * s + 16 * g
                nst[at : at + 16, :] = v[at : at + 16] + tcol[at : at + 16] * dev
                f = wrow[at : at + 16] * a + e15 * b
                p0 = f.astype(BF16)
                f = f - p0.astype(F32)
                p1 = f.astype(BF16)
                f = f - p1.astype(F32)
                cols = pl.ds(g * CH, CH)
                wbig[64 * s : 64 * s + 16, cols] = p0
                wbig[64 * s + 16 : 64 * s + 32, cols] = p1
                wbig[64 * s + 32 : 64 * s + 48, cols] = f.astype(BF16)
                wbig[64 * s + 48 : 64 * s + 64, cols] = jnp.zeros((16, CH), BF16)
        acc[...] = jnp.zeros_like(acc)
        grads[...] = jnp.zeros_like(grads)
        carry[...] = jnp.zeros_like(carry)
        for copy in copies:
            copy.wait()

    base = pl.multiple_of(step * BLK, BLK)
    pre_e = dot(xbig[pl.ds(base, BLK + 16), :], wbig[:, :CH])
    pre_o = dot(xbig[pl.ds(base, BLK), :], wbig[:, CH:])
    c_e, s_e = cdf_slope(pre_e)
    act_e = pre_e * c_e
    c_o, s_o = cdf_slope(pre_o)
    taps = jnp.concatenate(
        [act_e[:BLK].astype(BF16), (pre_o * c_o).astype(BF16), act_e[1 : BLK + 1].astype(BF16)], axis=1
    )
    late = dot(taps, w2[...])
    _c, slope = cdf_slope(late)
    row = lax.broadcasted_iota(jnp.int32, (BLK, 1), 0) + base
    drop = row == segs[0][1] + segs[0][2] - 1
    for _s, off, n in segs[1:]:
        drop = drop | (row == off + n - 1)
    grad = jnp.where(drop, 0.0, cot[pl.ds(base, BLK), :].astype(F32) * slope).astype(BF16)
    acc[...] += dot_t(grad, taps)

    third = dot_b(grad, w2[2 * CH :, :])
    row = lax.broadcasted_iota(jnp.int32, (BLK, 1), 0)
    shifted = jnp.where(row == 0, carry[0:1, :], pltpu.roll(third, 1, 0))
    carry[0:1, :] = third[BLK - 1 : BLK]
    ag_e = (dot_b(grad, w2[:CH, :]) + shifted) * s_e[:BLK]
    ag_o = dot_b(grad, w2[CH : 2 * CH, :]) * s_o
    total = grads[...]
    for g, ag in enumerate((ag_e, ag_o)):
        part = xs[g, :, pl.ds(base, BLK)]
        high = ag.astype(BF16)
        low = (ag - high.astype(F32)).astype(BF16)
        total = total + dot(part, high) + dot(part, low)
    grads[...] = total

    @pl.when(step == pl.num_programs(0) - 1)
    def _():
        z = jnp.zeros((32, CH), F32)
        g_bias = jnp.zeros((1, CH), F32)
        g_gain = jnp.zeros((1, CH), F32)
        g = gain[...]
        for s, (_slot, _off, n) in enumerate(segs):
            at = 32 * s
            a = grads[at : at + 32, :]
            inv, mean = im[s : s + 1, :], im[4 + s : 5 + s, :]
            count = 2.0 * n.astype(F32) - 1.0
            s1 = a[15:16] + a[31:32]
            s2 = inv * (jnp.sum(a * wst[...], axis=0, keepdims=True) - mean * s1)
            first = g * s1 / count
            cross = g * s2 / count
            z = z + inv * (
                g * a - first * tc[at : at + 32, 0:1] - (cross * inv) * nst[at : at + 32, :]
            )
            g_bias = g_bias + s1
            g_gain = g_gain + s2
        grads[0:10, :] = z[0:10] + z[21:31]
        grads[10:11, :] = g_gain
        grads[11:12, :] = g_bias
        small[0:12, :] = grads[0:12, 0:384]
        for j in range(3):
            small[12:16, 128 * j : 128 * (j + 1)] = grads[4 * j : 4 * j + 4, 384:512]
        core = sc[8]
        for k, (x, y) in enumerate(BLOCKS):
            lanes = pl.ds(384 * y, 384)
            rows = pl.ds(64 * k, 64)
            keep[rows, :] = acc[pl.ds(pl.multiple_of(x * 128 + core * 64, 64), 64), lanes]
            send[rows, :] = acc[
                pl.ds(pl.multiple_of(x * 128 + (1 - core) * 64, 64), 64), lanes
            ].astype(BF16)
        pack_small(small, small[...], send, 1024)


def pack_small(small, value, send, at):
    high = value.astype(BF16)
    low = (value - high.astype(F32)).astype(BF16)
    send[at : at + 16, :] = high
    send[at + 16 : at + 32, :] = low
    small[...] = high.astype(F32) + low.astype(F32)


def received_small(recv, at):
    if recv.dtype == F32:
        return recv[at:, :]
    return recv[at : at + 16, :].astype(F32) + recv[at + 16 : at + 32, :].astype(F32)


def quarters(sc, at):
    a, b = sc[at], sc[at + 1]
    return 2 * a + b, (2 * (1 - a) + 1 - b, 2 * a + 1 - b, 2 * (1 - a) + b)


def add_small(small, recvs, at):
    r = [received_small(recv, at) for recv in recvs]
    return small[...] + r[0] if len(r) == 1 else (small[...] + r[1]) + (r[2] + r[0])


def combine_kernel(n, recvs, flag, sc, keep, small, *refs):
    recv, (keep_out, small_out, *sends) = refs[:recvs], refs[recvs:]
    quarter = n // 4
    mine, others = quarters(sc, flag)

    def rows(index):
        at = pl.ds(pl.multiple_of(index * quarter, quarter), quarter)
        total = keep[at, :]
        for r in recv:
            total = total + r[at, :].astype(F32)
        return total

    keep_out[...] = rows(mine)
    small_out[...] = add_small(small, recv, n)
    for index, send in zip(others, sends):
        send[0:quarter, :] = rows(index).astype(BF16)
    value = small_out[...]
    for send in sends:
        pack_small(small_out, value, send, quarter)


def turn_kernel(sc, keep, small, r0, r1, r2, keep_out, small_out, s0, s1, s2, turned):
    total = keep[...]
    for r in (r0, r1, r2):
        total = total + r[0:64, :].astype(F32)
    total = total.T
    for mid in range(2):
        for low in range(2):
            at = [192 * high + 96 * (mid ^ high) + 48 * (low ^ high) for high in range(2)]
            turned[96 * low + 48 * mid : 96 * low + 48 * mid + 48, :] = jnp.concatenate(
                [total[at[0] : at[0] + 48], total[at[1] : at[1] + 48]], axis=1
            )
    mine, others = quarters(sc, 13)
    keep_out[...] = turned[pl.ds(pl.multiple_of(mine * 48, 8), 48), :]
    sums = add_small(small, (r0, r1, r2), 64)
    for j in range(3):
        small_out[16 * j : 16 * j + 16, :] = sums[:, 128 * j : 128 * (j + 1)]
    for index, send in zip(others, (s0, s1, s2)):
        send[0:48, :] = turned[pl.ds(pl.multiple_of(index * 48, 8), 48), :]
        send[48:96, :] = small_out[...]


def last_kernel(sc, keep, small, r0, r1, r2, keep_out, small_out, send):
    del sc
    kept = keep[...] + r0[0:48, :] + r1[0:48, :] + r2[0:48, :]
    sums = add_small(small, (r0, r1, r2), 48)
    keep_out[...] = kept
    small_out[...] = sums
    send[0:48, :] = kept
    send[48:96, :] = sums


def final_kernel(sc, keep, small, recv, second, first, g_gain, g_bias, flat):
    total = keep[...] + recv[0:48, :]
    second[...] = jnp.where(sc[15] == 1, total[:, 64:128], total[:, 0:64])
    sums = small[...] + recv[48:96, :]
    for j in range(3):
        part = sums[16 * j : 16 * j + 16]
        flat[0:12, 128 * j : 128 * (j + 1)] = part[0:12]
        flat[4 * j : 4 * j + 4, 384:512] = part[12:16]
    first[...] = flat[0:10, :]
    g_gain[...] = flat[10:11, :]
    g_bias[...] = flat[11:12, :]


def in_vmem(value):
    return pltpu.with_memory_space_constraint(value, pltpu.VMEM)


def window(sc, own_rows, moved, params, cot, w2):
    whole = pl.BlockSpec(memory_space=pltpu.VMEM)
    shapes = [((1024, 384), F32), ((1056, 384), BF16), ((16, 384), F32)]
    return pl.pallas_call(
        window_kernel,
        grid_spec=pltpu.PrefetchScalarGridSpec(
            num_scalar_prefetch=1,
            grid=(ROWS // BLK,),
            in_specs=[
                whole, whole, whole,
                pl.BlockSpec(memory_space=pltpu.HBM), pl.BlockSpec(memory_space=pltpu.HBM),
            ],
            out_specs=[pl.BlockSpec(memory_space=pltpu.VMEM)] * len(shapes),
            scratch_shapes=[
                pltpu.VMEM((320, 128), F32),
                pltpu.VMEM((64, 640), F32),
                pltpu.VMEM((64, 1024), F32),
                pltpu.VMEM((ROWS + GRAN, 128), F32),
                pltpu.VMEM((ROWS, 128), F32),
                pltpu.VMEM((ROWS + 16, 256), BF16),
                pltpu.VMEM((2, 128, ROWS), BF16),
                pltpu.VMEM((256, 2 * CH), BF16),
                pltpu.VMEM((CH, 3 * CH), F32),
                pltpu.VMEM((128, CH), F32),
                pltpu.VMEM((128, 128), F32),
                pltpu.VMEM((8, CH), F32),
                pltpu.VMEM((128, CH), F32),
                pltpu.VMEM((8, CH), F32),
                pltpu.VMEM((ROWS, CH), BF16),
                pltpu.VMEM((3 * CH, CH), BF16),
                pltpu.SemaphoreType.DMA,
                pltpu.SemaphoreType.DMA,
            ],
        ),
        out_shape=[pltpu.VMEM(s, d) for s, d in shapes],
        compiler_params=pltpu.CompilerParams(vmem_limit_bytes=40 * 2**20),
        cost_estimate=pl.CostEstimate(flops=14 * 10**9, bytes_accessed=10 * 10**6, transcendentals=0),
        name="window",
    )(
        sc, in_vmem(own_rows), in_vmem(moved), in_vmem(params),
        pltpu.with_memory_space_constraint(cot, pltpu.HBM), pltpu.with_memory_space_constraint(w2, pltpu.HBM),
    )


def small_call(kernel, name, sc, args, shapes, scratch=(), place=pltpu.VMEM):
    args = [in_vmem(a) for a in args]
    return pl.pallas_call(
        kernel,
        in_specs=[pl.BlockSpec(memory_space=pltpu.SMEM)] + [pl.BlockSpec(memory_space=pltpu.VMEM)] * len(args),
        out_specs=[pl.BlockSpec(memory_space=pltpu.VMEM)] * len(shapes),
        out_shape=[place(s, d) for s, d in shapes],
        scratch_shapes=list(scratch),
        compiler_params=pltpu.CompilerParams(vmem_limit_bytes=8 * 2**20),
        name=name,
    )(sc, *args)


def swap(value, wide, bulk=0):
    return lax.ppermute(value, ("wide", "bulk"), [(i, i ^ (8 * wide + bulk)) for i in range(256)])


def rows_kernel(lengths, waves, out):
    for s in range(SLOTS):
        for i in range(80):
            lines_at = 80 * s + i
            out[lines_at : lines_at + 1, :] = waves[s : s + 1, 128 * i : 128 * i + 128]
    lane = lax.broadcasted_iota(jnp.int32, (16, 128), 1)
    tail = jnp.zeros((16, 128), F32)
    for s in range(SLOTS):
        units = lengths[s] // TAPS
        tail = jnp.where(lane == 32 * s, (units // 32).astype(F32), tail)
        tail = jnp.where(lane == 32 * s + 1, (units % 32).astype(F32), tail)
    out[320:336, :] = tail.astype(BF16)


def lay_rows(lengths, waves):
    return pl.pallas_call(
        rows_kernel,
        in_specs=[pl.BlockSpec(memory_space=pltpu.SMEM), pl.BlockSpec(memory_space=pltpu.VMEM)],
        out_specs=pl.BlockSpec(memory_space=pltpu.VMEM),
        out_shape=pltpu.VMEM((336, 128), BF16),
        compiler_params=pltpu.CompilerParams(vmem_limit_bytes=8 * 2**20),
        name="rows",
    )(*(pltpu.with_memory_space_constraint(a, pltpu.HBM) for a in (lengths, waves)))


def pick_kernel(first, sc, own, got_a, got_b, got_both, out):
    lane = lax.broadcasted_iota(jnp.int32, (16, 128), 1)
    refs = (own, got_b, got_a, got_both)
    tails = [r[320:336, :].astype(F32) for r in refs]
    tail = tails[0]
    for s in range(SLOTS):
        mask = sc[s]
        z_high, y_high = (mask >> 2) & 1, (mask >> 4) & 1
        if first:
            code = 2 * ((mask & 1) ^ z_high) + (((mask >> 3) & 1) ^ y_high)
        else:
            code = 2 * (((mask >> 1) & 1) ^ z_high) + y_high
        at = pl.ds(80 * s, 80)
        for k, ref in enumerate(refs):

            @pl.when(code == k)
            def _(ref=ref):
                out[at, :] = ref[at, :]

            if k:
                tail = jnp.where((lane // 32 == s) & (code == k), tails[k], tail)
    out[320:336, :] = tail.astype(BF16)


def route(waves, lengths, masks):
    out = [((336, 128), BF16)]
    value = lay_rows(lengths, waves)
    for a, b in ((1, 8), (2, 24)):
        got = [swap(value, a), swap(value, b), swap(value, a ^ b)]
        (value,) = small_call(functools.partial(pick_kernel, a == 1), "pick%d" % a, masks, (value, *got), out)
    moved = swap(value, 7)
    far = ((masks & 4) != 0)[:, None]
    tail = jnp.where(far, moved[320].reshape(4, 32), value[320].reshape(4, 32)).astype(F32)
    return value, moved, (tail[:, 0] * 32.0 + tail[:, 1]).astype(jnp.int32)


def window_inputs(conv_first, gain, bias):
    w = conv_first.astype(F32)
    rows = [jnp.pad(w, ((0, 6), (0, 0))), jnp.pad(w, ((5, 1), (0, 0))), gain[None, :], bias[None, :]]
    return jnp.concatenate(rows + [jnp.zeros((6, CH), F32)], axis=0)


def local(value, moved, units, masks, places, cot, conv_first, norm_gain, norm_bias, conv_second):
    sc = jnp.concatenate([units, masks, places])
    params = window_inputs(conv_first, norm_gain, norm_bias)
    return sc, window(sc, value, moved, params, cot, conv_second)


def per_device(waveforms, owner_of, lengths, cotangent, conv_first, norm_gain, norm_bias, conv_second):
    me = lax.axis_index("wide")
    place = lax.axis_index("bulk")
    masks = jnp.bitwise_xor(owner_of[0], me)
    value, moved, units = route(waveforms[0], lengths[0], masks)
    x_low, x_high, y_low, y_high = (place // 2) % 2, place // 4, (me // 8) % 2, me // 16
    z_low, z_mid, z_high = me % 2, (me // 2) % 2, (me // 4) % 2
    places = jnp.stack(
        [place % 2, x_low ^ x_high, y_low ^ y_high, x_high, y_high, z_low ^ z_high, z_mid ^ z_high, z_high, me]
    ).astype(jnp.int32)
    sc, (keep, send, small) = local(
        value, moved, units, masks, places, cotangent[0, 0],
        conv_first, norm_gain, norm_bias, conv_second,
    )
    recv = [swap(send, 0, 1)]
    for n, flag, y, x in ((1024, 9, 8, 2), (256, 11, 24, 6)):
        out = [((n // 4, 384), F32), ((16, 384), F32)] + [((n // 4 + 32, 384), BF16)] * 3
        kernel = functools.partial(combine_kernel, n, len(recv), flag)
        keep, small, *sends = small_call(kernel, "combine%d" % n, sc, (keep, small, *recv), out)
        recv = [swap(sends[0], y, x), swap(sends[1], y), swap(sends[2], 0, x)]
    out = [((48, 128), F32), ((48, 128), F32)] + [((96, 128), F32)] * 3
    keep, small, *sends = small_call(
        turn_kernel, "turn", sc, (keep, small, *recv), out, [pltpu.VMEM((192, 128), F32)]
    )
    recv = [swap(sends[0], 3), swap(sends[1], 2), swap(sends[2], 1)]
    keep, small, send = small_call(last_kernel, "last", sc, (keep, small, *recv), out[:3])
    recv = swap(send, 7)
    out = [((48, 64), F32), ((10, CH), F32), ((1, CH), F32), ((1, CH), F32)]
    second, first, g_gain, g_bias = small_call(
        final_kernel, "final", sc, (keep, small, recv), out, [pltpu.VMEM((16, CH), F32)], jax.ShapeDtypeStruct
    )
    return (second, first, g_gain[0], g_bias[0])


def solution(mesh):
    placed = (
        P("bulk", "wide", None),
        P("bulk", "wide"),
        P("bulk", "wide"),
        P("bulk", "wide", None, None),
        P(),
        P(),
        P(),
        P(),
    )
    return jax.shard_map(
        per_device,
        mesh=mesh,
        in_specs=placed,
        out_specs=(P("wide", "bulk"), P(), P(), P()),
        check_vma=False,
    )
```

```python
import functools

import jax
import jax.numpy as jnp
from jax import lax
from jax.experimental import pallas as pl
from jax.experimental.pallas import tpu as pltpu
from jax.sharding import PartitionSpec as P

F32 = jnp.float32
BF16 = jnp.bfloat16
HIGHEST = lax.Precision.HIGHEST
SLOTS = 4
TAPS = 10
GRAN = 1024
ROWS = 2048
CH = 512
BLK = 1024
BLOCKS = [
    (2 * xh + (xl ^ xh), 2 * yh + (yl ^ yh)) for xl in range(2) for yl in range(2) for xh in range(2) for yh in range(2)
]


def dot(a, b, precision=None):
    return jnp.dot(a, b, preferred_element_type=F32, precision=precision)


def dot_b(a, b):
    return lax.dot_general(a, b, (((1,), (1,)), ((), ())), preferred_element_type=F32)


def dot_t(a, b, precision=None):
    return lax.dot_general(
        a, b, (((0,), (0,)), ((), ())), preferred_element_type=F32, precision=precision
    )


def cdf_slope(v):
    cdf = 0.5 + 0.5 * lax.erf(v * 0.7071067811865476)
    return cdf, cdf + v * (jnp.exp2(v * v * (-0.5 * 1.4426950408889634)) * 0.3989422804014327)


def plan(sc):
    size = [sc[s] for s in range(SLOTS)]
    src = [sc[SLOTS + s] ^ sc[16] for s in range(SLOTS)]
    rank, off = [], []
    for s in range(SLOTS):
        before = [(src[q] < src[s]).astype(jnp.int32) for q in range(SLOTS) if q != s]
        sizes = [size[q] for q in range(SLOTS) if q != s]
        rank.append(sum(before))
        off.append(sum(b * n for b, n in zip(before, sizes)))
    out = []
    for r in range(SLOTS):
        hit = [(rank[s] == r).astype(jnp.int32) for s in range(SLOTS)]
        out.append(
            (
                sum(h * s for s, h in enumerate(hit)),
                sum(h * o for o, h in zip(off, hit)),
                sum(h * n for n, h in zip(size, hit)),
            )
        )
    return out


def by_lane(values, index):
    out = values[0]
    for s in range(1, len(values)):
        out = jnp.where(index == s, values[s], out)
    return out


def window_kernel(
    sc, own_rows, moved, params, cot_hbm, w2_hbm,
    keep, send, small,
    lines, wide, lanes16, buf, xd, xbig, xs, wbig, acc, nst, tc, im, grads, carry, cot, w2, cot_sem, w2_sem,
):
    step = pl.program_id(0)
    segs = plan(sc)

    wst = params.at[0:32]
    gain = params.at[32:33]
    bias = params.at[33:34]
    copies = (
        pltpu.make_async_copy(w2_hbm, w2, w2_sem),
        pltpu.make_async_copy(cot_hbm, cot, cot_sem),
    )

    @pl.when(step == 0)
    def _():
        for copy in copies:
            copy.start()
        for s in range(SLOTS):
            at = pl.ds(80 * s, 80)
            lines[at, :] = jnp.where((sc[SLOTS + s] & 4) != 0, moved[at, :], own_rows[at, :]).astype(F32)
            for c in range(5):
                wide[16 * s : 16 * s + 16, 128 * c : 128 * c + 128] = lines[pl.ds(80 * s + c, 16, stride=5), :]
        place = lax.broadcasted_iota(jnp.int32, (1, 1024), 1)
        place = jnp.where(place % 16 < TAPS, place // 16 * TAPS + place % 16, -1)
        perm = (lax.broadcasted_iota(jnp.int32, (640, 1), 0) == place).astype(F32).astype(BF16)
        lanes16[...] = dot(wide[...].astype(BF16), perm)
        buf[pl.ds(ROWS, 8), :] = jnp.zeros((8, 128), F32)
        own = (
            lax.broadcasted_iota(jnp.int32, (8, 1024), 1) % 128 // 16
            == lax.broadcasted_iota(jnp.int32, (8, 1024), 0)
        )
        for slot, off, _n in segs:
            for r in range(16):
                line = jnp.where(own, lanes16[pl.ds(16 * slot + r, 1), :], 0.0)
                for j in range(8):
                    buf[pl.ds(off + 64 * r + 8 * j, 8), :] = line[:, 128 * j : 128 * j + 128]
        src = lax.broadcasted_iota(jnp.int32, (128, 256), 0) % 16
        tap = lax.broadcasted_iota(jnp.int32, (128, 256), 1) % 16
        r0 = ((tap == src) & (src < TAPS)).astype(F32).astype(BF16)
        r1 = ((tap == src + TAPS) & (src < 5)).astype(F32).astype(BF16)
        one = (lax.broadcasted_iota(jnp.int32, (1, 256), 1) % 16 == 15).astype(F32)
        lane = lax.broadcasted_iota(jnp.int32, (1, 256), 1)
        starts = [o for _s, o, _n in segs]
        ends = [o + n for _s, o, n in segs]
        lo_big, hi_big = by_lane(starts, lane // 64), by_lane(ends, lane // 64)
        lane1 = lane[:, :128]
        odd = (lane1 // 16) % 2
        lo_d = by_lane(starts, lane1 // 32)
        hi_all = by_lane(ends, lane1 // 32)
        hi_d = hi_all - odd
        count = (hi_d - lo_d).astype(F32)

        sums = jnp.zeros((1, 128), F32)
        for rb in range(ROWS // BLK):
            base = rb * BLK
            b0 = buf[pl.ds(base, BLK), :].astype(BF16)
            b1 = buf[pl.ds(base + 1, BLK), :].astype(BF16)
            xr = dot(b0, r0) + dot(b1, r1) + one
            row = lax.broadcasted_iota(jnp.int32, (BLK, 1), 0) + base
            xbig[pl.ds(base, BLK), :] = jnp.where((row >= lo_big) & (row < hi_big), xr, 0.0).astype(BF16)
            x1 = xr[:, :128]
            raw = jnp.where((row >= lo_d) & (row < hi_d), x1, 0.0)
            sums = sums + jnp.sum(raw, axis=0, keepdims=True)
            xd[pl.ds(base, BLK), :] = x1
            full = jnp.where((row >= lo_d) & (row < hi_all), x1, 0.0)
            xs[0, :, base : base + BLK] = jnp.where(odd == 0, full, 0.0).T.astype(BF16)
            xs[1, :, base : base + BLK] = jnp.where(odd == 1, full, 0.0).T.astype(BF16)
        xbig[pl.ds(ROWS, 16), :] = jnp.zeros((16, 256), BF16)
        mu = sums / count
        main = jnp.zeros((128, 128), F32)
        rest = jnp.zeros((128, 128), F32)
        for rb in range(ROWS // BLK):
            base = rb * BLK
            row = lax.broadcasted_iota(jnp.int32, (BLK, 1), 0) + base
            d = jnp.where((row >= lo_d) & (row < hi_d), xd[pl.ds(base, BLK), :] - mu, 0.0)
            high = d.astype(BF16)
            low = (d - high.astype(F32)).astype(BF16)
            main = main + dot_t(high, high)
            rest = rest + dot_t(high, low)
        ri = lax.broadcasted_iota(jnp.int32, (128, 128), 0)
        ci = lax.broadcasted_iota(jnp.int32, (128, 128), 1)
        moment = jnp.where(ri // 16 == ci // 16, main + (rest + rest.T), 0.0)
        wrow = jnp.concatenate([wst[...]] * SLOTS, axis=0)
        v = dot(moment, wrow, HIGHEST)
        block8 = (
            lax.broadcasted_iota(jnp.int32, (8, 128), 0)
            == lax.broadcasted_iota(jnp.int32, (8, 128), 1) // 16
        ).astype(F32)
        u8 = dot(block8 * mu, wrow, HIGHEST)
        q8 = dot(block8, v * wrow, HIGHEST)
        tcol = jnp.sum(jnp.where(ri == ci, sums, 0.0), axis=1, keepdims=True)
        tc[...] = jnp.broadcast_to(tcol, (128, 128))
        e15 = (lax.broadcasted_iota(jnp.int32, (16, 1), 0) == 15).astype(F32)
        for s, (_slot, _off, n) in enumerate(segs):
            n_even = n.astype(F32)
            n_odd = n_even - 1.0
            n_all = n_even + n_odd
            ue, uo = u8[2 * s : 2 * s + 1], u8[2 * s + 1 : 2 * s + 2]
            mean = (n_even * ue + n_odd * uo) / n_all
            de, do = ue - mean, uo - mean
            spread = (
                q8[2 * s : 2 * s + 1] + q8[2 * s + 1 : 2 * s + 2]
                + n_even * de * de + n_odd * do * do
            ) / n_all
            inv = lax.rsqrt(spread + 1e-05)
            a = gain[...] * inv
            b = bias[...] - a * mean
            im[s : s + 1, :] = inv
            im[4 + s : 5 + s, :] = mean
            for g, dev in enumerate((de, do)):
                at = 32 * s + 16 * g
                nst[at : at + 16, :] = v[at : at + 16] + tcol[at : at + 16] * dev
                f = wrow[at : at + 16] * a + e15 * b
                p0 = f.astype(BF16)
                f = f - p0.astype(F32)
                p1 = f.astype(BF16)
                f = f - p1.astype(F32)
                cols = pl.ds(g * CH, CH)
                wbig[64 * s : 64 * s + 16, cols] = p0
                wbig[64 * s + 16 : 64 * s + 32, cols] = p1
                wbig[64 * s + 32 : 64 * s + 48, cols] = f.astype(BF16)
                wbig[64 * s + 48 : 64 * s + 64, cols] = jnp.zeros((16, CH), BF16)
        acc[...] = jnp.zeros_like(acc)
        grads[...] = jnp.zeros_like(grads)
        carry[...] = jnp.zeros_like(carry)
        for copy in copies:
            copy.wait()

    base = pl.multiple_of(step * BLK, BLK)
    pre_e = dot(xbig[pl.ds(base, BLK + 16), :], wbig[:, :CH])
    pre_o = dot(xbig[pl.ds(base, BLK), :], wbig[:, CH:])
    c_e, s_e = cdf_slope(pre_e)
    act_e = pre_e * c_e
    c_o, s_o = cdf_slope(pre_o)
    taps = jnp.concatenate(
        [act_e[:BLK].astype(BF16), (pre_o * c_o).astype(BF16), act_e[1 : BLK + 1].astype(BF16)], axis=1
    )
    late = dot(taps, w2[...])
    _c, slope = cdf_slope(late)
    row = lax.broadcasted_iota(jnp.int32, (BLK, 1), 0) + base
    drop = row == segs[0][1] + segs[0][2] - 1
    for _s, off, n in segs[1:]:
        drop = drop | (row == off + n - 1)
    grad = jnp.where(drop, 0.0, cot[pl.ds(base, BLK), :].astype(F32) * slope).astype(BF16)
    acc[...] += dot_t(grad, taps)

    third = dot_b(grad, w2[2 * CH :, :])
    row = lax.broadcasted_iota(jnp.int32, (BLK, 1), 0)
    shifted = jnp.where(row == 0, carry[0:1, :], pltpu.roll(third, 1, 0))
    carry[0:1, :] = third[BLK - 1 : BLK]
    ag_e = (dot_b(grad, w2[:CH, :]) + shifted) * s_e[:BLK]
    ag_o = dot_b(grad, w2[CH : 2 * CH, :]) * s_o
    total = grads[...]
    for g, ag in enumerate((ag_e, ag_o)):
        part = xs[g, :, pl.ds(base, BLK)]
        high = ag.astype(BF16)
        low = (ag - high.astype(F32)).astype(BF16)
        total = total + dot(part, high) + dot(part, low)
    grads[...] = total

    @pl.when(step == pl.num_programs(0) - 1)
    def _():
        z = jnp.zeros((32, CH), F32)
        g_bias = jnp.zeros((1, CH), F32)
        g_gain = jnp.zeros((1, CH), F32)
        g = gain[...]
        for s, (_slot, _off, n) in enumerate(segs):
            at = 32 * s
            a = grads[at : at + 32, :]
            inv, mean = im[s : s + 1, :], im[4 + s : 5 + s, :]
            count = 2.0 * n.astype(F32) - 1.0
            s1 = a[15:16] + a[31:32]
            s2 = inv * (jnp.sum(a * wst[...], axis=0, keepdims=True) - mean * s1)
            first = g * s1 / count
            cross = g * s2 / count
            z = z + inv * (
                g * a - first * tc[at : at + 32, 0:1] - (cross * inv) * nst[at : at + 32, :]
            )
            g_bias = g_bias + s1
            g_gain = g_gain + s2
        grads[0:10, :] = z[0:10] + z[21:31]
        grads[10:11, :] = g_gain
        grads[11:12, :] = g_bias
        small[0:12, :] = grads[0:12, 0:384]
        for j in range(3):
            small[12:16, 128 * j : 128 * (j + 1)] = grads[4 * j : 4 * j + 4, 384:512]
        core = sc[8]
        for k, (x, y) in enumerate(BLOCKS):
            lanes = pl.ds(384 * y, 384)
            rows = pl.ds(64 * k, 64)
            keep[rows, :] = acc[pl.ds(pl.multiple_of(x * 128 + core * 64, 64), 64), lanes]
            send[rows, :] = acc[
                pl.ds(pl.multiple_of(x * 128 + (1 - core) * 64, 64), 64), lanes
            ].astype(BF16)
        pack_small(small, small[...], send, 1024)


def pack_small(small, value, send, at):
    high = value.astype(BF16)
    low = (value - high.astype(F32)).astype(BF16)
    send[at : at + 16, :] = high
    send[at + 16 : at + 32, :] = low
    small[...] = high.astype(F32) + low.astype(F32)


def received_small(recv, at):
    if recv.dtype == F32:
        return recv[at:, :]
    return recv[at : at + 16, :].astype(F32) + recv[at + 16 : at + 32, :].astype(F32)


def quarters(sc, at):
    a, b = sc[at], sc[at + 1]
    return 2 * a + b, (2 * (1 - a) + 1 - b, 2 * a + 1 - b, 2 * (1 - a) + b)


def add_small(small, recvs, at):
    r = [received_small(recv, at) for recv in recvs]
    return small[...] + r[0] if len(r) == 1 else (small[...] + r[1]) + (r[2] + r[0])


def combine_kernel(n, recvs, flag, sc, keep, small, *refs):
    recv, (keep_out, small_out, *sends) = refs[:recvs], refs[recvs:]
    quarter = n // 4
    mine, others = quarters(sc, flag)

    def rows(index):
        at = pl.ds(pl.multiple_of(index * quarter, quarter), quarter)
        total = keep[at, :]
        for r in recv:
            total = total + r[at, :].astype(F32)
        return total

    keep_out[...] = rows(mine)
    small_out[...] = add_small(small, recv, n)
    for index, send in zip(others, sends):
        send[0:quarter, :] = rows(index).astype(BF16)
    value = small_out[...]
    for send in sends:
        pack_small(small_out, value, send, quarter)


def turn_kernel(sc, keep, small, r0, r1, r2, keep_out, small_out, s0, s1, s2, turned):
    total = keep[...]
    for r in (r0, r1, r2):
        total = total + r[0:64, :].astype(F32)
    total = total.T
    for mid in range(2):
        for low in range(2):
            at = [192 * high + 96 * (mid ^ high) + 48 * (low ^ high) for high in range(2)]
            turned[96 * low + 48 * mid : 96 * low + 48 * mid + 48, :] = jnp.concatenate(
                [total[at[0] : at[0] + 48], total[at[1] : at[1] + 48]], axis=1
            )
    mine, others = quarters(sc, 13)
    keep_out[...] = turned[pl.ds(pl.multiple_of(mine * 48, 8), 48), :]
    sums = add_small(small, (r0, r1, r2), 64)
    for j in range(3):
        small_out[16 * j : 16 * j + 16, :] = sums[:, 128 * j : 128 * (j + 1)]
    for index, send in zip(others, (s0, s1, s2)):
        send[0:48, :] = turned[pl.ds(pl.multiple_of(index * 48, 8), 48), :]
        send[48:96, :] = small_out[...]


def last_kernel(sc, keep, small, r0, r1, r2, keep_out, small_out, send):
    del sc
    kept = keep[...] + r0[0:48, :] + r1[0:48, :] + r2[0:48, :]
    sums = add_small(small, (r0, r1, r2), 48)
    keep_out[...] = kept
    small_out[...] = sums
    send[0:48, :] = kept
    send[48:96, :] = sums


def final_kernel(sc, keep, small, recv, second, first, g_gain, g_bias, flat):
    total = keep[...] + recv[0:48, :]
    second[...] = jnp.where(sc[15] == 1, total[:, 64:128], total[:, 0:64])
    sums = small[...] + recv[48:96, :]
    for j in range(3):
        part = sums[16 * j : 16 * j + 16]
        flat[0:12, 128 * j : 128 * (j + 1)] = part[0:12]
        flat[4 * j : 4 * j + 4, 384:512] = part[12:16]
    first[...] = flat[0:10, :]
    g_gain[...] = flat[10:11, :]
    g_bias[...] = flat[11:12, :]


def in_vmem(value):
    return pltpu.with_memory_space_constraint(value, pltpu.VMEM)


def window(sc, own_rows, moved, params, cot, w2):
    whole = pl.BlockSpec(memory_space=pltpu.VMEM)
    shapes = [((1024, 384), F32), ((1056, 384), BF16), ((16, 384), F32)]
    return pl.pallas_call(
        window_kernel,
        grid_spec=pltpu.PrefetchScalarGridSpec(
            num_scalar_prefetch=1,
            grid=(ROWS // BLK,),
            in_specs=[
                whole, whole, whole,
                pl.BlockSpec(memory_space=pltpu.HBM), pl.BlockSpec(memory_space=pltpu.HBM),
            ],
            out_specs=[pl.BlockSpec(memory_space=pltpu.VMEM)] * len(shapes),
            scratch_shapes=[
                pltpu.VMEM((320, 128), F32),
                pltpu.VMEM((64, 640), F32),
                pltpu.VMEM((64, 1024), F32),
                pltpu.VMEM((ROWS + GRAN, 128), F32),
                pltpu.VMEM((ROWS, 128), F32),
                pltpu.VMEM((ROWS + 16, 256), BF16),
                pltpu.VMEM((2, 128, ROWS), BF16),
                pltpu.VMEM((256, 2 * CH), BF16),
                pltpu.VMEM((CH, 3 * CH), F32),
                pltpu.VMEM((128, CH), F32),
                pltpu.VMEM((128, 128), F32),
                pltpu.VMEM((8, CH), F32),
                pltpu.VMEM((128, CH), F32),
                pltpu.VMEM((8, CH), F32),
                pltpu.VMEM((ROWS, CH), BF16),
                pltpu.VMEM((3 * CH, CH), BF16),
                pltpu.SemaphoreType.DMA,
                pltpu.SemaphoreType.DMA,
            ],
        ),
        out_shape=[pltpu.VMEM(s, d) for s, d in shapes],
        compiler_params=pltpu.CompilerParams(vmem_limit_bytes=40 * 2**20),
        cost_estimate=pl.CostEstimate(flops=14 * 10**9, bytes_accessed=10 * 10**6, transcendentals=0),
        name="window",
    )(
        sc, in_vmem(own_rows), in_vmem(moved), in_vmem(params),
        pltpu.with_memory_space_constraint(cot, pltpu.HBM), pltpu.with_memory_space_constraint(w2, pltpu.HBM),
    )


def small_call(kernel, name, sc, args, shapes, scratch=(), place=pltpu.VMEM):
    args = [in_vmem(a) for a in args]
    return pl.pallas_call(
        kernel,
        in_specs=[pl.BlockSpec(memory_space=pltpu.SMEM)] + [pl.BlockSpec(memory_space=pltpu.VMEM)] * len(args),
        out_specs=[pl.BlockSpec(memory_space=pltpu.VMEM)] * len(shapes),
        out_shape=[place(s, d) for s, d in shapes],
        scratch_shapes=list(scratch),
        compiler_params=pltpu.CompilerParams(vmem_limit_bytes=8 * 2**20),
        name=name,
    )(sc, *args)


def swap(value, wide, bulk=0):
    return lax.ppermute(value, ("wide", "bulk"), [(i, i ^ (8 * wide + bulk)) for i in range(256)])


def rows_kernel(lengths, waves, out):
    for s in range(SLOTS):
        for i in range(80):
            lines_at = 80 * s + i
            out[lines_at : lines_at + 1, :] = waves[s : s + 1, 128 * i : 128 * i + 128]
    lane = lax.broadcasted_iota(jnp.int32, (16, 128), 1)
    tail = jnp.zeros((16, 128), F32)
    for s in range(SLOTS):
        units = lengths[s] // TAPS
        tail = jnp.where(lane == 32 * s, (units // 32).astype(F32), tail)
        tail = jnp.where(lane == 32 * s + 1, (units % 32).astype(F32), tail)
    out[320:336, :] = tail.astype(BF16)


def lay_rows(lengths, waves):
    return pl.pallas_call(
        rows_kernel,
        in_specs=[pl.BlockSpec(memory_space=pltpu.SMEM), pl.BlockSpec(memory_space=pltpu.VMEM)],
        out_specs=pl.BlockSpec(memory_space=pltpu.VMEM),
        out_shape=pltpu.VMEM((336, 128), BF16),
        compiler_params=pltpu.CompilerParams(vmem_limit_bytes=8 * 2**20),
        name="rows",
    )(*(pltpu.with_memory_space_constraint(a, pltpu.HBM) for a in (lengths, waves)))


def pick_kernel(first, sc, own, got_a, got_b, got_both, out):
    lane = lax.broadcasted_iota(jnp.int32, (16, 128), 1)
    refs = (own, got_b, got_a, got_both)
    tails = [r[320:336, :].astype(F32) for r in refs]
    tail = tails[0]
    for s in range(SLOTS):
        mask = sc[s]
        z_high, y_high = (mask >> 2) & 1, (mask >> 4) & 1
        if first:
            code = 2 * ((mask & 1) ^ z_high) + (((mask >> 3) & 1) ^ y_high)
        else:
            code = 2 * (((mask >> 1) & 1) ^ z_high) + y_high
        at = pl.ds(80 * s, 80)
        for k, ref in enumerate(refs):

            @pl.when(code == k)
            def _(ref=ref):
                out[at, :] = ref[at, :]

            if k:
                tail = jnp.where((lane // 32 == s) & (code == k), tails[k], tail)
    out[320:336, :] = tail.astype(BF16)


def route(waves, lengths, masks):
    out = [((336, 128), BF16)]
    value = lay_rows(lengths, waves)
    for a, b in ((2, 24), (1, 8)):
        got = [swap(value, a), swap(value, b), swap(value, a ^ b)]
        (value,) = small_call(functools.partial(pick_kernel, a == 1), "pick%d" % a, masks, (value, *got), out)
    moved = swap(value, 7)
    far = ((masks & 4) != 0)[:, None]
    tail = jnp.where(far, moved[320].reshape(4, 32), value[320].reshape(4, 32)).astype(F32)
    return value, moved, (tail[:, 0] * 32.0 + tail[:, 1]).astype(jnp.int32)


def window_inputs(conv_first, gain, bias):
    w = conv_first.astype(F32)
    rows = [jnp.pad(w, ((0, 6), (0, 0))), jnp.pad(w, ((5, 1), (0, 0))), gain[None, :], bias[None, :]]
    return jnp.concatenate(rows + [jnp.zeros((6, CH), F32)], axis=0)


def local(value, moved, units, masks, places, cot, conv_first, norm_gain, norm_bias, conv_second):
    sc = jnp.concatenate([units, masks, places])
    params = window_inputs(conv_first, norm_gain, norm_bias)
    return sc, window(sc, value, moved, params, cot, conv_second)


def per_device(waveforms, owner_of, lengths, cotangent, conv_first, norm_gain, norm_bias, conv_second):
    me = lax.axis_index("wide")
    place = lax.axis_index("bulk")
    masks = jnp.bitwise_xor(owner_of[0], me)
    value, moved, units = route(waveforms[0], lengths[0], masks)
    x_low, x_high, y_low, y_high = (place // 2) % 2, place // 4, (me // 8) % 2, me // 16
    z_low, z_mid, z_high = me % 2, (me // 2) % 2, (me // 4) % 2
    places = jnp.stack(
        [place % 2, x_low ^ x_high, y_low ^ y_high, x_high, y_high, z_low ^ z_high, z_mid ^ z_high, z_high, me]
    ).astype(jnp.int32)
    sc, (keep, send, small) = local(
        value, moved, units, masks, places, cotangent[0, 0],
        conv_first, norm_gain, norm_bias, conv_second,
    )
    recv = [swap(send, 0, 1)]
    for n, flag, y, x in ((1024, 9, 8, 2), (256, 11, 24, 6)):
        out = [((n // 4, 384), F32), ((16, 384), F32)] + [((n // 4 + 32, 384), BF16)] * 3
        kernel = functools.partial(combine_kernel, n, len(recv), flag)
        keep, small, *sends = small_call(kernel, "combine%d" % n, sc, (keep, small, *recv), out)
        recv = [swap(sends[0], y, x), swap(sends[1], y), swap(sends[2], 0, x)]
    out = [((48, 128), F32), ((48, 128), F32)] + [((96, 128), F32)] * 3
    keep, small, *sends = small_call(
        turn_kernel, "turn", sc, (keep, small, *recv), out, [pltpu.VMEM((192, 128), F32)]
    )
    recv = [swap(sends[0], 3), swap(sends[1], 2), swap(sends[2], 1)]
    keep, small, send = small_call(last_kernel, "last", sc, (keep, small, *recv), out[:3])
    recv = swap(send, 7)
    out = [((48, 64), F32), ((10, CH), F32), ((1, CH), F32), ((1, CH), F32)]
    second, first, g_gain, g_bias = small_call(
        final_kernel, "final", sc, (keep, small, recv), out, [pltpu.VMEM((16, CH), F32)], jax.ShapeDtypeStruct
    )
    return (second, first, g_gain[0], g_bias[0])


def solution(mesh):
    placed = (
        P("bulk", "wide", None),
        P("bulk", "wide"),
        P("bulk", "wide"),
        P("bulk", "wide", None, None),
        P(),
        P(),
        P(),
        P(),
    )
    return jax.shard_map(
        per_device,
        mesh=mesh,
        in_specs=placed,
        out_specs=(P("wide", "bulk"), P(), P(), P()),
        check_vma=False,
    )
```
